32 devices in a mesh: dp: 4 (over x, core), fsdp: 8 (over z, y).
Axes of the slice: x: 2, y: 2, z: 4, core: 2. Of those that a mesh axis runs over, the one named last changes fastest.
Arguments:
- tokens: bfloat16 [8192, 2048], P(('dp', 'fsdp')), may hold values from -6 to 6
- out_grad: bfloat16 [8192, 2048], P(('dp', 'fsdp')), may hold values from -6 to 6
- block_first: int32 [128], P(('dp', 'fsdp')), may hold values from 0 to 1, as said below
- block_live: int32 [128], P(('dp', 'fsdp')), may hold values from 0 to 64, as said below
- norm1_gain: bfloat16 [2048], P(('dp', 'fsdp')), may hold values from 0.5 to 1.5
- w_proj: bfloat16 [2048, 12288], P(('dp', 'fsdp')), may hold values from -0.125 to 0.125
- w_decay: bfloat16 [2048, 32], P(('dp', 'fsdp')), may hold values from -0.125 to 0.125
- conv_w: bfloat16 [4, 8192], P(None, ('dp', 'fsdp')), may hold values from -3 to 3
- w_out: bfloat16 [4096, 2048], P(('dp', 'fsdp')), may hold values from -0.1875 to 0.1875
- a_log: float32 [16], replicated, may hold values from 0 to 2.7
- dt_bias: float32 [16], replicated, may hold values from -6.5 to -2
- head_gain: float32 [256], replicated, may hold values from 0.5 to 1.5
- norm2_gain: bfloat16 [2048], P(('dp', 'fsdp')), may hold values from 0.5 to 1.5
- w_gate_up: bfloat16 [2048, 11264], P(('dp', 'fsdp')), may hold values from -0.125 to 0.125
- w_down: bfloat16 [5632, 2048], P(('dp', 'fsdp')), may hold values from -0.15625 to 0.15625
Outputs:
- layer_out: bfloat16 [8192, 2048], P(('dp', 'fsdp'))
- tokens_grad: bfloat16 [8192, 2048], P(('dp', 'fsdp'))
- norm1_gain_grad: float32 [2048], P(('dp', 'fsdp'))
- w_proj_grad: float32 [2048, 12288], P(('dp', 'fsdp'))
- w_decay_grad: float32 [2048, 32], P(('dp', 'fsdp'))
- conv_w_grad: float32 [4, 8192], P(None, ('dp', 'fsdp'))
- w_out_grad: float32 [4096, 2048], P(('dp', 'fsdp'))
- a_log_grad: float32 [16], replicated
- dt_bias_grad: float32 [16], replicated
- head_gain_grad: float32 [256], replicated
- norm2_gain_grad: float32 [2048], P(('dp', 'fsdp'))
- w_gate_up_grad: float32 [2048, 11264], P(('dp', 'fsdp'))
- w_down_grad: float32 [5632, 2048], P(('dp', 'fsdp'))
The draws below stay inside these ranges and needn't reach their ends.
Inputs may be any that keep to these rules, and one draw needn't show every extreme that they name: `block_first`: every device's first block begins a bucket; a bucket spans a power of two of blocks, at most 4, and begins at a multiple of its span within its device's blocks. `block_live`: A bucket holds one sequence whose length is more than half the bucket's rows; its live rows fill the bucket's blocks from the first one on.
All inputs are finite; a program needn't handle non-finite values.
Results may differ from the reference program's by a relative error of at most 0.012.
Values may be sent and summed in bfloat16 or wider, within the bound.
A program may use at most 640 MiB of HBM per device.

```python
import jax
import jax.numpy as jnp
from jax import lax

D = 2048
HEADS = 16
DK = 128
DV = 256
FF = 5632
CONV = 4
BLOCK = 64
BLOCKS_DEV = 4
BLOCKS = 128
TOKENS = 8192


def bucket_layout(key):
    block_count = BLOCKS
    level_count = BLOCKS_DEV.bit_length() - 1
    block_index = jnp.arange(block_count, dtype=jnp.int32)
    split_bits = jax.random.randint(jax.random.fold_in(key, 11), (max(level_count, 1), block_count), 0, 2)
    bucket_size = jnp.ones((block_count,), jnp.int32)
    active = jnp.ones((block_count,), jnp.bool_)
    for level_index in range(level_count):
        span_blocks = BLOCKS_DEV >> level_index
        decision = split_bits[level_index][block_index - block_index % span_blocks]
        settled = active & (decision == 0)
        bucket_size = jnp.where(settled, span_blocks, bucket_size)
        active = active & (decision == 1)
    bucket_first = block_index - block_index % bucket_size
    bucket_rows = bucket_size * BLOCK
    offsets = jax.random.randint(jax.random.fold_in(key, 12), (block_count,), 0, 1 << 20)
    seq_length = bucket_rows // 2 + 1 + offsets[bucket_first] % (bucket_rows - bucket_rows // 2)
    live_rows = jnp.clip(seq_length - (block_index - bucket_first) * BLOCK, 0, BLOCK)
    return ((block_index == bucket_first).astype(jnp.int32), live_rows.astype(jnp.int32))


def draw_block_first(key, part):
    starts, _ = bucket_layout(key)
    return starts


def draw_block_live(key, part):
    _, live_rows = bucket_layout(key)
    return live_rows


def block_levels(stream_key, dims, split, smallest, high):
    factor_of = 1.0
    for dim, shards_of in split:
        heights = jax.random.uniform(jax.random.fold_in(jax.random.fold_in(stream_key, 6), dim), (shards_of,), jnp.float32, smallest / len(split), high / len(split))
        factor_of = factor_of * jnp.repeat(jnp.exp(heights), dims[dim] // shards_of).reshape((-1,) + (1,) * (len(dims) - 1 - dim))
    return factor_of


def scatter_about(stream_key, dims, spread, reach, pieces=(), kind=jnp.bfloat16):
    loudness = block_levels(stream_key, dims, pieces, -0.22, 0.18) if pieces else 1.0
    values = jax.random.normal(stream_key, dims, jnp.float32) * spread * loudness
    return jnp.minimum(jnp.maximum(values, -reach), reach).astype(kind)


def setup_inputs(seed: int = 0) -> dict:
    key_list = jax.random.split(jax.random.key(seed), 16)
    tokens = scatter_about(key_list[0], (TOKENS, D), 1.0, 6.0, ((0, 32),))
    out_grad = scatter_about(key_list[1], (TOKENS, D), 1.0, 6.0, ((0, 32),))
    block_first = draw_block_first(jax.random.fold_in(key_list[15], 71), 0)
    block_live = draw_block_live(jax.random.fold_in(key_list[15], 71), 0)
    norm1_gain = jnp.clip(1.0 + 0.1 * jax.random.normal(key_list[4], (D,), jnp.float32), 0.5, 1.5).astype(jnp.bfloat16)
    w_proj = scatter_about(key_list[5], (D, HEADS * (2 * DK + 2 * DV)), D ** -0.5, 0.125, ((0, 32),))
    w_decay = scatter_about(key_list[6], (D, 2 * HEADS), D ** -0.5, 0.125, ((0, 32),))
    conv_w = scatter_about(key_list[7], (CONV, HEADS * (2 * DK + DV)), 0.5, 3.0, ((1, 32),))
    w_out = scatter_about(key_list[8], (HEADS * DV, D), (HEADS * DV // 4) ** -0.5, 0.1875, ((0, 32),))
    a_log = jnp.clip(jax.random.uniform(key_list[9], (HEADS,), jnp.float32, 0.0, 2.7), 0.0, 2.7)
    dt_bias = jnp.clip(jax.random.uniform(key_list[10], (HEADS,), jnp.float32, -6.5, -2.0), -6.5, -2.0)
    head_gain = jnp.clip(1.0 + 0.1 * jax.random.normal(key_list[11], (DV,), jnp.float32), 0.5, 1.5)
    norm2_gain = jnp.clip(1.0 + 0.1 * jax.random.normal(key_list[12], (D,), jnp.float32), 0.5, 1.5).astype(jnp.bfloat16)
    w_gate_up = scatter_about(key_list[13], (D, 2 * FF), D ** -0.5, 0.125, ((0, 32),))
    w_down = scatter_about(key_list[14], (FF, D), (FF // 4) ** -0.5, 0.15625, ((0, 32),))
    return {"tokens": tokens, "out_grad": out_grad, "block_first": block_first, "block_live": block_live, "norm1_gain": norm1_gain, "w_proj": w_proj, "w_decay": w_decay, "conv_w": conv_w, "w_out": w_out, "a_log": a_log, "dt_bias": dt_bias, "head_gain": head_gain, "norm2_gain": norm2_gain, "w_gate_up": w_gate_up, "w_down": w_down}


@jax.custom_vjp
def low(v):
    return lax.optimization_barrier(v.astype(jnp.bfloat16)).astype(jnp.float32)

@jax.custom_vjp
def low_back(v):
    return v

def low_keep(v):
    return (low(v), None)

def low_pass(kept, grad):
    return (grad,)

def back_keep(v):
    return (v, None)

def back_low(kept, grad):
    return (low(grad),)
low.defvjp(low_keep, low_pass)
low_back.defvjp(back_keep, back_low)
EPS = 1e-06
HIGH = lax.Precision.HIGHEST

def product(left, right):
    return jnp.dot(left, right, precision=HIGH, preferred_element_type=jnp.float32)

def rms_scale(values_in, gain_vec):
    return values_in * lax.rsqrt(lax.optimization_barrier(jnp.mean(values_in * values_in, axis=-1, keepdims=True)) + EPS) * gain_vec

def unit_rows(values_in):
    return values_in * lax.rsqrt(lax.optimization_barrier(jnp.sum(values_in * values_in, axis=-1, keepdims=True)) + EPS)

def row_layout(block_first, block_live, row_total):
    block_index = jnp.arange(block_first.shape[0], dtype=jnp.int32)
    bucket_starts = lax.cummax(jnp.where(block_first > 0, block_index * BLOCK, 0).astype(jnp.int32), axis=0)
    row_index = jnp.arange(row_total, dtype=jnp.int32)
    position = row_index - jnp.repeat(bucket_starts, BLOCK)
    live_mask = (row_index % BLOCK < jnp.repeat(block_live, BLOCK)).astype(jnp.float32)
    return (position, live_mask)

def short_conv(raw_input, conv_weight, position):
    running = raw_input * conv_weight[CONV - 1]
    for lag_steps in range(1, CONV):
        shifted = jnp.concatenate([jnp.zeros((lag_steps, raw_input.shape[1]), raw_input.dtype), raw_input[:-lag_steps]], axis=0)
        keep_rows = (position >= lag_steps).astype(raw_input.dtype)[:, None]
        running = running + shifted * keep_rows * conv_weight[CONV - 1 - lag_steps]
    return jax.nn.silu(running)

def prepare(projected, decay_raw, conv_weight, a_log, dt_bias, position):
    row_total = projected.shape[0]
    key_width = HEADS * DK
    conv_width = 2 * key_width + HEADS * DV
    conv_out = short_conv(projected[:, :conv_width], conv_weight, position)
    query = unit_rows(conv_out[:, :key_width].reshape(row_total, HEADS, DK)) * DK ** (-0.5)
    key_vec = unit_rows(conv_out[:, key_width:2 * key_width].reshape(row_total, HEADS, DK))
    value_vec = conv_out[:, 2 * key_width:].reshape(row_total, HEADS, DV)
    beta_gate = jax.nn.sigmoid(decay_raw[:, HEADS:])
    log_decay = -jnp.exp(a_log) * jax.nn.softplus(decay_raw[:, :HEADS] + dt_bias)
    return (query, key_vec, value_vec, beta_gate, log_decay, projected[:, conv_width:])

def finish(mix_heads, gate_raw, head_gain):
    normed = rms_scale(mix_heads, head_gain)
    return normed.reshape(mix_heads.shape[0], HEADS * DV) * jax.nn.silu(gate_raw)

def token_rule(query, key_vec, value_vec, beta_gate, log_decay, fresh_rows):

    def step_fn(carry_state, inputs):
        query_row, key_row, value_row, beta_row, decay_row, fresh_row = inputs
        decayed = carry_state * (jnp.exp(decay_row) * (1.0 - fresh_row))[:, None, None]
        predicted = jnp.einsum('hvk,hk->hv', decayed, key_row, precision=HIGH)
        carry_state = decayed + jnp.einsum('hv,hk->hvk', beta_row[:, None] * (value_row - predicted), key_row, precision=HIGH)
        return (carry_state, jnp.einsum('hvk,hk->hv', carry_state, query_row, precision=HIGH))

    def block_fn(carry_state, inputs):
        return lax.scan(step_fn, carry_state, inputs)
    row_total = query.shape[0]
    block_total = row_total // BLOCK
    inputs = tuple((array.reshape((block_total, BLOCK) + array.shape[1:]) for array in (query, key_vec, value_vec, beta_gate, log_decay, fresh_rows)))
    initial = jnp.zeros((HEADS, DV, DK), query.dtype)
    _, outputs = lax.scan(jax.checkpoint(block_fn), initial, inputs)
    return outputs.reshape(row_total, HEADS, DV)

def reference(tokens, out_grad, block_first, block_live, norm1_gain, w_proj, w_decay, conv_w, w_out, a_log, dt_bias, head_gain, norm2_gain, w_gate_up, w_down):
    position, live_mask = row_layout(block_first, block_live, tokens.shape[0])
    fresh_rows = (position == 0).astype(jnp.float32)
    params = (tokens.astype(jnp.float32), norm1_gain.astype(jnp.float32), w_proj.astype(jnp.float32), w_decay.astype(jnp.float32), conv_w.astype(jnp.float32), w_out.astype(jnp.float32), a_log, dt_bias, head_gain, norm2_gain.astype(jnp.float32), w_gate_up.astype(jnp.float32), w_down.astype(jnp.float32))

    def layer_fn(tokens_f, gain_one, proj_weight, decay_weight, conv_weight, out_weight, log_rate, step_bias, gain_head, gain_two, gate_up_weight, down_weight):
        normed_one = low(rms_scale(tokens_f, gain_one))
        projected = low_back(product(normed_one, proj_weight))
        decay_raw = low_back(product(normed_one, decay_weight))
        query, key_vec, value_vec, beta_gate, log_decay, gate_raw = prepare(projected, decay_raw, conv_weight, log_rate, step_bias, position)
        mix_heads = token_rule(query, key_vec, value_vec, beta_gate, log_decay, fresh_rows)
        mixed = low(finish(mix_heads, gate_raw, gain_head))
        residual = tokens_f + low_back(product(mixed, out_weight))
        normed_two = low(rms_scale(residual, gain_two))
        gate_up = low_back(product(normed_two, gate_up_weight))
        hidden = low(jax.nn.silu(gate_up[:, :FF]) * gate_up[:, FF:])
        return live_mask[:, None] * (residual + low_back(product(hidden, down_weight)))
    result, pullback = jax.vjp(layer_fn, *params)
    gradients = pullback(out_grad.astype(jnp.float32))
    return (result.astype(jnp.bfloat16), gradients[0].astype(jnp.bfloat16), gradients[1], gradients[2], gradients[3], gradients[4], gradients[5], gradients[6], gradients[7], gradients[8], gradients[9], gradients[10], gradients[11])
```

```python
from functools import partial

import jax
import jax.numpy as jnp
from jax import lax
from jax.experimental import pallas as pl
from jax.experimental.pallas import tpu as pltpu
from jax.sharding import PartitionSpec as P

HEADS = 16
DK = 128
DV = 256
CONV = 4
BLOCK = 64
TP = 4
LH = HEADS // TP
TAIL = 128
EPS = 1e-06
HIGH = lax.Precision.HIGHEST
F32 = jnp.float32
BF16 = jnp.bfloat16


def mm(left, right, dims=((1,), (0,))):
    return lax.dot_general(left, right, (dims, ((), ())), preferred_element_type=F32)


def mmb(left, right, dims=((1,), (0,))):
    return mm(left.astype(BF16), right.astype(BF16), dims)


def mm3(left, right):
    left_hi = left.astype(BF16)
    right_hi = right.astype(BF16)
    left_lo = (left - left_hi.astype(F32)).astype(BF16)
    right_lo = (right - right_hi.astype(F32)).astype(BF16)
    return mm(left_hi, right_hi) + (mm(left_hi, right_lo) + mm(left_lo, right_hi))


def mmx(left, right, dims=((1,), (0,))):
    return lax.dot_general(left, right, (dims, ((), ())), precision=HIGH, preferred_element_type=F32)


def sigmoid(v):
    return 1.0 / (1.0 + jnp.exp(-v))


def conv_rows(raw, taps, pos):
    total = raw * taps[CONV - 1 : CONV]
    for lag in range(1, CONV):
        moved = pltpu.roll(raw, lag, 0)
        total = total + jnp.where(pos >= lag, moved, 0.0) * taps[CONV - 1 - lag : CONV - lag]
    return total


def conv_back(grad, raw, taps, pos):
    rows = raw.shape[0]
    total = grad * taps[CONV - 1 : CONV]
    sums = [jnp.sum(grad * raw, axis=0, keepdims=True)]
    for lag in range(1, CONV):
        kept = jnp.where(pos >= lag, grad, 0.0)
        total = total + pltpu.roll(kept, rows - lag, 0) * taps[CONV - 1 - lag : CONV - lag]
        sums.append(jnp.sum(kept * pltpu.roll(raw, lag, 0), axis=0, keepdims=True))
    return total, sums[::-1]


def unit(v, scale):
    inv = lax.rsqrt(jnp.sum(v * v, axis=-1, keepdims=True) + EPS)
    return v * (inv * scale), inv


def unit_back(grad, v, inv, scale):
    g = grad * scale
    return inv * g - v * (inv * inv * inv * jnp.sum(v * g, axis=-1, keepdims=True))


def silu_back(grad, pre, sig):
    return grad * (sig * (1.0 + pre * (1.0 - sig)))


def group_terms(tail_ref, prm_ref, pos_ref):
    rows = tail_ref.shape[0]
    pos = pos_ref[:, 0:1].astype(jnp.int32)
    row_i = lax.broadcasted_iota(jnp.int32, (rows, rows), 0)
    row_j = lax.broadcasted_iota(jnp.int32, (rows, rows), 1)
    lower = (row_j <= row_i) & (row_j >= row_i - pos)
    raw = tail_ref[...]
    shifted = raw + prm_ref[1:2]
    soft = jnp.maximum(shifted, 0.0) + jnp.log1p(jnp.exp(-jnp.abs(shifted)))
    log_decay = prm_ref[0:1] * soft
    beta = sigmoid(raw)
    lower_f = lower.astype(F32)
    cum = mmx(lower_f, log_decay)
    return pos, row_i, row_j, lower, lower_f, raw, shifted, log_decay, beta, cum, cum.T


def unit_lower_inverse(low, bits):
    rows = low.shape[0]
    eye = (bits == 0).astype(F32)
    inv = eye - jnp.where(bits == 1, low, 0.0)
    step = 1
    while (2 << step) <= rows:
        part = jnp.where((bits >> step) == 1, low, 0.0)
        inv = inv - mm3(inv, mm3(part, inv))
        step += 1
    return inv


def head_slices(head):
    key_width = LH * DK
    return (
        slice(head * DK, (head + 1) * DK),
        slice(key_width + head * DK, key_width + (head + 1) * DK),
        slice(2 * key_width + head * DV, 2 * key_width + (head + 1) * DV),
        slice(2 * key_width + (LH + head) * DV, 2 * key_width + (LH + head + 1) * DV),
    )


def mixer_fwd_kernel(proj_ref, pos_ref, conv_ref, prm_ref, gain_ref, mixed_ref, inv_ref, new_ref):
    width = proj_ref.shape[1]
    tail_ref = proj_ref.at[:, width - TAIL :]
    pos, row_i, row_j, lower, _, _, _, _, beta_all, cum, cum_t = group_terms(tail_ref, prm_ref, pos_ref)
    strict = lower & (row_j < row_i)
    bits = row_i ^ row_j
    for head in range(LH):
        sq, sk, sv, sg = head_slices(head)
        q_pre = conv_rows(proj_ref[:, sq], conv_ref[:, sq], pos)
        k_pre = conv_rows(proj_ref[:, sk], conv_ref[:, sk], pos)
        v_pre = conv_rows(proj_ref[:, sv], conv_ref[:, sv], pos)
        query, _ = unit(q_pre * sigmoid(q_pre), DK**-0.5)
        key, _ = unit(k_pre * sigmoid(k_pre), 1.0)
        value = v_pre * sigmoid(v_pre)
        beta = beta_all[:, LH + head : LH + head + 1]
        gap = cum[:, head : head + 1] - cum_t[head : head + 1, :]
        decay = jnp.where(lower, jnp.exp(gap), 0.0)
        pair = mmb(key, key, ((1,), (1,)))
        attend = mmb(query, key, ((1,), (1,))) * decay
        low = jnp.where(strict, beta * pair * decay, 0.0)
        inv = unit_lower_inverse(low, bits)
        new = mmb(inv, beta * value)
        mix = mmb(attend, new)
        scale = lax.rsqrt(jnp.mean(mix * mix, axis=-1, keepdims=True) + EPS)
        gate = proj_ref[:, sg]
        out = mix * scale * gain_ref[0:1] * (gate * sigmoid(gate))
        mixed_ref[:, head * DV : (head + 1) * DV] = out.astype(BF16)
        inv_ref[head] = inv.astype(BF16)
        new_ref[:, head * DV : (head + 1) * DV] = new.astype(BF16)


def mixer_bwd_kernel(
    proj_ref, pos_ref, conv_ref, prm_ref, gain_ref, inv_ref, new_ref, gmix_ref, gproj_ref, gconv_ref, misc_ref
):
    width = proj_ref.shape[1]
    rows = proj_ref.shape[0]
    tail_ref = proj_ref.at[:, width - TAIL :]
    pos, row_i, row_j, lower, lower_f, raw, shifted, log_decay, beta_all, cum, cum_t = group_terms(
        tail_ref, prm_ref, pos_ref
    )
    strict = lower & (row_j < row_i)
    lane = lax.broadcasted_iota(jnp.int32, (rows, TAIL), 1)
    ones = jnp.ones((rows, TAIL), F32)
    grad_cum = jnp.zeros((rows, TAIL), F32)
    grad_beta_all = jnp.zeros((rows, TAIL), F32)
    gain_sum = jnp.zeros((1, DV), F32)
    gconv_ref[...] = jnp.zeros_like(gconv_ref)
    misc_ref[...] = jnp.zeros_like(misc_ref)
    for head in range(LH):
        sq, sk, sv, sg = head_slices(head)
        q_raw, k_raw, v_raw = proj_ref[:, sq], proj_ref[:, sk], proj_ref[:, sv]
        q_pre = conv_rows(q_raw, conv_ref[:, sq], pos)
        k_pre = conv_rows(k_raw, conv_ref[:, sk], pos)
        v_pre = conv_rows(v_raw, conv_ref[:, sv], pos)
        q_sig, k_sig, v_sig = sigmoid(q_pre), sigmoid(k_pre), sigmoid(v_pre)
        q_act, k_act, value = q_pre * q_sig, k_pre * k_sig, v_pre * v_sig
        query, q_inv = unit(q_act, DK**-0.5)
        key, k_inv = unit(k_act, 1.0)
        query_b, key_b = query.astype(BF16), key.astype(BF16)
        beta = beta_all[:, LH + head : LH + head + 1]
        gap = cum[:, head : head + 1] - cum_t[head : head + 1, :]
        decay = jnp.where(lower, jnp.exp(gap), 0.0)
        pair = mm(key_b, key_b, ((1,), (1,)))
        query_pair = mm(query_b, key_b, ((1,), (1,)))
        attend = (query_pair * decay).astype(BF16)
        inv = inv_ref[head]
        new = new_ref[:, head * DV : (head + 1) * DV]
        mix = mm(attend, new)
        scale = lax.rsqrt(jnp.mean(mix * mix, axis=-1, keepdims=True) + EPS)
        gate = proj_ref[:, sg]
        gate_sig = sigmoid(gate)
        grad_out = gmix_ref[:, head * DV : (head + 1) * DV]
        unscaled = mix * scale
        grad_norm = grad_out * (gate * gate_sig)
        grad_gate = silu_back(grad_out * unscaled * gain_ref[0:1], gate, gate_sig)
        gain_sum = gain_sum + jnp.sum(grad_norm * unscaled, axis=0, keepdims=True)
        weighted = grad_norm * gain_ref[0:1]
        grad_mix = scale * weighted - mix * (
            scale * scale * scale * jnp.mean(mix * weighted, axis=-1, keepdims=True)
        )
        grad_mix_b = grad_mix.astype(BF16)
        grad_new = mm(attend, grad_mix_b, ((0,), (0,)))
        grad_attend = mm(grad_mix_b, new, ((1,), (1,)))
        grad_rhs = mmb(inv, grad_new, ((0,), (0,)))
        grad_low = -mm(grad_rhs.astype(BF16), new, ((1,), (1,)))
        grad_value = beta * grad_rhs
        low_decay = jnp.where(strict, grad_low * decay, 0.0)
        low_pair = low_decay * pair
        grad_beta = jnp.sum(grad_rhs * value, axis=-1, keepdims=True) + jnp.sum(
            low_pair, axis=-1, keepdims=True
        )
        grad_pair = beta * low_decay
        grad_query_pair = grad_attend * decay
        both = beta * low_pair + grad_query_pair * query_pair
        column = jnp.sum(both, axis=-1, keepdims=True) - mmx(both, ones, ((0,), (0,)))
        grad_cum = jnp.where(lane == head, column, grad_cum)
        grad_beta_all = jnp.where(lane == LH + head, grad_beta, grad_beta_all)
        grad_pair_b = grad_pair.astype(BF16)
        grad_qp_b = grad_query_pair.astype(BF16)
        grad_query = mm(grad_qp_b, key_b)
        grad_key = (
            mm(grad_qp_b, query_b, ((0,), (0,))) + mm(grad_pair_b, key_b) + mm(grad_pair_b, key_b, ((0,), (0,)))
        )
        grad_q = silu_back(unit_back(grad_query, q_act, q_inv, DK**-0.5), q_pre, q_sig)
        grad_k = silu_back(unit_back(grad_key, k_act, k_inv, 1.0), k_pre, k_sig)
        grad_v = silu_back(grad_value, v_pre, v_sig)
        for grad, part, where in ((grad_q, q_raw, sq), (grad_k, k_raw, sk), (grad_v, v_raw, sv)):
            moved, sums = conv_back(grad, part, conv_ref[:, where], pos)
            gproj_ref[:, where] = moved.astype(BF16)
            for tap in range(CONV):
                gconv_ref[0, tap : tap + 1, where] = sums[tap]
        gproj_ref[:, sg] = grad_gate.astype(BF16)
    grad_log = mmx(lower_f, grad_cum, ((0,), (0,)))
    grad_step = grad_log * prm_ref[0:1] * sigmoid(shifted)
    grad_tail = grad_step + grad_beta_all * beta_all * (1.0 - beta_all)
    gproj_ref[:, width - TAIL :] = grad_tail.astype(BF16)
    misc_ref[0, 0:1, :] = gain_sum
    misc_ref[0, 1:2, 0:TAIL] = jnp.sum(grad_log * log_decay, axis=0, keepdims=True)
    misc_ref[0, 2:3, 0:TAIL] = jnp.sum(grad_step, axis=0, keepdims=True)


VMEM_LIMIT = 56 * 1024 * 1024


def mixer_fwd(proj, pos, conv, prm, gain):
    total, width = proj.shape
    rows = total // TP
    return pl.pallas_call(
        mixer_fwd_kernel,
        grid=(TP,),
        in_specs=[
            pl.BlockSpec((rows, width), lambda g: (g, 0)),
            pl.BlockSpec((rows, TAIL), lambda g: (g, 0)),
            pl.BlockSpec(conv.shape, lambda g: (0, 0)),
            pl.BlockSpec(prm.shape, lambda g: (0, 0)),
            pl.BlockSpec(gain.shape, lambda g: (0, 0)),
        ],
        out_specs=[
            pl.BlockSpec((rows, LH * DV), lambda g: (g, 0)),
            pl.BlockSpec((LH, rows, rows), lambda g: (g, 0, 0)),
            pl.BlockSpec((rows, LH * DV), lambda g: (g, 0)),
        ],
        out_shape=[
            jax.ShapeDtypeStruct((total, LH * DV), BF16),
            jax.ShapeDtypeStruct((TP * LH, rows, rows), BF16),
            jax.ShapeDtypeStruct((total, LH * DV), BF16),
        ],
        compiler_params=pltpu.CompilerParams(vmem_limit_bytes=VMEM_LIMIT),
        cost_estimate=pl.CostEstimate(flops=30_000_000_000, bytes_accessed=30_000_000, transcendentals=5_000_000),
        name="mixer_fwd",
    )(proj, pos, conv, prm, gain)


def mixer_bwd(proj, pos, conv, prm, gain, inv, new, gmix):
    total, width = proj.shape
    rows = total // TP
    return pl.pallas_call(
        mixer_bwd_kernel,
        grid=(TP,),
        in_specs=[
            pl.BlockSpec((rows, width), lambda g: (g, 0)),
            pl.BlockSpec((rows, TAIL), lambda g: (g, 0)),
            pl.BlockSpec(conv.shape, lambda g: (0, 0)),
            pl.BlockSpec(prm.shape, lambda g: (0, 0)),
            pl.BlockSpec(gain.shape, lambda g: (0, 0)),
            pl.BlockSpec((LH, rows, rows), lambda g: (g, 0, 0)),
            pl.BlockSpec((rows, LH * DV), lambda g: (g, 0)),
            pl.BlockSpec((rows, LH * DV), lambda g: (g, 0)),
        ],
        out_specs=[
            pl.BlockSpec((rows, width), lambda g: (g, 0)),
            pl.BlockSpec((1, 8, conv.shape[1]), lambda g: (g, 0, 0)),
            pl.BlockSpec((1, 8, DV), lambda g: (g, 0, 0)),
        ],
        out_shape=[
            jax.ShapeDtypeStruct((total, width), BF16),
            jax.ShapeDtypeStruct((TP, 8, conv.shape[1]), F32),
            jax.ShapeDtypeStruct((TP, 8, DV), F32),
        ],
        compiler_params=pltpu.CompilerParams(vmem_limit_bytes=VMEM_LIMIT),
        cost_estimate=pl.CostEstimate(flops=50_000_000_000, bytes_accessed=40_000_000, transcendentals=5_000_000),
        name="mixer_bwd",
    )(proj, pos, conv, prm, gain, inv, new, gmix)


def after(value, *earlier):
    return lax.optimization_barrier((value,) + earlier)[0]


class Moves:
    def __init__(self, fsdp_size):
        self.nf = fsdp_size
        self.nz = fsdp_size // 2
        self.f = lax.axis_index("fsdp")
        self.z = self.f // 2
        self.y = self.f % 2
        self.d = lax.axis_index("dp")

    def dp_swap(self, value, mask):
        return lax.ppermute(value, "dp", [(i, i ^ mask) for i in range(TP)])

    def y_swap(self, value):
        return lax.ppermute(value, "fsdp", [(i, i ^ 1) for i in range(self.nf)])

    def z_turn(self, value, step):
        pairs = [(i, ((i // 2 + step) % self.nz) * 2 + i % 2) for i in range(self.nf)]
        return lax.ppermute(value, "fsdp", pairs)

    def dp_gather(self, value):
        far = self.dp_swap(value, 2)
        near = self.dp_swap(value, 1)
        return jnp.stack([value, near, far, self.dp_swap(far, 1)])

    def dp_reduce(self, parts):
        got = self.dp_swap(jnp.stack([parts[1], parts[3]]), 1)
        mine = parts[0].astype(F32) + got[0].astype(F32)
        far = (parts[2].astype(F32) + got[1].astype(F32)).astype(BF16)
        return mine + self.dp_swap(far, 2).astype(F32)

    def gather(self, value, before=()):
        value = after(value, *before)
        turned = [value] + [self.z_turn(value, k) for k in range(1, self.nz)]
        full = jnp.zeros((self.nz, 2) + value.shape, value.dtype)
        for k, part in enumerate(turned):
            other = self.y_swap(part)
            where = (self.z - k) % self.nz
            zero = (0,) * value.ndim
            full = lax.dynamic_update_slice(full, part[None, None], (where, self.y) + zero)
            full = lax.dynamic_update_slice(full, other[None, None], (where, 1 - self.y) + zero)
        return full.reshape((self.nf,) + value.shape), tuple(turned[1:])

    def reduce(self, send, keep):
        total = keep + self.y_swap(send).astype(F32)
        rounded = total.astype(BF16)
        mine = lax.dynamic_index_in_dim(total, self.z, 0, keepdims=False)
        for k in range(1, self.nz):
            part = lax.dynamic_index_in_dim(rounded, (self.z + k) % self.nz, 0, keepdims=False)
            mine = mine + self.z_turn(part, k).astype(F32)
        return mine

    def halves(self, value, axis):
        shape = value.shape
        split = value.reshape(shape[:axis] + (self.nz, 2, shape[axis] // self.nf) + shape[axis + 1 :])
        return tuple(
            lax.dynamic_index_in_dim(split, which, axis + 1, keepdims=False).reshape(
                shape[:axis] + (shape[axis] // 2,) + shape[axis + 1 :]
            )
            for which in (1 - self.y, self.y)
        )


def local(
    tokens,
    out_grad,
    block_first,
    block_live,
    norm1_gain,
    w_proj,
    w_decay,
    conv_w,
    w_out,
    a_log,
    dt_bias,
    head_gain,
    norm2_gain,
    w_gate_up,
    w_down,
    *,
    fsdp_size,
):
    mv = Moves(fsdp_size)
    nf, nz = mv.nf, mv.nz
    rows, width = tokens.shape
    own = w_proj.shape[0]
    key_width = HEADS * DK
    value_width = HEADS * DV
    ff = w_down.shape[0] * nf

    def to_perm(value):
        return value.reshape(rows, TP, nf, own).swapaxes(1, 2).reshape(rows, width)

    def from_perm(value):
        return value.reshape(rows, nf, TP, own).swapaxes(1, 2).reshape(rows, width)

    block_index = jnp.arange(block_first.shape[0], dtype=jnp.int32)
    earlier = (block_index[:, None] >= block_index[None]) & (block_first[None] > 0)
    bucket_starts = jnp.max(jnp.where(earlier, block_index[None] * BLOCK, 0), axis=1)
    row_index = jnp.arange(rows, dtype=jnp.int32)
    position = row_index - jnp.repeat(bucket_starts, BLOCK)
    live = (row_index % BLOCK < jnp.repeat(block_live, BLOCK)).astype(F32)[:, None]

    def by_target(value):
        return value.reshape(own, TP, -1).swapaxes(0, 1)

    taps = conv_w.reshape(own, -1)
    tail = jnp.concatenate(
        [
            by_target(w_decay[:, :HEADS]),
            by_target(w_decay[:, HEADS:]),
            jnp.broadcast_to(
                jnp.concatenate([norm1_gain[:, None], norm2_gain[:, None], taps], axis=1)[None],
                (TP, own, 2 + taps.shape[1]),
            ),
        ],
        axis=2,
    )
    tail = jnp.pad(tail, ((0, 0), (0, 0), (0, TAIL - tail.shape[2])))
    pack_one = jnp.concatenate(
        [
            by_target(w_proj[:, :key_width]),
            by_target(w_proj[:, key_width : 2 * key_width]),
            by_target(w_proj[:, 2 * key_width : 2 * key_width + value_width]),
            by_target(w_proj[:, 2 * key_width + value_width :]),
            tail,
        ],
        axis=2,
    )
    pack_two = jnp.concatenate([by_target(w_gate_up[:, :ff * TP]), by_target(w_gate_up[:, ff * TP :])], axis=2)

    out_blocks, out_done = mv.gather(w_out)
    pack_one = lax.all_to_all(pack_one, "dp", 0, 0, tiled=True)
    pack_two = lax.all_to_all(pack_two, "dp", 0, 0, tiled=True)
    one_blocks, one_done = mv.gather(pack_one, out_done)
    two_blocks, two_done = mv.gather(pack_two, one_done)
    down_blocks, _ = mv.gather(w_down, two_done)
    out_full = out_blocks.reshape(-1, width)
    proj_full = one_blocks.reshape(width, -1)
    gate_up_full = two_blocks.reshape(width, -1)
    down_full = down_blocks.reshape(-1, width)

    tokens_perm = to_perm(tokens)
    extra = jnp.broadcast_to(position.astype(BF16)[:, None], (rows, TAIL))
    group = mv.dp_gather(jnp.concatenate([tokens_perm, extra], axis=1)).reshape(TP * rows, width + TAIL)
    group_pos = group[:, width:].astype(F32)
    group_tokens = group[:, :width].astype(F32)
    cotangent = live * out_grad.astype(F32)
    grad_down = mv.dp_gather(cotangent.astype(BF16)).reshape(TP * rows, width)

    tail_full = proj_full[:, -TAIL:]
    gain_one = tail_full[:, 2 * LH].astype(F32)
    gain_two = tail_full[:, 2 * LH + 1].astype(F32)
    taps_full = tail_full[:, 2 * LH + 2 : 2 * LH + 2 + taps.shape[1]]
    taps_full = (
        taps_full.reshape(nf, TP, CONV, -1).transpose(2, 1, 0, 3).reshape(CONV, 2 * key_width + value_width).astype(F32)
    )

    def my_columns(value):
        k, v = LH * DK, LH * DV
        return jnp.concatenate(
            [
                lax.dynamic_slice_in_dim(value, mv.d * k, k, 1),
                lax.dynamic_slice_in_dim(value, key_width + mv.d * k, k, 1),
                lax.dynamic_slice_in_dim(value, 2 * key_width + mv.d * v, v, 1),
            ],
            axis=1,
        )

    conv_mine = jnp.pad(my_columns(taps_full), ((0, 8 - CONV), (0, 0)))
    rate = -jnp.exp(lax.dynamic_slice_in_dim(a_log, mv.d * LH, LH))
    bias = lax.dynamic_slice_in_dim(dt_bias, mv.d * LH, LH)
    prm = jnp.pad(jnp.stack([rate, bias]), ((0, 6), (0, TAIL - LH)))
    gain_head = jnp.broadcast_to(head_gain[None], (8, DV))

    scale_one = lax.rsqrt(jnp.mean(group_tokens * group_tokens, axis=-1, keepdims=True) + EPS)
    normed_one = (group_tokens * scale_one * gain_one).astype(BF16)
    proj = mm(normed_one, proj_full)
    mixed, inv, new = mixer_fwd(proj, group_pos, conv_mine, prm, gain_head)
    mixed_out = mm(mixed, out_full).astype(BF16).reshape(TP, rows, width)
    residual = tokens.astype(F32) + mv.dp_reduce(mixed_out)
    residual_perm = to_perm(residual)
    scale_two = lax.rsqrt(jnp.mean(residual * residual, axis=-1, keepdims=True) + EPS)
    normed_two = mv.dp_gather((residual_perm * scale_two * gain_two).astype(BF16)).reshape(TP * rows, width)
    gate_up = mm(normed_two, gate_up_full)
    gate, up = gate_up[:, :ff], gate_up[:, ff:]
    gate_sig = jax.nn.sigmoid(gate)
    gate_act = gate * gate_sig
    hidden = (gate_act * up).astype(BF16)
    down_out = mm(hidden, down_full).astype(BF16).reshape(TP, rows, width)
    layer_out = (live * (residual + mv.dp_reduce(down_out))).astype(BF16)

    grad_wdown = mm(hidden, grad_down, ((0,), (0,)))
    down_send, down_keep = mv.halves(grad_wdown, 0)
    wdown_grad = mv.reduce(down_send.astype(BF16).reshape(nz, -1, width), down_keep.reshape(nz, -1, width))
    grad_hidden = mm(grad_down, down_full, ((1,), (1,)))
    grad_gate = (grad_hidden * up * gate_sig * (1.0 + gate * (1.0 - gate_sig))).astype(BF16)
    grad_up = (grad_hidden * gate_act).astype(BF16)
    grad_gate_up = jnp.concatenate([grad_gate, grad_up], axis=1)
    two_other, two_mine = mv.halves(normed_two, 1)
    two_shape = (nz, TP * own, 2 * ff)
    two_grad = mv.reduce(
        mm(two_other, grad_gate_up, ((0,), (0,))).astype(BF16).reshape(two_shape),
        mm(two_mine, grad_gate_up, ((0,), (0,))).reshape(two_shape),
    )
    grad_two = mv.dp_reduce(
        mm(grad_gate_up, gate_up_full, ((1,), (1,))).astype(BF16).reshape(TP, rows, width)
    )
    weighted = grad_two * gain_two
    gain_two_part = jnp.sum(grad_two * residual_perm * scale_two, axis=0)
    grad_residual = (
        to_perm(cotangent)
        + scale_two * weighted
        - residual_perm * (scale_two**3 * jnp.mean(residual_perm * weighted, axis=-1, keepdims=True))
    )

    grad_mixed_in = mv.dp_gather(from_perm(grad_residual).astype(BF16)).reshape(TP * rows, width)
    mixed_other, mixed_mine = mv.halves(mixed, 1)
    out_shape = (nz, -1, width)
    wout_grad = mv.reduce(
        mm(mixed_other, grad_mixed_in, ((0,), (0,))).astype(BF16).reshape(out_shape),
        mm(mixed_mine, grad_mixed_in, ((0,), (0,))).reshape(out_shape),
    )
    grad_mixed = mm(grad_mixed_in, out_full, ((1,), (1,)))
    grad_proj, grad_taps, misc = mixer_bwd(
        proj, group_pos, conv_mine, prm, gain_head, inv, new, grad_mixed
    )
    grad_one_part = mm(grad_proj, proj_full, ((1,), (1,)))
    gain_one_part = jnp.sum(grad_one_part * group_tokens * scale_one, axis=0)
    grad_one = mv.dp_reduce(grad_one_part.astype(BF16).reshape(TP, rows, width))

    grad_taps = jnp.sum(grad_taps[:, :CONV], axis=0)
    k, v = LH * DK, LH * DV
    taps_all = jnp.zeros((CONV, 2 * key_width + value_width), F32)
    taps_all = lax.dynamic_update_slice(taps_all, grad_taps[:, :k], (0, mv.d * k))
    taps_all = lax.dynamic_update_slice(taps_all, grad_taps[:, k : 2 * k], (0, key_width + mv.d * k))
    taps_all = lax.dynamic_update_slice(taps_all, grad_taps[:, 2 * k :], (0, 2 * key_width + mv.d * v))
    taps_all = (
        taps_all.reshape(CONV, TP, nf, -1).transpose(2, 1, 0, 3).reshape(width, taps.shape[1])
    )
    small = jnp.concatenate([gain_one_part[:, None], gain_two_part[:, None], taps_all], axis=1)
    small = small.reshape(nz, 2, TP * own, small.shape[1])
    columns = proj.shape[1]
    pads = ((0, 0), (0, 0), (columns - TAIL + 2 * LH, TAIL - 2 * LH - small.shape[3]))

    def small_of(which):
        return jnp.pad(lax.dynamic_index_in_dim(small, which, 1, keepdims=False), pads)

    one_other, one_mine = mv.halves(normed_one, 1)
    one_shape = (nz, TP * own, columns)
    one_grad = mv.reduce(
        (mm(one_other, grad_proj, ((0,), (0,))).reshape(one_shape) + small_of(1 - mv.y)).astype(BF16),
        mm(one_mine, grad_proj, ((0,), (0,))).reshape(one_shape) + small_of(mv.y),
    )

    def to_owner(value):
        return lax.all_to_all(
            value.astype(BF16).reshape(TP, own, value.shape[-1]), "dp", 0, 0, tiled=True
        ).astype(F32)

    def columns_of(value):
        return value.swapaxes(0, 1).reshape(own, -1)

    two_own = to_owner(two_grad)
    w_gate_up_grad = jnp.concatenate([columns_of(two_own[:, :, :ff]), columns_of(two_own[:, :, ff:])], axis=1)
    one_own = to_owner(one_grad)
    w_proj_grad = jnp.concatenate(
        [
            columns_of(one_own[:, :, :k]),
            columns_of(one_own[:, :, k : 2 * k]),
            columns_of(one_own[:, :, 2 * k : 2 * k + v]),
            columns_of(one_own[:, :, 2 * k + v : 2 * k + 2 * v]),
        ],
        axis=1,
    )
    own_tail = one_own[:, :, columns - TAIL :]
    w_decay_grad = jnp.concatenate(
        [columns_of(own_tail[:, :, :LH]), columns_of(own_tail[:, :, LH : 2 * LH])], axis=1
    )
    own_small = jnp.sum(own_tail[:, :, 2 * LH : 2 * LH + 2 + taps.shape[1]], axis=0)
    norm1_gain_grad = own_small[:, 0]
    norm2_gain_grad = own_small[:, 1]
    conv_grad = own_small[:, 2:].reshape(CONV, -1)

    tokens_perm_f = tokens_perm.astype(F32)
    scale_own = scale_one[:rows]
    weighted_one = grad_one * gain_one
    from_one = scale_own * weighted_one - tokens_perm_f * (
        scale_own**3 * jnp.mean(tokens_perm_f * weighted_one, axis=-1, keepdims=True)
    )
    tokens_grad = from_perm((grad_residual + from_one).astype(BF16))

    misc = jnp.sum(misc, axis=0)
    heads_zero = jnp.zeros((HEADS,), F32)
    head_vec = jnp.concatenate(
        [
            lax.dynamic_update_slice(heads_zero, misc[1, :LH], (mv.d * LH,)),
            lax.dynamic_update_slice(heads_zero, misc[2, :LH], (mv.d * LH,)),
            misc[0],
        ]
    )
    head_vec = lax.psum(head_vec, ("dp", "fsdp"))
    return (
        layer_out,
        tokens_grad,
        norm1_gain_grad,
        w_proj_grad,
        w_decay_grad,
        conv_grad,
        wout_grad.reshape(w_out.shape),
        head_vec[:HEADS],
        head_vec[HEADS : 2 * HEADS],
        head_vec[2 * HEADS :],
        norm2_gain_grad,
        w_gate_up_grad,
        wdown_grad.reshape(w_down.shape),
    )


def solution(mesh):
    rows = P(("dp", "fsdp"), None)
    flat = P(("dp", "fsdp"))
    in_specs = (rows, rows, flat, flat, flat, rows, rows, P(None, ("dp", "fsdp")), rows, P(), P(), P(), flat, rows, rows)
    out_specs = (rows, rows, flat, rows, rows, P(None, ("dp", "fsdp")), rows, P(), P(), P(), flat, rows, rows)
    return jax.shard_map(
        partial(local, fsdp_size=mesh.shape["fsdp"]),
        mesh=mesh,
        in_specs=in_specs,
        out_specs=out_specs,
        check_vma=False,
    )
```

```python
from functools import partial

import jax
import jax.numpy as jnp
from jax import lax
from jax.experimental import pallas as pl
from jax.experimental.pallas import tpu as pltpu
from jax.sharding import PartitionSpec as P

HEADS = 16
DK = 128
DV = 256
CONV = 4
BLOCK = 64
TP = 4
LH = HEADS // TP
TAIL = 128
EPS = 1e-06
HIGH = lax.Precision.HIGHEST
F32 = jnp.float32
BF16 = jnp.bfloat16


def mm(left, right, dims=((1,), (0,))):
    return lax.dot_general(left, right, (dims, ((), ())), preferred_element_type=F32)


def mmb(left, right, dims=((1,), (0,))):
    return mm(left.astype(BF16), right.astype(BF16), dims)


def mm3(left, right, dims=((1,), (0,))):
    left_hi = left.astype(BF16)
    right_hi = right.astype(BF16)
    left_lo = (left - left_hi.astype(F32)).astype(BF16)
    right_lo = (right - right_hi.astype(F32)).astype(BF16)
    return mm(left_hi, right_hi, dims) + (mm(left_hi, right_lo, dims) + mm(left_lo, right_hi, dims))


def mmx(left, right, dims=((1,), (0,))):
    return lax.dot_general(left, right, (dims, ((), ())), precision=HIGH, preferred_element_type=F32)


def sigmoid(v):
    return 1.0 / (1.0 + jnp.exp(-v))


def conv_rows(raw, taps, pos):
    total = raw * taps[CONV - 1 : CONV]
    for lag in range(1, CONV):
        moved = pltpu.roll(raw, lag, 0)
        total = total + jnp.where(pos >= lag, moved, 0.0) * taps[CONV - 1 - lag : CONV - lag]
    return total


def conv_back(grad, raw, taps, pos):
    rows = raw.shape[0]
    total = grad * taps[CONV - 1 : CONV]
    sums = [jnp.sum(grad * raw, axis=0, keepdims=True)]
    for lag in range(1, CONV):
        kept = jnp.where(pos >= lag, grad, 0.0)
        total = total + pltpu.roll(kept, rows - lag, 0) * taps[CONV - 1 - lag : CONV - lag]
        sums.append(jnp.sum(kept * pltpu.roll(raw, lag, 0), axis=0, keepdims=True))
    return total, sums[::-1]


def unit(v, scale):
    inv = lax.rsqrt(jnp.sum(v * v, axis=-1, keepdims=True) + EPS)
    return v * (inv * scale), inv


def unit_back(grad, v, inv, scale):
    g = grad * scale
    return inv * g - v * (inv * inv * inv * jnp.sum(v * g, axis=-1, keepdims=True))


def silu_back(grad, pre, sig):
    return grad * (sig * (1.0 + pre * (1.0 - sig)))


def group_terms(tail_ref, prm_ref, pos_ref):
    rows = tail_ref.shape[0]
    pos = pos_ref[:, 0:1].astype(jnp.int32)
    row_i = lax.broadcasted_iota(jnp.int32, (rows, rows), 0)
    row_j = lax.broadcasted_iota(jnp.int32, (rows, rows), 1)
    lower = (row_j <= row_i) & (row_j >= row_i - pos)
    raw = tail_ref[...]
    shifted = raw + prm_ref[1:2]
    soft = jnp.maximum(shifted, 0.0) + jnp.log1p(jnp.exp(-jnp.abs(shifted)))
    log_decay = prm_ref[0:1] * soft
    beta = sigmoid(raw)
    lower_f = lower.astype(F32)
    cum = mmx(lower_f, log_decay)
    return pos, row_i, row_j, lower, lower_f, raw, shifted, log_decay, beta, cum, cum.T


def head_slices(head):
    key_width = LH * DK
    return (
        slice(head * DK, (head + 1) * DK),
        slice(key_width + head * DK, key_width + (head + 1) * DK),
        slice(2 * key_width + head * DV, 2 * key_width + (head + 1) * DV),
        slice(2 * key_width + (LH + head) * DV, 2 * key_width + (LH + head + 1) * DV),
    )


def mixer_fwd_kernel(proj_ref, pos_ref, conv_ref, prm_ref, gain_ref, mixed_ref, inv_ref, new_ref):
    width = proj_ref.shape[1]
    tail_ref = proj_ref.at[:, width - TAIL :]
    pos, row_i, row_j, lower, _, _, _, _, beta_all, cum, cum_t = group_terms(tail_ref, prm_ref, pos_ref)
    strict = lower & (row_j < row_i)
    bits = row_i ^ row_j
    eye = (bits == 0).astype(F32)
    lows, attends, values = [], [], []
    for head in range(LH):
        sq, sk, sv, _ = head_slices(head)
        q_pre = conv_rows(proj_ref[:, sq], conv_ref[:, sq], pos)
        k_pre = conv_rows(proj_ref[:, sk], conv_ref[:, sk], pos)
        v_pre = conv_rows(proj_ref[:, sv], conv_ref[:, sv], pos)
        query, _ = unit(q_pre * sigmoid(q_pre), DK**-0.5)
        key, _ = unit(k_pre * sigmoid(k_pre), 1.0)
        beta = beta_all[:, LH + head : LH + head + 1]
        values.append(beta * (v_pre * sigmoid(v_pre)))
        gap = cum[:, head : head + 1] - cum_t[head : head + 1, :]
        decay = jnp.where(lower, jnp.exp(gap), 0.0)
        attends.append(mm3(query, key, ((1,), (1,))) * decay)
        lows.append(jnp.where(strict, beta * mm3(key, key, ((1,), (1,))) * decay, 0.0))
    invs = [eye - jnp.where(bits == 1, low, 0.0) for low in lows]
    step = 1
    while (2 << step) <= proj_ref.shape[0]:
        keep = (bits >> step) == 1
        parts = [mm3(jnp.where(keep, low, 0.0), inv) for low, inv in zip(lows, invs)]
        invs = [inv - mm3(inv, part) for inv, part in zip(invs, parts)]
        step += 1
    news = [mm3(inv, value) for inv, value in zip(invs, values)]
    mixes = [mm3(attend, new) for attend, new in zip(attends, news)]
    for head in range(LH):
        mix = mixes[head]
        scale = lax.rsqrt(jnp.mean(mix * mix, axis=-1, keepdims=True) + EPS)
        gate = proj_ref[:, head_slices(head)[3]]
        out = mix * scale * gain_ref[0:1] * (gate * sigmoid(gate))
        mixed_ref[:, head * DV : (head + 1) * DV] = out.astype(BF16)
        inv_ref[head] = invs[head]
        new_ref[:, head * DV : (head + 1) * DV] = news[head]


def mixer_bwd_kernel(
    proj_ref, pos_ref, conv_ref, prm_ref, gain_ref, inv_ref, new_ref, gmix_ref, gproj_ref, gconv_ref, misc_ref
):
    width = proj_ref.shape[1]
    rows = proj_ref.shape[0]
    tail_ref = proj_ref.at[:, width - TAIL :]
    pos, row_i, row_j, lower, lower_f, raw, shifted, log_decay, beta_all, cum, cum_t = group_terms(
        tail_ref, prm_ref, pos_ref
    )
    strict = lower & (row_j < row_i)
    lane = lax.broadcasted_iota(jnp.int32, (rows, TAIL), 1)
    ones = jnp.ones((rows, TAIL), F32)
    grad_cum = jnp.zeros((rows, TAIL), F32)
    grad_beta_all = jnp.zeros((rows, TAIL), F32)
    gain_sum = jnp.zeros((1, DV), F32)
    gconv_ref[...] = jnp.zeros_like(gconv_ref)
    misc_ref[...] = jnp.zeros_like(misc_ref)
    for head in range(LH):
        sq, sk, sv, sg = head_slices(head)
        q_raw, k_raw, v_raw = proj_ref[:, sq], proj_ref[:, sk], proj_ref[:, sv]
        q_pre = conv_rows(q_raw, conv_ref[:, sq], pos)
        k_pre = conv_rows(k_raw, conv_ref[:, sk], pos)
        v_pre = conv_rows(v_raw, conv_ref[:, sv], pos)
        q_sig, k_sig, v_sig = sigmoid(q_pre), sigmoid(k_pre), sigmoid(v_pre)
        q_act, k_act, value = q_pre * q_sig, k_pre * k_sig, v_pre * v_sig
        query, q_inv = unit(q_act, DK**-0.5)
        key, k_inv = unit(k_act, 1.0)
        query_b, key_b = query, key
        beta = beta_all[:, LH + head : LH + head + 1]
        gap = cum[:, head : head + 1] - cum_t[head : head + 1, :]
        decay = jnp.where(lower, jnp.exp(gap), 0.0)
        pair = mm3(key_b, key_b, ((1,), (1,)))
        query_pair = mm3(query_b, key_b, ((1,), (1,)))
        attend = query_pair * decay
        inv = inv_ref[head]
        new = new_ref[:, head * DV : (head + 1) * DV]
        mix = mm3(attend, new)
        scale = lax.rsqrt(jnp.mean(mix * mix, axis=-1, keepdims=True) + EPS)
        gate = proj_ref[:, sg]
        gate_sig = sigmoid(gate)
        grad_out = gmix_ref[:, head * DV : (head + 1) * DV]
        unscaled = mix * scale
        grad_norm = grad_out * (gate * gate_sig)
        grad_gate = silu_back(grad_out * unscaled * gain_ref[0:1], gate, gate_sig)
        gain_sum = gain_sum + jnp.sum(grad_norm * unscaled, axis=0, keepdims=True)
        weighted = grad_norm * gain_ref[0:1]
        grad_mix = scale * weighted - mix * (
            scale * scale * scale * jnp.mean(mix * weighted, axis=-1, keepdims=True)
        )
        grad_mix_b = grad_mix
        grad_new = mm3(attend, grad_mix_b, ((0,), (0,)))
        grad_attend = mm3(grad_mix_b, new, ((1,), (1,)))
        grad_rhs = mm3(inv, grad_new, ((0,), (0,)))
        grad_low = -mm3(grad_rhs, new, ((1,), (1,)))
        grad_value = beta * grad_rhs
        low_decay = jnp.where(strict, grad_low * decay, 0.0)
        low_pair = low_decay * pair
        grad_beta = jnp.sum(grad_rhs * value, axis=-1, keepdims=True) + jnp.sum(
            low_pair, axis=-1, keepdims=True
        )
        grad_pair = beta * low_decay
        grad_query_pair = grad_attend * decay
        both = beta * low_pair + grad_query_pair * query_pair
        column = jnp.sum(both, axis=-1, keepdims=True) - mmx(both, ones, ((0,), (0,)))
        grad_cum = jnp.where(lane == head, column, grad_cum)
        grad_beta_all = jnp.where(lane == LH + head, grad_beta, grad_beta_all)
        grad_pair_b = grad_pair
        grad_qp_b = grad_query_pair
        grad_query = mm3(grad_qp_b, key_b)
        grad_key = (
            mm3(grad_qp_b, query_b, ((0,), (0,))) + mm3(grad_pair_b, key_b) + mm3(grad_pair_b, key_b, ((0,), (0,)))
        )
        grad_q = silu_back(unit_back(grad_query, q_act, q_inv, DK**-0.5), q_pre, q_sig)
        grad_k = silu_back(unit_back(grad_key, k_act, k_inv, 1.0), k_pre, k_sig)
        grad_v = silu_back(grad_value, v_pre, v_sig)
        for grad, part, where in ((grad_q, q_raw, sq), (grad_k, k_raw, sk), (grad_v, v_raw, sv)):
            moved, sums = conv_back(grad, part, conv_ref[:, where], pos)
            gproj_ref[:, where] = moved.astype(BF16)
            for tap in range(CONV):
                gconv_ref[0, tap : tap + 1, where] = sums[tap]
        gproj_ref[:, sg] = grad_gate.astype(BF16)
    grad_log = mmx(lower_f, grad_cum, ((0,), (0,)))
    grad_step = grad_log * prm_ref[0:1] * sigmoid(shifted)
    grad_tail = grad_step + grad_beta_all * beta_all * (1.0 - beta_all)
    gproj_ref[:, width - TAIL :] = grad_tail.astype(BF16)
    misc_ref[0, 0:1, :] = gain_sum
    misc_ref[0, 1:2, 0:TAIL] = jnp.sum(grad_log * log_decay, axis=0, keepdims=True)
    misc_ref[0, 2:3, 0:TAIL] = jnp.sum(grad_step, axis=0, keepdims=True)


VMEM_LIMIT = 56 * 1024 * 1024


def mixer_fwd(proj, pos, conv, prm, gain):
    total, width = proj.shape
    rows = total // TP
    return pl.pallas_call(
        mixer_fwd_kernel,
        grid=(TP,),
        in_specs=[
            pl.BlockSpec((rows, width), lambda g: (g, 0)),
            pl.BlockSpec((rows, TAIL), lambda g: (g, 0)),
            pl.BlockSpec(conv.shape, lambda g: (0, 0)),
            pl.BlockSpec(prm.shape, lambda g: (0, 0)),
            pl.BlockSpec(gain.shape, lambda g: (0, 0)),
        ],
        out_specs=[
            pl.BlockSpec((rows, LH * DV), lambda g: (g, 0)),
            pl.BlockSpec((LH, rows, rows), lambda g: (g, 0, 0)),
            pl.BlockSpec((rows, LH * DV), lambda g: (g, 0)),
        ],
        out_shape=[
            jax.ShapeDtypeStruct((total, LH * DV), BF16),
            jax.ShapeDtypeStruct((TP * LH, rows, rows), F32),
            jax.ShapeDtypeStruct((total, LH * DV), F32),
        ],
        compiler_params=pltpu.CompilerParams(vmem_limit_bytes=VMEM_LIMIT),
        cost_estimate=pl.CostEstimate(flops=30_000_000_000, bytes_accessed=30_000_000, transcendentals=5_000_000),
        name="mixer_fwd",
    )(proj, pos, conv, prm, gain)


def mixer_bwd(proj, pos, conv, prm, gain, inv, new, gmix):
    total, width = proj.shape
    rows = total // TP
    return pl.pallas_call(
        mixer_bwd_kernel,
        grid=(TP,),
        in_specs=[
            pl.BlockSpec((rows, width), lambda g: (g, 0)),
            pl.BlockSpec((rows, TAIL), lambda g: (g, 0)),
            pl.BlockSpec(conv.shape, lambda g: (0, 0)),
            pl.BlockSpec(prm.shape, lambda g: (0, 0)),
            pl.BlockSpec(gain.shape, lambda g: (0, 0)),
            pl.BlockSpec((LH, rows, rows), lambda g: (g, 0, 0)),
            pl.BlockSpec((rows, LH * DV), lambda g: (g, 0)),
            pl.BlockSpec((rows, LH * DV), lambda g: (g, 0)),
        ],
        out_specs=[
            pl.BlockSpec((rows, width), lambda g: (g, 0)),
            pl.BlockSpec((1, 8, conv.shape[1]), lambda g: (g, 0, 0)),
            pl.BlockSpec((1, 8, DV), lambda g: (g, 0, 0)),
        ],
        out_shape=[
            jax.ShapeDtypeStruct((total, width), BF16),
            jax.ShapeDtypeStruct((TP, 8, conv.shape[1]), F32),
            jax.ShapeDtypeStruct((TP, 8, DV), F32),
        ],
        compiler_params=pltpu.CompilerParams(vmem_limit_bytes=VMEM_LIMIT),
        cost_estimate=pl.CostEstimate(flops=50_000_000_000, bytes_accessed=40_000_000, transcendentals=5_000_000),
        name="mixer_bwd",
    )(proj, pos, conv, prm, gain, inv, new, gmix)


MESH = pl.DeviceIdType.MESH
AHEAD = 3


class Place:
    def __init__(self, nf):
        self.nf, self.nz = nf, nf // 2
        self.d = lax.axis_index("dp")
        self.f = lax.axis_index("fsdp")
        self.z, self.y = self.f // 2, self.f % 2
        self.over = self.z < self.nz - 1
        self.under = self.z > 0

    def flip(self, value, mask):
        return value + mask * (1 - 2 * ((value // mask) % 2))

    def dp(self, mask):
        if mask == 3:
            return (self.flip(self.flip(self.d, 1), 2), self.f)
        return (self.flip(self.d, mask), self.f)

    def at_z(self, z):
        return (self.d, z * 2 + self.y)

    def beside(self):
        return (self.d, self.flip(self.f, 1))

    def greet(self):
        barrier = pltpu.get_barrier_semaphore()
        for mask in (1, 2, 3):
            pl.semaphore_signal(barrier, inc=1, device_id=self.dp(mask), device_id_type=MESH)
        pl.semaphore_signal(barrier, inc=1, device_id=self.beside(), device_id_type=MESH)

        @pl.when(self.over)
        def _():
            pl.semaphore_signal(barrier, inc=1, device_id=self.at_z(self.z + 1), device_id_type=MESH)

        @pl.when(self.under)
        def _():
            pl.semaphore_signal(barrier, inc=1, device_id=self.at_z(self.z - 1), device_id_type=MESH)

        pl.semaphore_wait(barrier, 4 + self.over.astype(jnp.int32) + self.under.astype(jnp.int32))


def send(src, dst, send_sem, recv_sem, device):
    return pltpu.make_async_remote_copy(
        src_ref=src, dst_ref=dst, send_sem=send_sem, recv_sem=recv_sem, device_id=device, device_id_type=MESH
    )


class Gather:
    def __init__(self, place, views, ready, up_send, down_send, z_recv, y_send, y_recv, pair_send, pair_recv):
        self.p, self.views, self.ready = place, views, ready
        self.up_send, self.down_send, self.z_recv = up_send, down_send, z_recv
        self.y_send, self.y_recv, self.pair_send, self.pair_recv = y_send, y_recv, pair_send, pair_recv
        self.ticks = len(views) + place.nz - 1

    @staticmethod
    def scratch(units, nz):
        return [
            pltpu.SemaphoreType.DMA((units, nz)),
            pltpu.SemaphoreType.DMA((units, nz)),
            pltpu.SemaphoreType.DMA((units, nz)),
            pltpu.SemaphoreType.DMA((units, nz)),
            pltpu.SemaphoreType.DMA((units, nz)),
            pltpu.SemaphoreType.DMA((units,)),
            pltpu.SemaphoreType.DMA((units,)),
        ]

    def block(self, u, z, y):
        return self.views[u](z * 2 + y)

    def up(self, u, r):
        ref = self.block(u, self.p.z - (r - 1), self.p.y)
        return send(ref, ref, self.up_send.at[u, r], self.z_recv.at[u, r], self.p.at_z(self.p.z + 1))

    def down(self, u, r):
        ref = self.block(u, self.p.z + (r - 1), self.p.y)
        nz = self.p.nz
        return send(ref, ref, self.down_send.at[u, r], self.z_recv.at[u, nz - r], self.p.at_z(self.p.z - 1))

    def over_y(self, u, r):
        ref = self.block(u, lax.rem(self.p.z - r + self.p.nz, self.p.nz), self.p.y)
        return send(ref, ref, self.y_send.at[u, r], self.y_recv.at[u, r], self.p.beside())

    def pair(self, u):
        ref = self.block(u, self.p.z, 1 - self.p.y)
        return send(ref, ref, self.pair_send.at[u], self.pair_recv.at[u], self.p.at_z(self.p.flip(self.p.z, 1)))

    def wait_z(self, u, r):
        ref = self.block(u, lax.rem(self.p.z - r + self.p.nz, self.p.nz), self.p.y)
        send(ref, ref, self.up_send.at[u, 1], self.z_recv.at[u, r], self.p.beside()).wait_recv()

    def wait_y(self, u, r):
        ref = self.block(u, lax.rem(self.p.z - r + self.p.nz, self.p.nz), 1 - self.p.y)
        send(ref, ref, self.y_send.at[u, r], self.y_recv.at[u, r], self.p.beside()).wait_recv()

    def wait_pair(self, u):
        other = self.p.flip(self.p.z, 1)
        ref = self.block(u, other, 1 - self.p.y)
        send(ref, ref, self.pair_send.at[u], self.pair_recv.at[u], self.p.at_z(other)).wait_recv()

    def odd(self, u):
        return u % 2 == 1

    def skips(self, u, r):
        if not self.odd(u) or r not in (1, self.p.nz - 1):
            return None
        odd = self.p.z % 2 == 1
        if self.p.nz == 2:
            return odd | ~odd
        return odd if r == 1 else ~odd

    def unless_skipped(self, u, r, action):
        skip = self.skips(u, r)
        if skip is None:
            action()
        else:
            pl.when(~skip)(action)

    def own(self, t):
        p = self.p
        self.ready[t]()

        @pl.when(p.over)
        def _():
            self.up(t, 1).start()

        @pl.when(p.under)
        def _():
            self.down(t, 1).start()

        self.over_y(t, 0).start()

    def tick(self, t):
        p, nz = self.p, self.p.nz
        for u in range(AHEAD + 1) if t == 0 else (t + AHEAD,):
            if u < len(self.views):
                self.own(u)
        for s in range(1, nz):
            u = t - s
            if not 0 <= u < len(self.views):
                continue

            @pl.when(p.z >= s)
            def _():
                self.wait_z(u, s)

                @pl.when(p.over)
                def _():
                    self.up(u, s + 1).start()

                self.unless_skipped(u, s, self.over_y(u, s).start)

            @pl.when(p.z <= nz - 1 - s)
            def _():
                self.wait_z(u, nz - s)

                @pl.when(p.under)
                def _():
                    self.down(u, s + 1).start()

                self.unless_skipped(u, nz - s, self.over_y(u, nz - s).start)

            if s == min(AHEAD, nz - 1) and self.odd(u):
                self.wait_y(u, 0)
                self.pair(u).start()

    def finish(self):
        p, nz = self.p, self.p.nz
        for u in range(len(self.views)):
            if not self.odd(u):
                self.wait_y(u, 0)
            else:
                self.wait_pair(u)
                self.pair(u).wait_send()
            self.over_y(u, 0).wait_send()
            for r in range(1, nz):

                def both():
                    self.wait_y(u, r)
                    self.over_y(u, r).wait_send()

                self.unless_skipped(u, r, both)
            for r in range(1, nz):

                @pl.when(p.over & (p.z >= r - 1))
                def _():
                    self.up(u, r).wait_send()

                @pl.when(p.under & (p.z <= nz - r))
                def _():
                    self.down(u, r).wait_send()


def gather_kernel(nf, packs, shards, groups, *refs):
    count = len(packs) + len(shards) + groups
    ins, outs = refs[:count], refs[count : 2 * count]
    to_send, to_recv, near_send, near_recv, local_sem = refs[2 * count : 2 * count + 5]
    p = Place(nf)
    pack_in, shard_in, group_in = ins[: len(packs)], ins[len(packs) : len(packs) + len(shards)], ins[count - groups :]
    pack_out, shard_out, group_out = (
        outs[: len(packs)],
        outs[len(packs) : len(packs) + len(shards)],
        outs[count - groups :],
    )

    def own_pack(i, d):
        return pack_out[i].at[d, p.f] if packs[i] else pack_out[i].at[d]

    def exchange(i, m):
        target = p.dp(m)
        return send(pack_in[i].at[target[0]], own_pack(i, p.d), to_send.at[i, m], to_recv.at[i, m], target)

    def wait_exchange(i, m):
        source = p.dp(m)
        ref = own_pack(i, source[0])
        send(ref, ref, to_send.at[i, m], to_recv.at[i, m], source).wait_recv()

    def near(j, k):
        src, dst, mask = ((group_in[j], 2, 2), (group_in[j], 1, 1), (group_out[j].at[2], 3, 1))[k]
        return send(src, group_out[j].at[dst], near_send.at[j, k], near_recv.at[j, k], p.dp(mask))

    def wait_near(j, k):
        ref = group_out[j].at[(2, 1, 3)[k]]
        send(ref, ref, near_send.at[j, k], near_recv.at[j, k], p.dp(1)).wait_recv()

    def local(n):
        if n < len(packs):
            return pltpu.make_async_copy(pack_in[n].at[p.d], own_pack(n, p.d), local_sem.at[n])
        if n < len(packs) + len(shards):
            i = n - len(packs)
            return pltpu.make_async_copy(shard_in[i], shard_out[i].at[p.f], local_sem.at[n])
        j = n - len(packs) - len(shards)
        return pltpu.make_async_copy(group_in[j], group_out[j].at[0], local_sem.at[n])

    p.greet()
    views, ready = [], []
    for i, whole in enumerate(packs):
        for m in range(TP if whole else 0):
            source = p.dp(m)[0] if m else p.d
            views.append(lambda f, i=i, d=source: pack_out[i].at[d, f])
            ready.append(partial(wait_exchange, i, m) if m else local(i).wait)
    for i in range(len(shards)):
        views.append(lambda f, i=i: shard_out[i].at[f])
        ready.append(local(len(packs) + i).wait)
    gather = Gather(p, views, ready, *refs[2 * count + 5 :])
    for n in range(count):
        local(n).start()
    for m in (1, 2, 3):
        exchange(0, m).start()
    for j in range(groups):
        near(j, 0).start()
        near(j, 1).start()
    for i in range(1, len(packs)):
        for m in (2, 3, 1):
            exchange(i, m).start()
    for t in range(gather.ticks):
        gather.tick(t)
        if t == 2:
            for j in range(groups):
                wait_near(j, 0)
                near(j, 2).start()
    gather.finish()
    for i, whole in enumerate(packs):
        for m in (1, 2, 3):
            exchange(i, m).wait_send()
            if not whole:
                wait_exchange(i, m)
        if not whole:
            local(i).wait()
    for j in range(groups):
        wait_near(j, 1)
        wait_near(j, 2)
        for k in range(3):
            near(j, k).wait_send()
        local(len(packs) + len(shards) + j).wait()


def gather_all(nf, collective_id, packs, shards, groups):
    marks = tuple(whole for _, whole in packs)
    ins = [array for array, _ in packs] + list(shards) + list(groups)
    outs = (
        [
            jax.ShapeDtypeStruct(array.shape[:1] + ((nf,) if whole else ()) + array.shape[1:], array.dtype)
            for array, whole in packs
        ]
        + [jax.ShapeDtypeStruct((nf,) + array.shape, array.dtype) for array in shards]
        + [jax.ShapeDtypeStruct((TP,) + array.shape, array.dtype) for array in groups]
    )
    units = TP * sum(marks) + len(shards)
    sent = sum(out.size * 2 for out in outs)
    any_space = pl.BlockSpec(memory_space=pl.ANY)
    return pl.pallas_call(
        partial(gather_kernel, nf, marks, (True,) * len(shards), len(groups)),
        in_specs=[any_space] * len(ins),
        out_specs=[any_space] * len(outs),
        out_shape=outs,
        scratch_shapes=[
            pltpu.SemaphoreType.DMA((len(packs), TP)),
            pltpu.SemaphoreType.DMA((len(packs), TP)),
            pltpu.SemaphoreType.DMA((max(len(groups), 1), 3)),
            pltpu.SemaphoreType.DMA((max(len(groups), 1), 3)),
            pltpu.SemaphoreType.DMA((len(ins),)),
        ]
        + Gather.scratch(units, nf // 2),
        compiler_params=pltpu.CompilerParams(
            collective_id=collective_id, has_side_effects=True, vmem_limit_bytes=1024 * 1024
        ),
        cost_estimate=pl.CostEstimate(flops=0, bytes_accessed=2 * sent, transcendentals=0),
        name="gather_" + str(collective_id),
    )(*ins)


def add_into(dst, srcs):
    rows = dst.shape[-2]
    size = 16 if rows % 16 == 0 else rows
    lead = dst.shape[0] if len(dst.shape) == 3 else 1

    def body(i, _):
        at = pl.ds(pl.multiple_of((i % (rows // size)) * size, size), size)
        where = (i // (rows // size), at) if len(dst.shape) == 3 else (at,)
        total = srcs[0][where].astype(F32)
        for src in srcs[1:]:
            total = total + src[where].astype(F32)
        dst[where] = total.astype(dst.dtype)
        return 0

    lax.fori_loop(0, lead * (rows // size), body, 0)


class Reduce:
    def __init__(self, place, part, done, y_in, z_in, pair_in, sems):
        self.p, self.part, self.done = place, part, done
        self.y_in, self.z_in, self.pair_in = y_in, z_in, pair_in
        self.y_send, self.y_recv, self.z_send, self.z_recv, self.pair_send, self.pair_recv = sems
        self.count = len(y_in)
        self.ticks = self.count + place.nz

    @staticmethod
    def scratch(blocks, nz):
        units = len(blocks)
        return (
            [pltpu.VMEM((nz,) + block, BF16) for block in blocks]
            + [pltpu.VMEM((nz + 1,) + block, BF16) for block in blocks]
            + [pltpu.VMEM(block, BF16) for block in blocks]
            + [pltpu.SemaphoreType.DMA((units, nz))] * 3
            + [pltpu.SemaphoreType.DMA((units, nz + 1))]
            + [pltpu.SemaphoreType.DMA((units,))] * 2
        )

    def odd(self, u):
        return u % 2 == 1

    def copy_y(self, u, z0):
        src = self.part(u, z0 * 2 + 1 - self.p.y)
        return send(src, self.y_in[u].at[z0], self.y_send.at[u, z0], self.y_recv.at[u, z0], self.p.beside())

    def copy_late(self, u):
        z = self.p.z
        return send(self.pair_in[u], self.y_in[u].at[z], self.y_send.at[u, z], self.y_recv.at[u, z], self.p.beside())

    def copy_pair(self, u):
        other = self.p.flip(self.p.z, 1)
        src = self.part(u, other * 2 + 1 - self.p.y)
        return send(src, self.pair_in[u], self.pair_send.at[u], self.pair_recv.at[u], self.p.at_z(other))

    def copy_z(self, u, z0, slot, z):
        return send(self.y_in[u].at[z0], self.z_in[u].at[slot], self.z_send.at[u, z0], self.z_recv.at[u, slot], self.p.at_z(z))

    def wait_z(self, u, slot):
        ref = self.z_in[u].at[slot]
        send(ref, ref, self.z_send.at[u, 0], self.z_recv.at[u, slot], self.p.beside()).wait_recv()

    def pass_on(self, u, z0, arrived, slot, z):
        own = self.part(u, z0 * 2 + self.p.y)
        here = self.y_in[u].at[z0]
        if self.odd(u):
            other = self.p.flip(self.p.z, 1)

            @pl.when(other != z0)
            def _():
                add_into(here, [own, here] + arrived)

            @pl.when(other == z0)
            def _():
                add_into(here, [own] + arrived)
        else:
            add_into(here, [own, here] + arrived)
        self.copy_z(u, z0, slot, z).start()

    def tick(self, t):
        p, nz = self.p, self.p.nz
        if t < self.count:
            if self.odd(t):
                self.copy_pair(t).start()
                other = p.flip(p.z, 1)
                for z0 in range(nz):

                    @pl.when((z0 != p.z) & (z0 != other))
                    def _():
                        self.copy_y(t, z0).start()
            else:
                for z0 in range(nz):
                    self.copy_y(t, z0).start()
        u = t - 1
        if 0 <= u < self.count:
            if self.odd(u):
                self.copy_pair(u).wait_recv()
                add_into(self.pair_in[u], [self.pair_in[u], self.part(u, p.z * 2 + 1 - p.y)])
                self.copy_late(u).start()
            other = p.flip(p.z, 1)
            for z0 in range(nz):
                needed = (z0 != p.z) & (z0 != other) if self.odd(u) else z0 != p.z

                @pl.when(needed)
                def _():
                    self.copy_y(u, z0).wait_recv()

            @pl.when(p.z == nz - 1)
            def _():
                for z0 in range(nz - 1):
                    self.pass_on(u, z0, [], z0, p.z - 1)

            @pl.when(p.z == 0)
            def _():
                for z0 in range(nz - 1, 0, -1):
                    self.pass_on(u, z0, [], nz if z0 == 1 else z0, p.z + 1)

        for hop in range(1, nz):
            u = t - 1 - hop
            if not 0 <= u < self.count:
                continue

            @pl.when(p.z == nz - 1 - hop)
            def _():
                for z0 in range(nz - hop):
                    self.wait_z(u, z0)
                    if z0 < nz - 1 - hop:
                        self.pass_on(u, z0, [self.z_in[u].at[z0]], z0, p.z - 1)

            @pl.when(p.z == hop)
            def _():
                for z0 in range(nz - 1, hop - 1, -1):
                    slot = nz if z0 == hop else z0
                    self.wait_z(u, slot)
                    if z0 > hop:
                        self.pass_on(u, z0, [self.z_in[u].at[z0]], nz if z0 == hop + 1 else z0, p.z + 1)

        u = t - nz
        if 0 <= u < self.count:
            self.copy_y(u, p.z).wait_recv()
            own = [self.part(u, p.f), self.y_in[u].at[p.z]]
            above, below = self.z_in[u].at[p.z], self.z_in[u].at[nz]

            @pl.when(p.z == 0)
            def _():
                self.done(u, own + [above])

            @pl.when(p.z == nz - 1)
            def _():
                self.done(u, own + [below])

            @pl.when(p.over & p.under)
            def _():
                self.done(u, own + [above, below])

    def finish(self):
        p, nz = self.p, self.p.nz
        other = p.flip(p.z, 1)
        for u in range(self.count):
            if self.odd(u):
                self.copy_pair(u).wait_send()
                self.copy_late(u).wait_send()
            for z0 in range(nz):
                needed = (z0 != p.z) & (z0 != other) if self.odd(u) else None
                if needed is None:
                    self.copy_y(u, z0).wait_send()
                else:

                    @pl.when(needed)
                    def _():
                        self.copy_y(u, z0).wait_send()

                @pl.when(z0 != p.z)
                def _():
                    self.copy_z(u, z0, z0, p.z).wait_send()


def reduce_kernel(nf, kinds, units, groups, vecs, *refs):
    arrays = len(kinds)
    count = arrays + groups + vecs
    ins, outs, rest = refs[:count], refs[count : 2 * count], refs[2 * count :]
    p = Place(nf)
    nz = p.nz
    n = len(units)
    y_in, z_in, pair_in, rest = rest[:n], rest[n : 2 * n], rest[2 * n : 3 * n], rest[3 * n :]
    sems, rest = rest[:6], rest[6:]
    packs = [u for u, (i, _, _) in enumerate(units) if kinds[i]]
    final = dict(zip(packs, rest[: len(packs)]))
    rest = rest[len(packs) :]
    to_send, to_recv, to_local, rest = rest[0], rest[1], rest[2], rest[3:]
    if groups:
        group_in, group_sems, rest = rest[0], rest[1:3], rest[3:]
    if vecs:
        vec_in, vec_own, vec_sems = rest[0], rest[1], rest[2:4]

    def part(u, f):
        i, start, size = units[u]
        columns = pl.ds(start, size)
        return ins[i].at[:, f, :, columns] if kinds[i] else ins[i].at[f, :, columns]

    def owner_copy(u, m):
        i, start, size = units[u]
        target = p.dp(m)
        return send(
            final[u].at[target[0]],
            outs[i].at[p.d, :, pl.ds(start, size)],
            to_send.at[u, m],
            to_recv.at[u, m],
            target,
        )

    def owner_local(u):
        i, start, size = units[u]
        return pltpu.make_async_copy(final[u].at[p.d], outs[i].at[p.d, :, pl.ds(start, size)], to_local.at[u])

    def done(u, sources):
        i, start, size = units[u]
        if kinds[i]:
            add_into(final[u], sources)
        else:
            add_into(outs[i].at[:, pl.ds(start, size)], sources)

    def wait_owner(u, m):
        i, start, size = units[u]
        source = p.dp(m)
        ref = outs[i].at[source[0], :, pl.ds(start, size)]
        send(ref, ref, to_send.at[u, m], to_recv.at[u, m], source).wait_recv()

    def group_copy(j, k):
        src, mask = ((ins[arrays + j].at[1], 1), (ins[arrays + j].at[3], 1), (group_in.at[j, 1], 2))[k]
        return send(src, group_in.at[j, (0, 1, 2)[k]], group_sems[0].at[j, k], group_sems[1].at[j, k], p.dp(mask))

    def vec_copy(k):
        device = (p.dp(1), p.dp(2), p.beside())[k]
        return send(vec_own.at[k], vec_in.at[k], vec_sems[0].at[k], vec_sems[1].at[k], device)

    def vec_z(k):
        z = lax.rem(p.z + k, nz)
        return send(vec_own.at[3], vec_in.at[3 + p.z], vec_sems[0].at[2 + k], vec_sems[1].at[2 + k], p.at_z(z))

    def vec_step(k):
        if k:
            vec_copy(k - 1).wait()
            vec_own[k] = vec_own[k - 1] + vec_in[k - 1]
        else:
            vec_own[0] = ins[arrays + groups][...]
        if k < 3:
            vec_copy(k).start()

    p.greet()
    red = Reduce(p, part, done, y_in, z_in, pair_in, sems)
    for j in range(groups):
        group_copy(j, 0).start()
        group_copy(j, 1).start()
    for t in range(red.ticks):
        red.tick(t)
        u = t - nz
        if u in final:
            for m in (2, 3, 1):
                owner_copy(u, m).start()
            owner_local(u).start()
        if t == 0:
            for j in range(groups):
                group_copy(j, 0).wait_recv()
                group_copy(j, 1).wait_recv()
                add_into(group_in.at[j, 1], [ins[arrays + j].at[2], group_in.at[j, 1]])
                group_copy(j, 2).start()
        if vecs and t < 4:
            vec_step(t)
    for j in range(groups):
        group_copy(j, 2).wait_recv()
        add_into(outs[arrays + j], [ins[arrays + j].at[0], group_in.at[j, 0], group_in.at[j, 2]])
        for k in range(3):
            group_copy(j, k).wait_send()
    if vecs:
        vec_in[3 + p.z] = vec_own[3]
        for k in range(1, nz):
            vec_z(k).start()
        for k in range(1, nz):
            source = lax.rem(p.z - k + nz, nz)
            ref = vec_in.at[3 + source]
            send(ref, ref, vec_sems[0].at[2 + k], vec_sems[1].at[2 + k], p.at_z(source)).wait_recv()
        total = vec_in[3]
        for k in range(1, nz):
            total = total + vec_in[3 + k]
        outs[arrays + groups][...] = total
        for k in range(1, nz):
            vec_z(k).wait_send()
    red.finish()
    for u in packs:
        owner_local(u).wait()
        for m in (1, 2, 3):
            owner_copy(u, m).wait_send()
            wait_owner(u, m)


def reduce_all(nf, collective_id, arrays, widths, groups=(), vec=None):
    nz = nf // 2
    kinds = tuple(array.ndim == 4 for array in arrays)
    units, blocks = [], []
    for i, (array, width) in enumerate(zip(arrays, widths)):
        for start in range(0, array.shape[-1], width):
            size = min(width, array.shape[-1] - start)
            units.append((i, start, size))
            blocks.append(((TP,) if kinds[i] else ()) + (array.shape[-2], size))
    final = [pltpu.VMEM(block, BF16) for block, unit in zip(blocks, units) if kinds[unit[0]]]
    scratch = Reduce.scratch(blocks, nz) + final
    scratch += [
        pltpu.SemaphoreType.DMA((len(units), TP)),
        pltpu.SemaphoreType.DMA((len(units), TP)),
        pltpu.SemaphoreType.DMA((len(units),)),
    ]
    if groups:
        scratch += [pltpu.VMEM((len(groups), 3) + groups[0].shape[1:], BF16)]
        scratch += [pltpu.SemaphoreType.DMA((len(groups), 3))] * 2
    if vec is not None:
        scratch += [pltpu.VMEM((3 + nz, 8, TAIL), F32), pltpu.VMEM((4, 8, TAIL), F32)]
        scratch += [pltpu.SemaphoreType.DMA((2 + nz,))] * 2
    vmem, any_space = pl.BlockSpec(memory_space=pltpu.VMEM), pl.BlockSpec(memory_space=pl.ANY)
    outs, out_specs = [], []
    for array, kind in zip(arrays, kinds):
        if kind:
            outs.append(jax.ShapeDtypeStruct((TP,) + array.shape[2:], BF16))
            out_specs.append(any_space)
        else:
            outs.append(jax.ShapeDtypeStruct(array.shape[1:], F32))
            out_specs.append(vmem)
    for array in groups:
        outs.append(jax.ShapeDtypeStruct(array.shape[1:], F32))
        out_specs.append(vmem)
    vecs = []
    if vec is not None:
        vecs = [vec]
        outs.append(jax.ShapeDtypeStruct(vec.shape, F32))
        out_specs.append(vmem)
    ins = list(arrays) + list(groups) + vecs
    return pl.pallas_call(
        partial(reduce_kernel, nf, kinds, tuple(units), len(groups), len(vecs)),
        in_specs=[vmem] * len(ins),
        out_specs=out_specs,
        out_shape=outs,
        scratch_shapes=scratch,
        compiler_params=pltpu.CompilerParams(
            collective_id=collective_id, has_side_effects=True, vmem_limit_bytes=VMEM_LIMIT
        ),
        cost_estimate=pl.CostEstimate(
            flops=0, bytes_accessed=sum(2 * a.size * a.dtype.itemsize for a in ins), transcendentals=0
        ),
        name="reduce_" + str(collective_id),
    )(*ins)


def dp_swap(value, mask):
    return lax.ppermute(value, "dp", [(i, i ^ mask) for i in range(TP)])


def dp_gather(value):
    far = dp_swap(value, 2)
    near = dp_swap(value, 1)
    return jnp.stack([value, near, far, dp_swap(far, 1)])


def dp_reduce(parts):
    got = dp_swap(jnp.stack([parts[1], parts[3]]), 1)
    mine = parts[0].astype(F32) + got[0].astype(F32)
    far = (parts[2].astype(F32) + got[1].astype(F32)).astype(BF16)
    return mine + dp_swap(far, 2).astype(F32)


def local(
    tokens,
    out_grad,
    block_first,
    block_live,
    norm1_gain,
    w_proj,
    w_decay,
    conv_w,
    w_out,
    a_log,
    dt_bias,
    head_gain,
    norm2_gain,
    w_gate_up,
    w_down,
    *,
    fsdp_size,
):
    nf = fsdp_size
    me = lax.axis_index("dp")
    rows, width = tokens.shape
    own = w_proj.shape[0]
    key_width = HEADS * DK
    value_width = HEADS * DV
    ff = w_down.shape[0] * nf

    block_index = jnp.arange(block_first.shape[0], dtype=jnp.int32)
    earlier = (block_index[:, None] >= block_index[None]) & (block_first[None] > 0)
    bucket_starts = jnp.max(jnp.where(earlier, block_index[None] * BLOCK, 0), axis=1)
    row_index = jnp.arange(rows, dtype=jnp.int32)
    position = row_index - jnp.repeat(bucket_starts, BLOCK)
    live = (row_index % BLOCK < jnp.repeat(block_live, BLOCK)).astype(F32)[:, None]

    def by_target(value):
        return value.reshape(own, TP, -1).swapaxes(0, 1)

    taps = conv_w.reshape(own, -1)
    tail = jnp.concatenate(
        [
            by_target(w_decay[:, :HEADS]),
            by_target(w_decay[:, HEADS:]),
            jnp.broadcast_to(
                jnp.concatenate([norm1_gain[:, None], norm2_gain[:, None], taps], axis=1)[None],
                (TP, own, 2 + taps.shape[1]),
            ),
        ],
        axis=2,
    )
    tail = jnp.pad(tail, ((0, 0), (0, 0), (0, TAIL - tail.shape[2])))
    pack_one = jnp.concatenate(
        [
            by_target(w_proj[:, :key_width]),
            by_target(w_proj[:, key_width : 2 * key_width]),
            by_target(w_proj[:, 2 * key_width : 2 * key_width + value_width]),
            by_target(w_proj[:, 2 * key_width + value_width :]),
            tail,
        ],
        axis=2,
    )
    pack_gate = by_target(w_gate_up[:, : ff * TP])
    pack_up = by_target(w_gate_up[:, ff * TP :])
    extra = jnp.broadcast_to(position.astype(BF16)[:, None], (rows, TAIL))
    cotangent = live * out_grad.astype(F32)
    proj_full, gate_full, up_full, out_full, down_full, group, grad_down = gather_all(
        nf,
        1,
        ((pack_one, True), (pack_gate, True), (pack_up, True)),
        (w_out, w_down),
        (jnp.concatenate([tokens, extra], axis=1), cotangent.astype(BF16)),
    )
    proj_full = proj_full.reshape(width, -1)
    gate_full = gate_full.reshape(width, ff)
    up_full = up_full.reshape(width, ff)
    out_full = out_full.reshape(-1, width)
    down_full = down_full.reshape(ff, width)
    group = group.reshape(TP * rows, width + TAIL)
    grad_down = grad_down.reshape(TP * rows, width)
    group_pos = group[:, width:].astype(F32)
    group_tokens = group[:, :width].astype(F32)

    tail_full = proj_full[:, -TAIL:]
    gain_one = tail_full[:, 2 * LH].astype(F32)
    gain_two = tail_full[:, 2 * LH + 1].astype(F32)
    taps_full = tail_full[:, 2 * LH + 2 : 2 * LH + 2 + taps.shape[1]]
    taps_full = (
        taps_full.reshape(TP * nf, CONV, -1).swapaxes(0, 1).reshape(CONV, 2 * key_width + value_width).astype(F32)
    )

    def my_columns(value):
        k, v = LH * DK, LH * DV
        return jnp.concatenate(
            [
                lax.dynamic_slice_in_dim(value, me * k, k, 1),
                lax.dynamic_slice_in_dim(value, key_width + me * k, k, 1),
                lax.dynamic_slice_in_dim(value, 2 * key_width + me * v, v, 1),
            ],
            axis=1,
        )

    conv_mine = jnp.pad(my_columns(taps_full), ((0, 8 - CONV), (0, 0)))
    rate = -jnp.exp(lax.dynamic_slice_in_dim(a_log, me * LH, LH))
    bias = lax.dynamic_slice_in_dim(dt_bias, me * LH, LH)
    prm = jnp.pad(jnp.stack([rate, bias]), ((0, 6), (0, TAIL - LH)))
    gain_head = jnp.broadcast_to(head_gain[None], (8, DV))

    scale_one = lax.rsqrt(jnp.mean(group_tokens * group_tokens, axis=-1, keepdims=True) + EPS)
    normed_one = (group_tokens * scale_one * gain_one).astype(BF16)
    proj = mm(normed_one, proj_full)
    mixed, inv, new = mixer_fwd(proj, group_pos, conv_mine, prm, gain_head)
    mixed_out = mm(mixed, out_full).astype(BF16).reshape(TP, rows, width)
    residual = tokens.astype(F32) + dp_reduce(mixed_out)
    scale_two = lax.rsqrt(jnp.mean(residual * residual, axis=-1, keepdims=True) + EPS)
    normed_two = dp_gather((residual * scale_two * gain_two).astype(BF16)).reshape(TP * rows, width)
    gate = mm(normed_two, gate_full)
    up = mm(normed_two, up_full)
    gate_sig = jax.nn.sigmoid(gate)
    gate_act = gate * gate_sig
    hidden = (gate_act * up).astype(BF16)
    down_out = mm(hidden, down_full).astype(BF16).reshape(TP, rows, width)
    layer_out = (live * (residual + dp_reduce(down_out))).astype(BF16)

    grad_wdown = mm(hidden, grad_down, ((0,), (0,))).astype(BF16).reshape(nf, -1, width)
    grad_hidden = mm(grad_down, down_full, ((1,), (1,)))
    grad_gate = (grad_hidden * up * gate_sig * (1.0 + gate * (1.0 - gate_sig))).astype(BF16)
    grad_up = (grad_hidden * gate_act).astype(BF16)
    gate_grad, up_grad = (
        mm(normed_two, grad, ((0,), (0,))).astype(BF16).reshape(TP, nf, own, ff) for grad in (grad_gate, grad_up)
    )
    gate_grad, up_grad, wdown_grad = reduce_all(nf, 2, (gate_grad, up_grad, grad_wdown), (768, 768, 1024))
    grad_two = mm(grad_gate, gate_full, ((1,), (1,))) + mm(grad_up, up_full, ((1,), (1,)))
    grad_two = dp_reduce(grad_two.astype(BF16).reshape(TP, rows, width))
    weighted = grad_two * gain_two
    gain_two_part = jnp.sum(grad_two * residual * scale_two, axis=0)
    grad_residual = (
        cotangent
        + scale_two * weighted
        - residual * (scale_two**3 * jnp.mean(residual * weighted, axis=-1, keepdims=True))
    )

    grad_mixed_in = dp_gather(grad_residual.astype(BF16)).reshape(TP * rows, width)
    wout_grad = mm(mixed, grad_mixed_in, ((0,), (0,))).astype(BF16).reshape(nf, -1, width)
    grad_mixed = mm(grad_mixed_in, out_full, ((1,), (1,)))
    grad_proj, grad_taps, misc = mixer_bwd(
        proj, group_pos, conv_mine, prm, gain_head, inv, new, grad_mixed
    )
    grad_one_part = mm(grad_proj, proj_full, ((1,), (1,)))
    gain_one_part = jnp.sum(grad_one_part * group_tokens * scale_one, axis=0)

    grad_taps = jnp.sum(grad_taps[:, :CONV], axis=0)
    k, v = LH * DK, LH * DV
    taps_all = jnp.zeros((CONV, 2 * key_width + value_width), F32)
    taps_all = lax.dynamic_update_slice(taps_all, grad_taps[:, :k], (0, me * k))
    taps_all = lax.dynamic_update_slice(taps_all, grad_taps[:, k : 2 * k], (0, key_width + me * k))
    taps_all = lax.dynamic_update_slice(taps_all, grad_taps[:, 2 * k :], (0, 2 * key_width + me * v))
    taps_all = taps_all.reshape(CONV, TP * nf, -1).swapaxes(0, 1).reshape(width, taps.shape[1])
    small = jnp.concatenate([gain_one_part[:, None], gain_two_part[:, None], taps_all], axis=1)
    columns = proj.shape[1]
    small = jnp.pad(small, ((0, 0), (columns - TAIL + 2 * LH, TAIL - 2 * LH - small.shape[1])))
    one_grad = (mm(normed_one, grad_proj, ((0,), (0,))) + small).astype(BF16).reshape(TP, nf, own, columns)

    misc = jnp.sum(misc, axis=0)
    heads_zero = jnp.zeros((HEADS,), F32)
    head_vec = jnp.concatenate(
        [
            lax.dynamic_update_slice(heads_zero, misc[1, :LH], (me * LH,)),
            lax.dynamic_update_slice(heads_zero, misc[2, :LH], (me * LH,)),
            misc[0],
        ]
    )
    head_vec = jnp.pad(head_vec, (0, 8 * TAIL - head_vec.shape[0])).reshape(8, TAIL)
    one_own, wout_grad, grad_one, head_vec = reduce_all(
        nf,
        3,
        (one_grad, wout_grad),
        (640, 2048),
        (grad_one_part.astype(BF16).reshape(TP, rows, width),),
        head_vec,
    )
    head_vec = head_vec.reshape(-1)
    one_own = one_own.astype(F32)

    def columns_of(value):
        return value.swapaxes(0, 1).reshape(own, -1)

    w_gate_up_grad = jnp.concatenate(
        [columns_of(gate_grad.astype(F32)), columns_of(up_grad.astype(F32))], axis=1
    )
    w_proj_grad = jnp.concatenate(
        [
            columns_of(one_own[:, :, :k]),
            columns_of(one_own[:, :, k : 2 * k]),
            columns_of(one_own[:, :, 2 * k : 2 * k + v]),
            columns_of(one_own[:, :, 2 * k + v : 2 * k + 2 * v]),
        ],
        axis=1,
    )
    own_tail = one_own[:, :, columns - TAIL :]
    w_decay_grad = jnp.concatenate(
        [columns_of(own_tail[:, :, :LH]), columns_of(own_tail[:, :, LH : 2 * LH])], axis=1
    )
    own_small = jnp.sum(own_tail[:, :, 2 * LH : 2 * LH + 2 + taps.shape[1]], axis=0)
    norm1_gain_grad = own_small[:, 0]
    norm2_gain_grad = own_small[:, 1]
    conv_grad = own_small[:, 2:].reshape(CONV, -1)

    tokens_f = tokens.astype(F32)
    scale_own = scale_one[:rows]
    weighted_one = grad_one * gain_one
    from_one = scale_own * weighted_one - tokens_f * (
        scale_own**3 * jnp.mean(tokens_f * weighted_one, axis=-1, keepdims=True)
    )
    tokens_grad = (grad_residual + from_one).astype(BF16)
    return (
        layer_out,
        tokens_grad,
        norm1_gain_grad,
        w_proj_grad,
        w_decay_grad,
        conv_grad,
        wout_grad.reshape(w_out.shape),
        head_vec[:HEADS],
        head_vec[HEADS : 2 * HEADS],
        head_vec[2 * HEADS : 2 * HEADS + DV],
        norm2_gain_grad,
        w_gate_up_grad,
        wdown_grad.reshape(w_down.shape),
    )


def solution(mesh):
    rows = P(("dp", "fsdp"), None)
    flat = P(("dp", "fsdp"))
    in_specs = (rows, rows, flat, flat, flat, rows, rows, P(None, ("dp", "fsdp")), rows, P(), P(), P(), flat, rows, rows)
    out_specs = (rows, rows, flat, rows, rows, P(None, ("dp", "fsdp")), rows, P(), P(), P(), flat, rows, rows)
    return jax.shard_map(
        partial(local, fsdp_size=mesh.shape["fsdp"]),
        mesh=mesh,
        in_specs=in_specs,
        out_specs=out_specs,
        check_vma=False,
    )
```

```python
from functools import partial

import jax
import jax.numpy as jnp
from jax import lax
from jax.experimental import pallas as pl
from jax.experimental.pallas import tpu as pltpu
from jax.sharding import PartitionSpec as P

HEADS = 16
DK = 128
DV = 256
CONV = 4
BLOCK = 64
TP = 4
LH = HEADS // TP
TAIL = 128
EPS = 1e-06
HIGH = lax.Precision.HIGHEST
F32 = jnp.float32
BF16 = jnp.bfloat16


def mm(left, right, dims=((1,), (0,))):
    return lax.dot_general(left, right, (dims, ((), ())), preferred_element_type=F32)


def mmb(left, right, dims=((1,), (0,))):
    return mm(left.astype(BF16), right.astype(BF16), dims)


def mm3(left, right, dims=((1,), (0,))):
    left_hi = left.astype(BF16)
    right_hi = right.astype(BF16)
    left_lo = (left - left_hi.astype(F32)).astype(BF16)
    right_lo = (right - right_hi.astype(F32)).astype(BF16)
    return mm(left_hi, right_hi, dims) + (mm(left_hi, right_lo, dims) + mm(left_lo, right_hi, dims))


def mmx(left, right, dims=((1,), (0,))):
    return lax.dot_general(left, right, (dims, ((), ())), precision=HIGH, preferred_element_type=F32)


def sigmoid(v):
    return 1.0 / (1.0 + jnp.exp(-v))


def conv_rows(raw, taps, pos):
    total = raw * taps[CONV - 1 : CONV]
    for lag in range(1, CONV):
        moved = pltpu.roll(raw, lag, 0)
        total = total + jnp.where(pos >= lag, moved, 0.0) * taps[CONV - 1 - lag : CONV - lag]
    return total


def conv_back(grad, raw, taps, pos):
    rows = raw.shape[0]
    total = grad * taps[CONV - 1 : CONV]
    sums = [jnp.sum(grad * raw, axis=0, keepdims=True)]
    for lag in range(1, CONV):
        kept = jnp.where(pos >= lag, grad, 0.0)
        total = total + pltpu.roll(kept, rows - lag, 0) * taps[CONV - 1 - lag : CONV - lag]
        sums.append(jnp.sum(kept * pltpu.roll(raw, lag, 0), axis=0, keepdims=True))
    return total, sums[::-1]


def unit(v, scale):
    inv = lax.rsqrt(jnp.sum(v * v, axis=-1, keepdims=True) + EPS)
    return v * (inv * scale), inv


def unit_back(grad, v, inv, scale):
    g = grad * scale
    return inv * g - v * (inv * inv * inv * jnp.sum(v * g, axis=-1, keepdims=True))


def silu_back(grad, pre, sig):
    return grad * (sig * (1.0 + pre * (1.0 - sig)))


def group_terms(tail_ref, prm_ref, pos_ref):
    rows = tail_ref.shape[0]
    pos = pos_ref[:, 0:1].astype(jnp.int32)
    row_i = lax.broadcasted_iota(jnp.int32, (rows, rows), 0)
    row_j = lax.broadcasted_iota(jnp.int32, (rows, rows), 1)
    lower = (row_j <= row_i) & (row_j >= row_i - pos)
    raw = tail_ref[...]
    shifted = raw + prm_ref[1:2]
    soft = jnp.maximum(shifted, 0.0) + jnp.log1p(jnp.exp(-jnp.abs(shifted)))
    log_decay = prm_ref[0:1] * soft
    beta = sigmoid(raw)
    lower_f = lower.astype(F32)
    cum = mmx(lower_f, log_decay)
    return pos, row_i, row_j, lower, lower_f, raw, shifted, log_decay, beta, cum, cum.T


def head_slices(head):
    key_width = LH * DK
    return (
        slice(head * DK, (head + 1) * DK),
        slice(key_width + head * DK, key_width + (head + 1) * DK),
        slice(2 * key_width + head * DV, 2 * key_width + (head + 1) * DV),
        slice(2 * key_width + (LH + head) * DV, 2 * key_width + (LH + head + 1) * DV),
    )


def mixer_forward(proj_ref, pos_ref, conv_ref, prm_ref, gain_ref, mixed_ref, inv_ref, new_ref):
    width = proj_ref.shape[1]
    tail_ref = proj_ref.at[:, width - TAIL :]
    pos, row_i, row_j, lower, _, _, _, _, beta_all, cum, cum_t = group_terms(tail_ref, prm_ref, pos_ref)
    strict = lower & (row_j < row_i)
    bits = row_i ^ row_j
    eye = (bits == 0).astype(F32)
    lows, attends, values = [], [], []
    for head in range(LH):
        sq, sk, sv, _ = head_slices(head)
        q_pre = conv_rows(proj_ref[:, sq], conv_ref[:, sq], pos)
        k_pre = conv_rows(proj_ref[:, sk], conv_ref[:, sk], pos)
        v_pre = conv_rows(proj_ref[:, sv], conv_ref[:, sv], pos)
        query, _ = unit(q_pre * sigmoid(q_pre), DK**-0.5)
        key, _ = unit(k_pre * sigmoid(k_pre), 1.0)
        beta = beta_all[:, LH + head : LH + head + 1]
        values.append(beta * (v_pre * sigmoid(v_pre)))
        gap = cum[:, head : head + 1] - cum_t[head : head + 1, :]
        decay = jnp.where(lower, jnp.exp(gap), 0.0)
        attends.append(mm3(query, key, ((1,), (1,))) * decay)
        lows.append(jnp.where(strict, beta * mm3(key, key, ((1,), (1,))) * decay, 0.0))
    invs = [eye - jnp.where(bits == 1, low, 0.0) for low in lows]
    step = 1
    while (2 << step) <= proj_ref.shape[0]:
        keep = (bits >> step) == 1
        parts = [mm3(jnp.where(keep, low, 0.0), inv) for low, inv in zip(lows, invs)]
        invs = [inv - mm3(inv, part) for inv, part in zip(invs, parts)]
        step += 1
    news = [mm3(inv, value) for inv, value in zip(invs, values)]
    mixes = [mm3(attend, new) for attend, new in zip(attends, news)]
    for head in range(LH):
        mix = mixes[head]
        scale = lax.rsqrt(jnp.mean(mix * mix, axis=-1, keepdims=True) + EPS)
        gate = proj_ref[:, head_slices(head)[3]]
        out = mix * scale * gain_ref[0:1] * (gate * sigmoid(gate))
        mixed_ref[:, head * DV : (head + 1) * DV] = out.astype(BF16)
        inv_ref[head] = invs[head]
        new_ref[:, head * DV : (head + 1) * DV] = news[head]


def mixer_back(
    proj_ref, pos_ref, conv_ref, prm_ref, gain_ref, inv_ref, new_ref, gmix_ref, gproj_ref, gconv_ref, misc_ref
):
    width = proj_ref.shape[1]
    rows = proj_ref.shape[0]
    tail_ref = proj_ref.at[:, width - TAIL :]
    pos, row_i, row_j, lower, lower_f, raw, shifted, log_decay, beta_all, cum, cum_t = group_terms(
        tail_ref, prm_ref, pos_ref
    )
    strict = lower & (row_j < row_i)
    lane = lax.broadcasted_iota(jnp.int32, (rows, TAIL), 1)
    ones = jnp.ones((rows, TAIL), F32)
    grad_cum = jnp.zeros((rows, TAIL), F32)
    grad_beta_all = jnp.zeros((rows, TAIL), F32)
    gain_sum = jnp.zeros((1, DV), F32)
    for head in range(LH):
        sq, sk, sv, sg = head_slices(head)
        q_raw, k_raw, v_raw = proj_ref[:, sq], proj_ref[:, sk], proj_ref[:, sv]
        q_pre = conv_rows(q_raw, conv_ref[:, sq], pos)
        k_pre = conv_rows(k_raw, conv_ref[:, sk], pos)
        v_pre = conv_rows(v_raw, conv_ref[:, sv], pos)
        q_sig, k_sig, v_sig = sigmoid(q_pre), sigmoid(k_pre), sigmoid(v_pre)
        q_act, k_act, value = q_pre * q_sig, k_pre * k_sig, v_pre * v_sig
        query, q_inv = unit(q_act, DK**-0.5)
        key, k_inv = unit(k_act, 1.0)
        query_b, key_b = query, key
        beta = beta_all[:, LH + head : LH + head + 1]
        gap = cum[:, head : head + 1] - cum_t[head : head + 1, :]
        decay = jnp.where(lower, jnp.exp(gap), 0.0)
        pair = mm3(key_b, key_b, ((1,), (1,)))
        query_pair = mm3(query_b, key_b, ((1,), (1,)))
        attend = query_pair * decay
        inv = inv_ref[head]
        new = new_ref[:, head * DV : (head + 1) * DV]
        mix = mm3(attend, new)
        scale = lax.rsqrt(jnp.mean(mix * mix, axis=-1, keepdims=True) + EPS)
        gate = proj_ref[:, sg]
        gate_sig = sigmoid(gate)
        grad_out = gmix_ref[:, head * DV : (head + 1) * DV]
        unscaled = mix * scale
        grad_norm = grad_out * (gate * gate_sig)
        grad_gate = silu_back(grad_out * unscaled * gain_ref[0:1], gate, gate_sig)
        gain_sum = gain_sum + jnp.sum(grad_norm * unscaled, axis=0, keepdims=True)
        weighted = grad_norm * gain_ref[0:1]
        grad_mix = scale * weighted - mix * (
            scale * scale * scale * jnp.mean(mix * weighted, axis=-1, keepdims=True)
        )
        grad_mix_b = grad_mix
        grad_new = mm3(attend, grad_mix_b, ((0,), (0,)))
        grad_attend = mm3(grad_mix_b, new, ((1,), (1,)))
        grad_rhs = mm3(inv, grad_new, ((0,), (0,)))
        grad_low = -mm3(grad_rhs, new, ((1,), (1,)))
        grad_value = beta * grad_rhs
        low_decay = jnp.where(strict, grad_low * decay, 0.0)
        low_pair = low_decay * pair
        grad_beta = jnp.sum(grad_rhs * value, axis=-1, keepdims=True) + jnp.sum(
            low_pair, axis=-1, keepdims=True
        )
        grad_pair = beta * low_decay
        grad_query_pair = grad_attend * decay
        both = beta * low_pair + grad_query_pair * query_pair
        column = jnp.sum(both, axis=-1, keepdims=True) - mmx(both, ones, ((0,), (0,)))
        grad_cum = jnp.where(lane == head, column, grad_cum)
        grad_beta_all = jnp.where(lane == LH + head, grad_beta, grad_beta_all)
        grad_pair_b = grad_pair
        grad_qp_b = grad_query_pair
        grad_query = mm3(grad_qp_b, key_b)
        grad_key = (
            mm3(grad_qp_b, query_b, ((0,), (0,))) + mm3(grad_pair_b, key_b) + mm3(grad_pair_b, key_b, ((0,), (0,)))
        )
        grad_q = silu_back(unit_back(grad_query, q_act, q_inv, DK**-0.5), q_pre, q_sig)
        grad_k = silu_back(unit_back(grad_key, k_act, k_inv, 1.0), k_pre, k_sig)
        grad_v = silu_back(grad_value, v_pre, v_sig)
        for grad, part, where in ((grad_q, q_raw, sq), (grad_k, k_raw, sk), (grad_v, v_raw, sv)):
            moved, sums = conv_back(grad, part, conv_ref[:, where], pos)
            gproj_ref[:, where] = moved.astype(BF16)
            for tap in range(CONV):
                gconv_ref[tap : tap + 1, where] += sums[tap]
        gproj_ref[:, sg] = grad_gate.astype(BF16)
    grad_log = mmx(lower_f, grad_cum, ((0,), (0,)))
    grad_step = grad_log * prm_ref[0:1] * sigmoid(shifted)
    grad_tail = grad_step + grad_beta_all * beta_all * (1.0 - beta_all)
    gproj_ref[:, width - TAIL :] = grad_tail.astype(BF16)
    misc_ref[0:1, :] += gain_sum
    misc_ref[1:2, 0:TAIL] += jnp.sum(grad_log * log_decay, axis=0, keepdims=True)
    misc_ref[2:3, 0:TAIL] += jnp.sum(grad_step, axis=0, keepdims=True)


VMEM_LIMIT = 60 * 1024 * 1024


MESH = pl.DeviceIdType.MESH


class Place:
    def __init__(self, nf):
        self.nf, self.nz = nf, nf // 2
        self.d = lax.axis_index("dp")
        self.f = lax.axis_index("fsdp")
        self.z, self.y = self.f // 2, self.f % 2
        self.over = self.z < self.nz - 1
        self.under = self.z > 0

    def flip(self, value, mask):
        return value + mask * (1 - 2 * ((value // mask) % 2))

    def dp(self, mask):
        if mask == 3:
            return (self.flip(self.flip(self.d, 1), 2), self.f)
        return (self.flip(self.d, mask), self.f)

    def at_z(self, z):
        return (self.d, z * 2 + self.y)

    def beside(self):
        return (self.d, self.flip(self.f, 1))

    def greet(self):
        barrier = pltpu.get_barrier_semaphore()
        for mask in (1, 2, 3):
            pl.semaphore_signal(barrier, inc=1, device_id=self.dp(mask), device_id_type=MESH)
        pl.semaphore_signal(barrier, inc=1, device_id=self.beside(), device_id_type=MESH)

        @pl.when(self.over)
        def _():
            pl.semaphore_signal(barrier, inc=1, device_id=self.at_z(self.z + 1), device_id_type=MESH)

        @pl.when(self.under)
        def _():
            pl.semaphore_signal(barrier, inc=1, device_id=self.at_z(self.z - 1), device_id_type=MESH)

        pl.semaphore_wait(barrier, 4 + self.over.astype(jnp.int32) + self.under.astype(jnp.int32))


def send(src, dst, send_sem, recv_sem, device):
    return pltpu.make_async_remote_copy(
        src_ref=src, dst_ref=dst, send_sem=send_sem, recv_sem=recv_sem, device_id=device, device_id_type=MESH
    )


def pieces(columns, count):
    tiles = columns // 128
    edges = [128 * (tiles * c // count) for c in range(count + 1)]
    return [(edge, after - edge) for edge, after in zip(edges, edges[1:])]


def nothing():
    return None


class Gather:
    def __init__(self, place, ahead, lag, views, ready, up_send, down_send, z_recv, y_send, y_recv, pair_send, pair_recv):
        self.p, self.ahead, self.views, self.ready = place, ahead, views, ready
        self.up_send, self.down_send, self.z_recv = up_send, down_send, z_recv
        self.y_send, self.y_recv, self.pair_send, self.pair_recv = y_send, y_recv, pair_send, pair_recv
        self.lag = lag
        self.ticks = len(views) + lag * (place.nz - 1)

    @staticmethod
    def scratch(units, nz):
        return [
            pltpu.SemaphoreType.DMA((units, nz)),
            pltpu.SemaphoreType.DMA((units, nz)),
            pltpu.SemaphoreType.DMA((units, nz)),
            pltpu.SemaphoreType.DMA((units, nz)),
            pltpu.SemaphoreType.DMA((units, nz)),
            pltpu.SemaphoreType.DMA((units,)),
            pltpu.SemaphoreType.DMA((units,)),
        ]

    def block(self, u, z, y):
        return self.views[u](z * 2 + y)

    def up(self, u, r):
        ref = self.block(u, self.p.z - (r - 1), self.p.y)
        return send(ref, ref, self.up_send.at[u, r], self.z_recv.at[u, r], self.p.at_z(self.p.z + 1))

    def down(self, u, r):
        ref = self.block(u, self.p.z + (r - 1), self.p.y)
        nz = self.p.nz
        return send(ref, ref, self.down_send.at[u, r], self.z_recv.at[u, nz - r], self.p.at_z(self.p.z - 1))

    def over_y(self, u, r):
        ref = self.block(u, lax.rem(self.p.z - r + self.p.nz, self.p.nz), self.p.y)
        return send(ref, ref, self.y_send.at[u, r], self.y_recv.at[u, r], self.p.beside())

    def pair(self, u):
        ref = self.block(u, self.p.z, 1 - self.p.y)
        return send(ref, ref, self.pair_send.at[u], self.pair_recv.at[u], self.p.at_z(self.p.flip(self.p.z, 1)))

    def wait_z(self, u, r):
        ref = self.block(u, lax.rem(self.p.z - r + self.p.nz, self.p.nz), self.p.y)
        send(ref, ref, self.up_send.at[u, 1], self.z_recv.at[u, r], self.p.beside()).wait_recv()

    def wait_y(self, u, r):
        ref = self.block(u, lax.rem(self.p.z - r + self.p.nz, self.p.nz), 1 - self.p.y)
        send(ref, ref, self.y_send.at[u, r], self.y_recv.at[u, r], self.p.beside()).wait_recv()

    def wait_pair(self, u):
        other = self.p.flip(self.p.z, 1)
        ref = self.block(u, other, 1 - self.p.y)
        send(ref, ref, self.pair_send.at[u], self.pair_recv.at[u], self.p.at_z(other)).wait_recv()

    def odd(self, u):
        return u % 2 == 1

    def skips(self, u, r):
        if not self.odd(u) or r not in (1, self.p.nz - 1):
            return None
        odd = self.p.z % 2 == 1
        if self.p.nz == 2:
            return odd | ~odd
        return odd if r == 1 else ~odd

    def unless_skipped(self, u, r, action):
        skip = self.skips(u, r)
        if skip is None:
            action()
        else:
            pl.when(~skip)(action)

    def own(self, t):
        p = self.p
        self.ready[t]()

        @pl.when(p.over)
        def _():
            self.up(t, 1).start()

        @pl.when(p.under)
        def _():
            self.down(t, 1).start()

        self.over_y(t, 0).start()

    def tick(self, t):
        p, nz = self.p, self.p.nz
        for u in range(self.ahead + 1) if t == 0 else (t + self.ahead,):
            if u < len(self.views):
                self.own(u)
        for s in range(1, nz):
            u = t - s * self.lag
            if not 0 <= u < len(self.views):
                continue

            @pl.when(p.z >= s)
            def _():
                self.wait_z(u, s)

                @pl.when(p.over)
                def _():
                    self.up(u, s + 1).start()

                self.unless_skipped(u, s, self.over_y(u, s).start)

            @pl.when(p.z <= nz - 1 - s)
            def _():
                self.wait_z(u, nz - s)

                @pl.when(p.under)
                def _():
                    self.down(u, s + 1).start()

                self.unless_skipped(u, nz - s, self.over_y(u, nz - s).start)

            if s == nz - 1 and self.odd(u):
                self.wait_y(u, 0)
                self.pair(u).start()

    def finish(self):
        p, nz = self.p, self.p.nz
        for u in range(len(self.views)):
            if not self.odd(u):
                self.wait_y(u, 0)
            else:
                self.wait_pair(u)
                self.pair(u).wait_send()
            self.over_y(u, 0).wait_send()
            for r in range(1, nz):

                def both():
                    self.wait_y(u, r)
                    self.over_y(u, r).wait_send()

                self.unless_skipped(u, r, both)
            for r in range(1, nz):

                @pl.when(p.over & (p.z >= r - 1))
                def _():
                    self.up(u, r).wait_send()

                @pl.when(p.under & (p.z <= nz - r))
                def _():
                    self.down(u, r).wait_send()


def gather_kernel(nf, splits, packs, shards, groups, *refs):
    count = len(packs) + len(shards) + groups
    ins, outs = refs[:count], refs[count : 2 * count]
    to_send, to_recv, near_send, near_recv, local_sem = refs[2 * count : 2 * count + 5]
    p = Place(nf)
    pack_in, shard_in, group_in = ins[: len(packs)], ins[len(packs) : len(packs) + len(shards)], ins[count - groups :]
    pack_out, shard_out, group_out = (
        outs[: len(packs)],
        outs[len(packs) : len(packs) + len(shards)],
        outs[count - groups :],
    )

    def own_pack(i, d):
        return pack_out[i].at[d, p.f] if packs[i] else pack_out[i].at[d]

    def exchange(i, m):
        target = p.dp(m)
        return send(pack_in[i].at[target[0]], own_pack(i, p.d), to_send.at[i, m], to_recv.at[i, m], target)

    def wait_exchange(i, m):
        source = p.dp(m)
        ref = own_pack(i, source[0])
        send(ref, ref, to_send.at[i, m], to_recv.at[i, m], source).wait_recv()

    def near(j, k):
        src, dst, mask = ((group_in[j], 2, 2), (group_in[j], 1, 1), (group_out[j].at[2], 3, 1))[k]
        return send(src, group_out[j].at[dst], near_send.at[j, k], near_recv.at[j, k], p.dp(mask))

    def wait_near(j, k):
        ref = group_out[j].at[(2, 1, 3)[k]]
        send(ref, ref, near_send.at[j, k], near_recv.at[j, k], p.dp(1)).wait_recv()

    def local(n):
        if n < len(packs):
            return pltpu.make_async_copy(pack_in[n].at[p.d], own_pack(n, p.d), local_sem.at[n])
        if n < len(packs) + len(shards):
            i = n - len(packs)
            return pltpu.make_async_copy(shard_in[i], shard_out[i].at[p.f], local_sem.at[n])
        j = n - len(packs) - len(shards)
        return pltpu.make_async_copy(group_in[j], group_out[j].at[0], local_sem.at[n])

    p.greet()
    views, ready = [], []
    for i, whole in enumerate(packs):
        for m in range(TP if whole else 0):
            source = p.dp(m)[0] if m else p.d
            for c, (start, size) in enumerate(pieces(pack_in[i].shape[-1], splits[0])):
                views.append(lambda f, i=i, d=source, at=pl.ds(start, size): pack_out[i].at[d, f, :, at])
                ready.append(nothing if c else partial(wait_exchange, i, m) if m else local(i).wait)
    for i in range(len(shards)):
        for c, (start, size) in enumerate(pieces(shard_in[i].shape[-1], splits[1])):
            views.append(lambda f, i=i, at=pl.ds(start, size): shard_out[i].at[f, :, at])
            ready.append(nothing if c else local(len(packs) + i).wait)
    gather = Gather(p, 3, 1, views, ready, *refs[2 * count + 5 :])
    for n in range(count):
        local(n).start()
    for m in (1, 2, 3):
        exchange(0, m).start()
    for j in range(groups):
        near(j, 0).start()
        near(j, 1).start()
    for i in range(1, len(packs)):
        for m in (2, 3, 1):
            exchange(i, m).start()
    for t in range(gather.ticks):
        gather.tick(t)
        if t == 2:
            for j in range(groups):
                wait_near(j, 0)
                near(j, 2).start()
    gather.finish()
    for i, whole in enumerate(packs):
        for m in (1, 2, 3):
            exchange(i, m).wait_send()
            if not whole:
                wait_exchange(i, m)
        if not whole:
            local(i).wait()
    for j in range(groups):
        wait_near(j, 1)
        wait_near(j, 2)
        for k in range(3):
            near(j, k).wait_send()
        local(len(packs) + len(shards) + j).wait()


def gather_all(nf, collective_id, splits, packs, shards, groups):
    marks = tuple(whole for _, whole in packs)
    ins = [array for array, _ in packs] + list(shards) + list(groups)
    outs = (
        [
            jax.ShapeDtypeStruct(array.shape[:1] + ((nf,) if whole else ()) + array.shape[1:], array.dtype)
            for array, whole in packs
        ]
        + [jax.ShapeDtypeStruct((nf,) + array.shape, array.dtype) for array in shards]
        + [jax.ShapeDtypeStruct((TP,) + array.shape, array.dtype) for array in groups]
    )
    units = TP * sum(marks) * splits[0] + len(shards) * splits[1]
    sent = sum(out.size * 2 for out in outs)
    any_space = pl.BlockSpec(memory_space=pl.ANY)
    return pl.pallas_call(
        partial(gather_kernel, nf, splits, marks, (True,) * len(shards), len(groups)),
        in_specs=[any_space] * len(ins),
        out_specs=[any_space] * len(outs),
        out_shape=outs,
        scratch_shapes=[
            pltpu.SemaphoreType.DMA((len(packs), TP)),
            pltpu.SemaphoreType.DMA((len(packs), TP)),
            pltpu.SemaphoreType.DMA((max(len(groups), 1), 3)),
            pltpu.SemaphoreType.DMA((max(len(groups), 1), 3)),
            pltpu.SemaphoreType.DMA((len(ins),)),
        ]
        + Gather.scratch(units, nf // 2),
        compiler_params=pltpu.CompilerParams(
            collective_id=collective_id, has_side_effects=True, vmem_limit_bytes=1024 * 1024
        ),
        cost_estimate=pl.CostEstimate(flops=0, bytes_accessed=2 * sent, transcendentals=0),
        name="gather_" + str(collective_id),
    )(*ins)


def add_into(dst, srcs):
    rows = dst.shape[-2]
    size = 16 if rows % 16 == 0 else rows
    lead = dst.shape[0] if len(dst.shape) == 3 else 1

    def body(i, _):
        at = pl.ds(pl.multiple_of((i % (rows // size)) * size, size), size)
        where = (i // (rows // size), at) if len(dst.shape) == 3 else (at,)
        total = srcs[0][where].astype(F32)
        for src in srcs[1:]:
            total = total + src[where].astype(F32)
        dst[where] = total.astype(dst.dtype)
        return 0

    lax.fori_loop(0, lead * (rows // size), body, 0)


PER = 2


def forward_kernel(nf, split, *refs):
    (x_hbm, w_hbm, out_hbm, pos_ref, conv_ref, prm_ref, gain_ref, gain_two_ref, tokens_ref), refs = refs[:9], refs[9:]
    pack_in, shard_in, refs = refs[:2], refs[2], refs[3:]
    (proj_hbm, mixed_hbm, inv_hbm, new_hbm, residual_ref, group_hbm), refs = refs[:6], refs[6:]
    pack_out, shard_out, refs = refs[:2], refs[2], refs[3:]
    (proj_ref, mixed_ref, inv_ref, new_ref, parts_ref, near_ref, stage_sem), refs = refs[:7], refs[7:]
    (part_send, part_recv, group_send, group_recv, local_sem), refs = refs[:5], refs[5:]
    (x_ref, w_ref, out_ref, normed_ref, load_sem), refs = refs[:5], refs[5:]
    p = Place(nf)
    quarter = w_hbm.shape[0] // 4
    loads = [pltpu.make_async_copy(x_hbm, x_ref, load_sem.at[0])]
    for k in range(4):
        at = pl.ds(k * quarter, quarter)
        loads.append(pltpu.make_async_copy(w_hbm.at[at], w_ref.at[at], load_sem.at[1 + k]))
    loads.append(pltpu.make_async_copy(out_hbm, out_ref, load_sem.at[5]))
    rows = tokens_ref.shape[0]
    width = tokens_ref.shape[1]

    local = [pltpu.make_async_copy(pack_in[i], pack_out[i].at[:, p.f], local_sem.at[i]) for i in range(2)]
    local.append(pltpu.make_async_copy(shard_in, shard_out.at[p.f], local_sem.at[2]))

    views, ready = [], []
    for i in range(2):
        for d in range(TP):
            views.append(lambda f, i=i, d=d: pack_out[i].at[d, f])
            ready.append(nothing if d else local[i].wait)
    for c, (start, size) in enumerate(pieces(width, split)):
        views.append(lambda f, at=pl.ds(start, size): shard_out.at[f, :, at])
        ready.append(nothing if c else local[2].wait)
    p.greet()
    for copy in local:
        copy.start()
    gather = Gather(p, 3, 1, views, ready, *refs)

    def part_copy(k):
        src, mask = ((parts_ref.at[1], 1), (parts_ref.at[3], 1), (near_ref.at[1], 2))[k]
        return send(src, near_ref.at[k], part_send.at[k], part_recv.at[k], p.dp(mask))

    def group_copy(k):
        src, dst, mask = ((normed_ref, 2, 2), (normed_ref, 1, 1), (group_hbm.at[2], 3, 1))[k]
        return send(src, group_hbm.at[dst], group_send.at[k], group_recv.at[k], p.dp(mask))

    own_normed = pltpu.make_async_copy(normed_ref, group_hbm.at[0], load_sem.at[6])

    def stage_copies(g):
        at = pl.ds(pl.multiple_of(g * rows, rows), rows)
        return (
            pltpu.make_async_copy(proj_ref, proj_hbm.at[at], stage_sem.at[0]),
            pltpu.make_async_copy(mixed_ref, mixed_hbm.at[at], stage_sem.at[1]),
            pltpu.make_async_copy(inv_ref, inv_hbm.at[pl.ds(pl.multiple_of(g * LH, LH), LH)], stage_sem.at[2]),
            pltpu.make_async_copy(new_ref, new_hbm.at[at], stage_sem.at[3]),
        )

    columns = w_ref.shape[1]
    tile = 640
    gather.tick(0)
    for load in loads:
        load.start()
    for load in loads:
        load.wait()

    def group(i, _):
        half = i // 2
        g = 2 * i + 1 - half * (3 + 4 * (i - 2 * half))

        @pl.when(i > 0)
        def _():
            for copy in stage_copies(0):
                copy.wait()

        at = pl.ds(pl.multiple_of(g * rows, rows), rows)

        def project(c, _):
            where = pl.ds(pl.multiple_of(c * tile, tile), tile)
            proj_ref[:, where] = mm(x_ref[at, :], w_ref[:, where])
            return 0

        lax.fori_loop(0, columns // tile, project, 0)
        for step in range(TP):

            @pl.when(i == step)
            def _():
                for t in range(PER // 2):
                    gather.tick(1 + PER * step + t)

        mixer_forward(proj_ref, pos_ref.at[at], conv_ref, prm_ref, gain_ref, mixed_ref, inv_ref, new_ref)
        for copy in stage_copies(g):
            copy.start()

        def project_out(c, _):
            where = pl.ds(pl.multiple_of(c * 512, 512), 512)
            parts_ref[g, :, where] = mm(mixed_ref[...], out_ref[:, where]).astype(BF16)
            return 0

        lax.fori_loop(0, width // 512, project_out, 0)
        for step in range(TP):

            @pl.when(i == step)
            def _():
                if step < 2:
                    part_copy(step).start()
                if step == 2:
                    part_copy(1).wait_recv()
                    add_into(parts_ref.at[2], [parts_ref.at[2], near_ref.at[1]])
                    send(parts_ref.at[2], near_ref.at[2], part_send.at[2], part_recv.at[2], p.dp(2)).start()
                for t in range(PER // 2, PER):
                    gather.tick(1 + PER * step + t)

        return 0

    lax.fori_loop(0, TP, group, 0)
    part_copy(0).wait_recv()
    far = send(parts_ref.at[2], near_ref.at[2], part_send.at[2], part_recv.at[2], p.dp(2))
    far.wait_recv()

    def norm(c, _):
        where = pl.ds(pl.multiple_of(c * 64, 64), 64)
        total = tokens_ref[where, :].astype(F32) + parts_ref[0, where, :].astype(F32)
        total = total + near_ref[0, where, :].astype(F32) + near_ref[2, where, :].astype(F32)
        residual_ref[where, :] = total
        scale = lax.rsqrt(jnp.mean(total * total, axis=-1, keepdims=True) + EPS)
        normed_ref[where, :] = (total * scale * gain_two_ref[0:1]).astype(BF16)
        return 0

    lax.fori_loop(0, rows // 64, norm, 0)
    group_copy(0).start()
    group_copy(1).start()
    own_normed.start()
    for t in range(1 + PER * TP, gather.ticks):
        gather.tick(t)
        if t == min(2 + PER * TP, gather.ticks - 1):
            group_copy(0).wait_recv()
            group_copy(2).start()
    gather.finish()
    for copy in stage_copies(0):
        copy.wait()
    part_copy(0).wait_send()
    part_copy(1).wait_send()
    far.wait_send()
    own_normed.wait()
    for k in (1, 2):
        group_copy(k).wait_recv()
    for k in range(3):
        group_copy(k).wait_send()


def forward(nf, x, w, out, pos, conv, prm, gain, gain_two, tokens, packs, shard):
    total, columns = x.shape[0], w.shape[1]
    rows, width = tokens.shape
    split = 4 if nf <= 8 else 1
    vmem, any_space = pl.BlockSpec(memory_space=pltpu.VMEM), pl.BlockSpec(memory_space=pl.ANY)
    outs = [
        jax.ShapeDtypeStruct((total, columns), F32),
        jax.ShapeDtypeStruct((total, LH * DV), BF16),
        jax.ShapeDtypeStruct((TP * LH, rows, rows), F32),
        jax.ShapeDtypeStruct((total, LH * DV), F32),
        jax.ShapeDtypeStruct((rows, width), F32),
        jax.ShapeDtypeStruct((TP, rows, width), BF16),
    ]
    outs += [jax.ShapeDtypeStruct((TP, nf) + pack.shape[1:], BF16) for pack in packs]
    outs += [jax.ShapeDtypeStruct((nf,) + shard.shape, BF16)]
    return pl.pallas_call(
        partial(forward_kernel, nf, split),
        in_specs=[any_space] * 3 + [vmem] * 6 + [any_space] * 3,
        out_specs=[any_space] * 4 + [vmem] + [any_space] * 4,
        out_shape=outs,
        scratch_shapes=[
            pltpu.VMEM((rows, columns), F32),
            pltpu.VMEM((rows, LH * DV), BF16),
            pltpu.VMEM((LH, rows, rows), F32),
            pltpu.VMEM((rows, LH * DV), F32),
            pltpu.VMEM((TP, rows, width), BF16),
            pltpu.VMEM((3, rows, width), BF16),
            pltpu.SemaphoreType.DMA((4,)),
            pltpu.SemaphoreType.DMA((3,)),
            pltpu.SemaphoreType.DMA((3,)),
            pltpu.SemaphoreType.DMA((3,)),
            pltpu.SemaphoreType.DMA((3,)),
            pltpu.SemaphoreType.DMA((3,)),
            pltpu.VMEM(x.shape, BF16),
            pltpu.VMEM(w.shape, BF16),
            pltpu.VMEM(out.shape, BF16),
            pltpu.VMEM((rows, width), BF16),
            pltpu.SemaphoreType.DMA((7,)),
        ]
        + Gather.scratch(2 * TP + split, nf // 2),
        compiler_params=pltpu.CompilerParams(
            collective_id=4, has_side_effects=True, vmem_limit_bytes=VMEM_LIMIT
        ),
        cost_estimate=pl.CostEstimate(flops=45_000_000_000, bytes_accessed=80_000_000, transcendentals=5_000_000),
        name="forward",
    )(x, w, out, pos, conv, prm, gain, gain_two, tokens, *packs, shard)


AHEAD, OLD_FIRST = 2, True


class Reduce:
    def __init__(self, place, part, done, own, y_in, z_in, pair_in, sems):
        self.p, self.part, self.done = place, part, done
        self.own, self.y_in, self.z_in, self.pair_in = own, y_in, z_in, pair_in
        self.y_send, self.y_recv, self.z_send, self.z_recv, self.pair_send, self.pair_recv, self.load_sem = sems
        self.count = len(y_in)
        self.ticks = self.count + place.nz

    @staticmethod
    def scratch(blocks, nz):
        units = len(blocks)
        return (
            [pltpu.VMEM((nz + u % 2,) + block, BF16) for u, block in enumerate(blocks)]
            + [pltpu.VMEM((nz,) + block, BF16) for block in blocks]
            + [pltpu.VMEM((nz + 1,) + block, BF16) for block in blocks]
            + [pltpu.VMEM(block if u % 2 else (8, 128), BF16) for u, block in enumerate(blocks)]
            + [pltpu.SemaphoreType.DMA((units, nz))] * 3
            + [pltpu.SemaphoreType.DMA((units, nz + 1))]
            + [pltpu.SemaphoreType.DMA((units,))] * 2
            + [pltpu.SemaphoreType.DMA((units, nz + 1))]
        )

    def odd(self, u):
        return u % 2 == 1

    def copy_y(self, u, z0):
        src = self.part(u, z0 * 2 + 1 - self.p.y)
        return send(src, self.y_in[u].at[z0], self.y_send.at[u, z0], self.y_recv.at[u, z0], self.p.beside())

    def copy_late(self, u):
        z = self.p.z
        return send(self.pair_in[u], self.y_in[u].at[z], self.y_send.at[u, z], self.y_recv.at[u, z], self.p.beside())

    def copy_pair(self, u):
        other = self.p.flip(self.p.z, 1)
        src = self.part(u, other * 2 + 1 - self.p.y)
        return send(src, self.pair_in[u], self.pair_send.at[u], self.pair_recv.at[u], self.p.at_z(other))

    def copy_z(self, u, z0, slot, z):
        return send(self.y_in[u].at[z0], self.z_in[u].at[slot], self.z_send.at[u, z0], self.z_recv.at[u, slot], self.p.at_z(z))

    def wait_z(self, u, slot):
        ref = self.z_in[u].at[slot]
        send(ref, ref, self.z_send.at[u, 0], self.z_recv.at[u, slot], self.p.beside()).wait_recv()

    def pass_on(self, u, z0, arrived, slot, z):
        own = self.own[u].at[z0]
        here = self.y_in[u].at[z0]
        if self.odd(u):
            other = self.p.flip(self.p.z, 1)

            @pl.when(other != z0)
            def _():
                add_into(here, [own, here] + arrived)

            @pl.when(other == z0)
            def _():
                add_into(here, [own] + arrived)
        else:
            add_into(here, [own, here] + arrived)
        self.copy_z(u, z0, slot, z).start()

    def loads(self, u):
        p, nz = self.p, self.p.nz
        copies = [
            pltpu.make_async_copy(self.part(u, z0 * 2 + p.y), self.own[u].at[z0], self.load_sem.at[u, z0])
            for z0 in range(nz)
        ]
        if self.odd(u):
            src = self.part(u, p.z * 2 + 1 - p.y)
            copies.append(pltpu.make_async_copy(src, self.own[u].at[nz], self.load_sem.at[u, nz]))
        return copies

    def begin(self, u):
        p, nz = self.p, self.p.nz
        if self.odd(u):
            self.copy_pair(u).start()
            other = p.flip(p.z, 1)
            for z0 in range(nz):

                @pl.when((z0 != p.z) & (z0 != other))
                def _():
                    self.copy_y(u, z0).start()
        else:
            for z0 in range(nz):
                self.copy_y(u, z0).start()
        for load in self.loads(u):
            load.start()

    def set_out(self, u):
        p, nz = self.p, self.p.nz
        for load in self.loads(u):
            load.wait()
        if self.odd(u):
            self.copy_pair(u).wait_recv()
            add_into(self.pair_in[u], [self.pair_in[u], self.own[u].at[nz]])
            self.copy_late(u).start()
        other = p.flip(p.z, 1)
        for z0 in range(nz):
            needed = (z0 != p.z) & (z0 != other) if self.odd(u) else z0 != p.z

            @pl.when(needed)
            def _():
                self.copy_y(u, z0).wait_recv()

        @pl.when(p.z == nz - 1)
        def _():
            for z0 in range(nz - 1):
                self.pass_on(u, z0, [], z0, p.z - 1)

        @pl.when(p.z == 0)
        def _():
            for z0 in range(nz - 1, 0, -1):
                self.pass_on(u, z0, [], nz if z0 == 1 else z0, p.z + 1)

    def relay(self, u, hop):
        p, nz = self.p, self.p.nz

        @pl.when(p.z == nz - 1 - hop)
        def _():
            for z0 in range(nz - hop):
                self.wait_z(u, z0)
                if z0 < nz - 1 - hop:
                    self.pass_on(u, z0, [self.z_in[u].at[z0]], z0, p.z - 1)

        @pl.when(p.z == hop)
        def _():
            for z0 in range(nz - 1, hop - 1, -1):
                slot = nz if z0 == hop else z0
                self.wait_z(u, slot)
                if z0 > hop:
                    self.pass_on(u, z0, [self.z_in[u].at[z0]], nz if z0 == hop + 1 else z0, p.z + 1)

    def settle(self, u):
        p, nz = self.p, self.p.nz
        self.copy_y(u, p.z).wait_recv()
        own = [self.own[u].at[p.z], self.y_in[u].at[p.z]]
        above, below = self.z_in[u].at[p.z], self.z_in[u].at[nz]

        @pl.when(p.z == 0)
        def _():
            self.done(u, own + [above])

        @pl.when(p.z == nz - 1)
        def _():
            self.done(u, own + [below])

        @pl.when(p.over & p.under)
        def _():
            self.done(u, own + [above, below])

    def tick(self, t):
        for u in range(1 + AHEAD) if t == 0 else (t + AHEAD,):
            if u < self.count:
                self.begin(u)
        stages = [(t - 1 - hop, hop) for hop in range(self.p.nz - 1, -1, -1)]
        if not OLD_FIRST:
            stages = stages[::-1]
        for u, hop in stages:
            if 0 <= u < self.count:
                if hop:
                    self.relay(u, hop)
                else:
                    self.set_out(u)
        if 0 <= t - self.p.nz < self.count:
            self.settle(t - self.p.nz)

    def finish(self):
        p, nz = self.p, self.p.nz
        other = p.flip(p.z, 1)
        for u in range(self.count):
            if self.odd(u):
                self.copy_pair(u).wait_send()
                self.copy_late(u).wait_send()
            for z0 in range(nz):
                needed = (z0 != p.z) & (z0 != other) if self.odd(u) else None
                if needed is None:
                    self.copy_y(u, z0).wait_send()
                else:

                    @pl.when(needed)
                    def _():
                        self.copy_y(u, z0).wait_send()

                @pl.when(z0 != p.z)
                def _():
                    self.copy_z(u, z0, z0, p.z).wait_send()


class Owners:
    def __init__(self, place, kinds, units, ins, outs, final, to_send, to_recv, to_local):
        self.p, self.kinds, self.units, self.ins, self.outs = place, kinds, units, ins, outs
        self.packs = [u for u, (i, _, _) in enumerate(units) if kinds[i]]
        self.final = dict(zip(self.packs, final))
        self.to_send, self.to_recv, self.to_local = to_send, to_recv, to_local

    @staticmethod
    def scratch(kinds, units, blocks):
        final = [pltpu.VMEM(block, BF16) for block, unit in zip(blocks, units) if kinds[unit[0]]]
        return final, [
            pltpu.SemaphoreType.DMA((len(units), TP)),
            pltpu.SemaphoreType.DMA((len(units), TP)),
            pltpu.SemaphoreType.DMA((len(units),)),
        ]

    def part(self, u, f):
        i, start, size = self.units[u]
        columns = pl.ds(start, size)
        return self.ins[i].at[:, f, :, columns] if self.kinds[i] else self.ins[i].at[f, :, columns]

    def place(self, u, d):
        i, start, size = self.units[u]
        return self.outs[i].at[d, :, pl.ds(start, size)]

    def copy(self, u, m):
        target = self.p.dp(m)
        src = self.final[u].at[target[0]]
        return send(src, self.place(u, self.p.d), self.to_send.at[u, m], self.to_recv.at[u, m], target)

    def local(self, u):
        return pltpu.make_async_copy(self.final[u].at[self.p.d], self.place(u, self.p.d), self.to_local.at[u])

    def done(self, u, sources):
        i, start, size = self.units[u]
        add_into(self.final[u] if self.kinds[i] else self.outs[i].at[:, pl.ds(start, size)], sources)

    def send_off(self, u):
        if u in self.final:
            for m in (2, 3, 1):
                self.copy(u, m).start()
            self.local(u).start()

    def finish(self):
        for u in self.packs:
            self.local(u).wait()
            for m in (1, 2, 3):
                self.copy(u, m).wait_send()
                source = self.p.dp(m)
                ref = self.place(u, source[0])
                send(ref, ref, self.to_send.at[u, m], self.to_recv.at[u, m], source).wait_recv()


def take(refs, *counts):
    parts = []
    for count in counts:
        parts.append(refs[:count])
        refs = refs[count:]
    return parts + [refs]


def reduce_kernel(nf, kinds, units, groups, chain, vecs, *refs):
    arrays, n = len(kinds), len(units)
    ins, group, more, vec, outs, group_outs, vec_out, refs = take(
        refs, arrays, groups, 3 if chain else 0, vecs, arrays, 3 if chain else groups, vecs
    )
    p = Place(nf)
    nz = p.nz
    own, y_in, z_in, pair_in, sems, refs = take(refs, n, n, n, n, 7)
    final, to_sems, (near, kept, near_send, near_recv, keep_sem), refs = take(
        refs, sum(kinds[i] for i, _, _ in units), 3, 5
    )
    owners = Owners(p, kinds, units, ins, outs, final, *to_sems)
    red = Reduce(p, owners.part, owners.done, own, y_in, z_in, pair_in, sems)
    if chain:
        (residual_ref, cotangent_ref, gain_ref), (sum_ref, all_ref, gain_sum_ref) = more, group_outs
        normed_ref, spread_send, spread_recv, spread_local = refs
        own_spread = pltpu.make_async_copy(normed_ref, all_ref.at[0], spread_local)
    if vecs:
        vec_in, vec_own, vec_send, vec_recv = refs

    def group_copy(j, k):
        src, mask = ((group[j].at[1], 1), (group[j].at[3], 1), (near.at[j, 1], 2))[k]
        return send(src, near.at[j, k], near_send.at[j, k], near_recv.at[j, k], p.dp(mask))

    def spread(k):
        src, dst, mask = ((normed_ref, 2, 2), (normed_ref, 1, 1), (all_ref.at[2], 3, 1))[k]
        return send(src, all_ref.at[dst], spread_send.at[k], spread_recv.at[k], p.dp(mask))

    def keep(j, k):
        return pltpu.make_async_copy(group[j].at[2 * k], kept.at[j, k], keep_sem.at[j, k])

    def norm_back(c, gain_sum):
        where = pl.ds(pl.multiple_of(c * 32, 32), 32)
        grad = kept[0, 0, where, :].astype(F32) + near[0, 0, where, :].astype(F32)
        grad = grad + near[0, 2, where, :].astype(F32)
        value = residual_ref[where, :]
        scale = lax.rsqrt(jnp.mean(value * value, axis=-1, keepdims=True) + EPS)
        weighted = grad * gain_ref[0:1]
        total = (
            cotangent_ref[where, :].astype(F32)
            + scale * weighted
            - value * (scale * scale * scale * jnp.mean(value * weighted, axis=-1, keepdims=True))
        )
        sum_ref[where, :] = total
        normed_ref[where, :] = total.astype(BF16)
        return gain_sum + jnp.sum(grad * value * scale, axis=0, keepdims=True)

    def vec_copy(k):
        device = (p.dp(1), p.dp(2), p.beside())[k]
        return send(vec_own.at[k], vec_in.at[k], vec_send.at[k], vec_recv.at[k], device)

    def vec_z(k):
        z = lax.rem(p.z + k, nz)
        return send(vec_own.at[3], vec_in.at[3 + p.z], vec_send.at[2 + k], vec_recv.at[2 + k], p.at_z(z))

    def vec_step(k):
        if k:
            vec_copy(k - 1).wait()
            vec_own[k] = vec_own[k - 1] + vec_in[k - 1]
        else:
            vec_own[0] = vec[0][...]
        if k < 3:
            vec_copy(k).start()

    p.greet()
    for j in range(groups):
        group_copy(j, 0).start()
        group_copy(j, 1).start()
        keep(j, 0).start()
        keep(j, 1).start()
    for t in range(red.ticks):
        red.tick(t)
        if t >= nz:
            owners.send_off(t - nz)
        if t == 0:
            for j in range(groups):
                group_copy(j, 0).wait_recv()
                group_copy(j, 1).wait_recv()
                keep(j, 0).wait()
                keep(j, 1).wait()
                add_into(near.at[j, 1], [kept.at[j, 1], near.at[j, 1]])
                group_copy(j, 2).start()
        if t == 1:
            if chain:
                group_copy(0, 2).wait_recv()
                rows, width = residual_ref.shape
                gain_sum = lax.fori_loop(0, rows // 32, norm_back, jnp.zeros((1, width), F32))
                gain_sum_ref[...] = jnp.broadcast_to(gain_sum, gain_sum_ref.shape)
                spread(0).start()
                spread(1).start()
                own_spread.start()
        if chain and t == 3:
            spread(0).wait_recv()
            spread(2).start()
        if vecs and t < 4:
            vec_step(t)
    for j in range(groups):
        if not chain:
            group_copy(j, 2).wait_recv()
            add_into(group_outs[j], [kept.at[j, 0], near.at[j, 0], near.at[j, 2]])
        for k in range(3):
            group_copy(j, k).wait_send()
    if chain:
        own_spread.wait()
        spread(1).wait_recv()
        spread(2).wait_recv()
        for k in range(3):
            spread(k).wait_send()
    if vecs:
        vec_in[3 + p.z] = vec_own[3]
        for k in range(1, nz):
            vec_z(k).start()
        for k in range(1, nz):
            source = lax.rem(p.z - k + nz, nz)
            ref = vec_in.at[3 + source]
            send(ref, ref, vec_send.at[2 + k], vec_recv.at[2 + k], p.at_z(source)).wait_recv()
        total = vec_in[3]
        for k in range(1, nz):
            total = total + vec_in[3 + k]
        vec_out[0][...] = total
        for k in range(1, nz):
            vec_z(k).wait_send()
    red.finish()
    owners.finish()


def make_units(nf, arrays, units):
    kinds = tuple(array.ndim == 4 for array in arrays)
    if nf > 8:
        units = [(i, array.shape[-1]) for i, array in enumerate(arrays)]
    start = [0] * len(arrays)
    full, blocks = [], []
    for i, size in units:
        full.append((i, start[i], size))
        start[i] += size
        blocks.append(((TP,) if kinds[i] else ()) + (arrays[i].shape[-2], size))
    assert all(done == array.shape[-1] for done, array in zip(start, arrays))
    return kinds, tuple(full), blocks


def reduce_outs(arrays, kinds):
    vmem, any_space = pl.BlockSpec(memory_space=pltpu.VMEM), pl.BlockSpec(memory_space=pl.ANY)
    outs = [
        jax.ShapeDtypeStruct((TP,) + array.shape[2:], BF16) if kind else jax.ShapeDtypeStruct(array.shape[1:], F32)
        for array, kind in zip(arrays, kinds)
    ]
    return outs, [any_space if kind else vmem for kind in kinds]


def reduce_all(nf, collective_id, arrays, units, groups, chain=None, vec=None):
    nz = nf // 2
    kinds, units, blocks = make_units(nf, arrays, units)
    final, to_sems = Owners.scratch(kinds, units, blocks)
    scratch = Reduce.scratch(blocks, nz) + final + to_sems
    group = groups[0]
    scratch += [pltpu.VMEM((len(groups), 3) + group.shape[1:], BF16), pltpu.VMEM((len(groups), 2) + group.shape[1:], BF16)]
    scratch += [pltpu.SemaphoreType.DMA((len(groups), 3))] * 2 + [pltpu.SemaphoreType.DMA((len(groups), 2))]
    vmem = pl.BlockSpec(memory_space=pltpu.VMEM)
    outs, out_specs = reduce_outs(arrays, kinds)
    outs += [jax.ShapeDtypeStruct(group.shape[1:], F32)] * len(groups)
    ins = list(arrays) + list(groups)
    held = len(ins)
    any_space = pl.BlockSpec(memory_space=pl.ANY)
    group_specs = [vmem] * (len(groups) + int(vec is not None))
    if chain is not None:
        group_specs = [vmem, any_space, vmem]
        scratch += [pltpu.VMEM(group.shape[1:], BF16)] + [pltpu.SemaphoreType.DMA((3,))] * 2 + [pltpu.SemaphoreType.DMA]
        outs.append(jax.ShapeDtypeStruct(group.shape, BF16))
        outs.append(jax.ShapeDtypeStruct((8, group.shape[2]), F32))
        ins += chain
    if vec is not None:
        scratch += [pltpu.VMEM((3 + nz, 8, TAIL), F32), pltpu.VMEM((4, 8, TAIL), F32)]
        scratch += [pltpu.SemaphoreType.DMA((2 + nz,))] * 2
        outs.append(jax.ShapeDtypeStruct(vec.shape, F32))
        ins.append(vec)
    return pl.pallas_call(
        partial(reduce_kernel, nf, kinds, units, len(groups), chain is not None, int(vec is not None)),
        in_specs=[any_space] * held + [vmem] * (len(ins) - held),
        out_specs=out_specs + group_specs,
        out_shape=outs,
        scratch_shapes=scratch,
        compiler_params=pltpu.CompilerParams(
            collective_id=collective_id, has_side_effects=True, vmem_limit_bytes=VMEM_LIMIT
        ),
        cost_estimate=pl.CostEstimate(
            flops=0, bytes_accessed=sum(2 * a.size * a.dtype.itemsize for a in ins), transcendentals=0
        ),
        name="reduce_" + str(collective_id),
    )(*ins)


def mixer_back_kernel(nf, kinds, units, *refs):
    arrays, n = len(kinds), len(units)
    ins, (grad_hbm, out_hbm, pos_ref, conv_ref, prm_ref, gain_ref), (proj_hbm, inv_hbm, new_hbm), refs = take(
        refs, arrays, 6, 3
    )
    outs, (gproj_hbm, gconv_ref, misc_ref), refs = take(refs, arrays, 3)
    p = Place(nf)
    own, y_in, z_in, pair_in, sems, refs = take(refs, n, n, n, n, 7)
    final, to_sems, refs = take(refs, sum(kinds[i] for i, _, _ in units), 3)
    proj_ref, inv_ref, new_ref, gmix_ref, gproj_ref, grad_ref, out_ref, load_sem, store_sem = refs
    owners = Owners(p, kinds, units, ins, outs, final, *to_sems)
    red = Reduce(p, owners.part, owners.done, own, y_in, z_in, pair_in, sems)
    rows = proj_ref.shape[0]

    def loads(g):
        at = pl.ds(pl.multiple_of(g * rows, rows), rows)
        return (
            pltpu.make_async_copy(proj_hbm.at[at], proj_ref, load_sem.at[0]),
            pltpu.make_async_copy(inv_hbm.at[pl.ds(pl.multiple_of(g * LH, LH), LH)], inv_ref, load_sem.at[1]),
            pltpu.make_async_copy(new_hbm.at[at], new_ref, load_sem.at[2]),
        )

    whole = (
        pltpu.make_async_copy(grad_hbm, grad_ref, load_sem.at[3]),
        pltpu.make_async_copy(out_hbm, out_ref, load_sem.at[4]),
    )

    def store(g):
        at = pl.ds(pl.multiple_of(g * rows, rows), rows)
        return pltpu.make_async_copy(gproj_ref, gproj_hbm.at[at], store_sem)

    def tick(t):
        if t < red.ticks:
            red.tick(t)
            if t >= p.nz:
                owners.send_off(t - p.nz)

    p.greet()
    for copy in loads(0):
        copy.start()
    gconv_ref[...] = jnp.zeros_like(gconv_ref)
    misc_ref[...] = jnp.zeros_like(misc_ref)
    tick(0)
    for copy in whole:
        copy.start()
    for copy in whole:
        copy.wait()
    every = 2

    def group(g, _):
        at = pl.ds(pl.multiple_of(g * rows, rows), rows)

        def back(c, _):
            where = pl.ds(pl.multiple_of(c * 256, 256), 256)
            gmix_ref[:, where] = mm(grad_ref[at, :], out_ref[where, :], ((1,), (1,)))
            return 0

        lax.fori_loop(0, LH * DV // 256, back, 0)
        for copy in loads(g):
            copy.wait()

        @pl.when(g > 0)
        def _():
            store(0).wait()

        for step in range(TP):

            @pl.when(g == step)
            def _():
                tick(1 + every * step)

        mixer_back(
            proj_ref, pos_ref.at[at], conv_ref, prm_ref, gain_ref, inv_ref, new_ref, gmix_ref, gproj_ref, gconv_ref, misc_ref
        )
        store(g).start()

        @pl.when(g < TP - 1)
        def _():
            for copy in loads(g + 1):
                copy.start()

        for step in range(TP):

            @pl.when(g == step)
            def _():
                tick(2 + every * step)

        return 0

    lax.fori_loop(0, TP, group, 0)
    for t in range(1 + every * TP, red.ticks):
        tick(t)
    store(0).wait()
    red.finish()
    owners.finish()


def mixer_back_all(nf, collective_id, arrays, units, grad, out, pos, conv, prm, gain, proj, inv, new):
    nz = nf // 2
    kinds, units, blocks = make_units(nf, arrays, units)
    final, to_sems = Owners.scratch(kinds, units, blocks)
    total, columns = proj.shape
    rows = total // TP
    vmem, any_space = pl.BlockSpec(memory_space=pltpu.VMEM), pl.BlockSpec(memory_space=pl.ANY)
    outs, out_specs = reduce_outs(arrays, kinds)
    outs += [
        jax.ShapeDtypeStruct((total, columns), BF16),
        jax.ShapeDtypeStruct(conv.shape, F32),
        jax.ShapeDtypeStruct((8, DV), F32),
    ]
    return pl.pallas_call(
        partial(mixer_back_kernel, nf, kinds, units),
        in_specs=[any_space] * (len(arrays) + 2) + [vmem] * 4 + [any_space] * 3,
        out_specs=out_specs + [any_space, vmem, vmem],
        out_shape=outs,
        scratch_shapes=Reduce.scratch(blocks, nz)
        + final
        + to_sems
        + [
            pltpu.VMEM((rows, columns), F32),
            pltpu.VMEM((LH, rows, rows), F32),
            pltpu.VMEM((rows, LH * DV), F32),
            pltpu.VMEM((rows, LH * DV), F32),
            pltpu.VMEM((rows, columns), BF16),
            pltpu.VMEM(grad.shape, BF16),
            pltpu.VMEM(out.shape, BF16),
            pltpu.SemaphoreType.DMA((5,)),
            pltpu.SemaphoreType.DMA,
        ],
        compiler_params=pltpu.CompilerParams(
            collective_id=collective_id, has_side_effects=True, vmem_limit_bytes=VMEM_LIMIT
        ),
        cost_estimate=pl.CostEstimate(flops=60_000_000_000, bytes_accessed=80_000_000, transcendentals=5_000_000),
        name="mixer_back",
    )(*arrays, grad, out, pos, conv, prm, gain, proj, inv, new)


def local(
    tokens,
    out_grad,
    block_first,
    block_live,
    norm1_gain,
    w_proj,
    w_decay,
    conv_w,
    w_out,
    a_log,
    dt_bias,
    head_gain,
    norm2_gain,
    w_gate_up,
    w_down,
    *,
    fsdp_size,
):
    nf = fsdp_size
    me = lax.axis_index("dp")
    rows, width = tokens.shape
    own = w_proj.shape[0]
    key_width = HEADS * DK
    value_width = HEADS * DV
    ff = w_down.shape[0] * nf

    block_index = jnp.arange(block_first.shape[0], dtype=jnp.int32)
    earlier = (block_index[:, None] >= block_index[None]) & (block_first[None] > 0)
    bucket_starts = jnp.max(jnp.where(earlier, block_index[None] * BLOCK, 0), axis=1)
    row_index = jnp.arange(rows, dtype=jnp.int32)
    position = row_index - jnp.repeat(bucket_starts, BLOCK)
    live = (row_index % BLOCK < jnp.repeat(block_live, BLOCK)).astype(F32)[:, None]

    def by_target(value):
        return value.reshape(own, TP, -1).swapaxes(0, 1)

    taps = conv_w.reshape(own, -1)
    tail = jnp.concatenate(
        [
            by_target(w_decay[:, :HEADS]),
            by_target(w_decay[:, HEADS:]),
            jnp.broadcast_to(
                jnp.concatenate([norm1_gain[:, None], norm2_gain[:, None], taps], axis=1)[None],
                (TP, own, 2 + taps.shape[1]),
            ),
        ],
        axis=2,
    )
    tail = jnp.pad(tail, ((0, 0), (0, 0), (0, TAIL - tail.shape[2])))
    pack_one = jnp.concatenate(
        [
            by_target(w_proj[:, :key_width]),
            by_target(w_proj[:, key_width : 2 * key_width]),
            by_target(w_proj[:, 2 * key_width : 2 * key_width + value_width]),
            by_target(w_proj[:, 2 * key_width + value_width :]),
            tail,
        ],
        axis=2,
    )
    pack_gate = by_target(w_gate_up[:, : ff * TP])
    pack_up = by_target(w_gate_up[:, ff * TP :])
    extra = jnp.broadcast_to(position.astype(BF16)[:, None], (rows, TAIL))
    cotangent = live * out_grad.astype(F32)
    proj_full, pack_gate, pack_up, out_full, group, grad_down = gather_all(
        nf,
        1,
        (1, 2) if nf <= 8 else (1, 1),
        ((pack_one, True), (pack_gate, False), (pack_up, False)),
        (w_out,),
        (jnp.concatenate([tokens, extra], axis=1), cotangent.astype(BF16)),
    )
    proj_full = proj_full.reshape(width, -1)
    out_full = out_full.reshape(-1, width)
    group = group.reshape(TP * rows, width + TAIL)
    grad_down = grad_down.reshape(TP * rows, width)
    group_pos = group[:, width:].astype(F32)
    group_tokens = group[:, :width].astype(F32)

    tail_full = proj_full[:, -TAIL:]
    gain_one = tail_full[:, 2 * LH].astype(F32)
    gain_two = tail_full[:, 2 * LH + 1].astype(F32)
    taps_full = tail_full[:, 2 * LH + 2 : 2 * LH + 2 + taps.shape[1]]
    taps_full = (
        taps_full.reshape(TP * nf, CONV, -1).swapaxes(0, 1).reshape(CONV, 2 * key_width + value_width).astype(F32)
    )

    def my_columns(value):
        k, v = LH * DK, LH * DV
        return jnp.concatenate(
            [
                lax.dynamic_slice_in_dim(value, me * k, k, 1),
                lax.dynamic_slice_in_dim(value, key_width + me * k, k, 1),
                lax.dynamic_slice_in_dim(value, 2 * key_width + me * v, v, 1),
            ],
            axis=1,
        )

    conv_mine = jnp.pad(my_columns(taps_full), ((0, 8 - CONV), (0, 0)))
    rate = -jnp.exp(lax.dynamic_slice_in_dim(a_log, me * LH, LH))
    bias = lax.dynamic_slice_in_dim(dt_bias, me * LH, LH)
    prm = jnp.pad(jnp.stack([rate, bias]), ((0, 6), (0, TAIL - LH)))
    gain_head = jnp.broadcast_to(head_gain[None], (8, DV))

    scale_one = lax.rsqrt(jnp.mean(group_tokens * group_tokens, axis=-1, keepdims=True) + EPS)
    normed_one = (group_tokens * scale_one * gain_one).astype(BF16)
    gain_two_rows = jnp.broadcast_to(gain_two[None], (8, width))
    proj, mixed, inv, new, residual, normed_two, gate_full, up_full, down_full = forward(
        nf,
        normed_one,
        proj_full,
        out_full,
        group_pos,
        conv_mine,
        prm,
        gain_head,
        gain_two_rows,
        tokens,
        (pack_gate, pack_up),
        w_down,
    )
    gate_full = gate_full.reshape(width, ff)
    up_full = up_full.reshape(width, ff)
    down_full = down_full.reshape(ff, width)
    normed_two = normed_two.reshape(TP * rows, width)
    gate = mm(normed_two, gate_full)
    up = mm(normed_two, up_full)
    gate_sig = jax.nn.sigmoid(gate)
    gate_act = gate * gate_sig
    hidden = (gate_act * up).astype(BF16)
    down_out = mm(hidden, down_full).astype(BF16).reshape(TP, rows, width)

    grad_wdown = mm(hidden, grad_down, ((0,), (0,))).astype(BF16).reshape(nf, -1, width)
    grad_hidden = mm(grad_down, down_full, ((1,), (1,)))
    grad_gate = (grad_hidden * up * gate_sig * (1.0 + gate * (1.0 - gate_sig))).astype(BF16)
    grad_up = (grad_hidden * gate_act).astype(BF16)
    gate_grad, up_grad = (
        mm(normed_two, grad, ((0,), (0,))).astype(BF16).reshape(TP, nf, own, ff) for grad in (grad_gate, grad_up)
    )
    grad_two = mm(grad_gate, gate_full, ((1,), (1,))) + mm(grad_up, up_full, ((1,), (1,)))
    gate_grad, up_grad, grad_residual, grad_mixed_in, gain_two_part = reduce_all(
        nf,
        2,
        (gate_grad, up_grad),
        ((0, 128), (0, 256), (0, 512), (0, 512), (1, 640), (1, 512), (1, 128), (1, 128)),
        (grad_two.astype(BF16).reshape(TP, rows, width),),
        chain=[residual, cotangent.astype(BF16), gain_two_rows],
    )
    gain_two_part = gain_two_part[0]
    grad_mixed_in = grad_mixed_in.reshape(TP * rows, width)

    wout_grad = mm(mixed, grad_mixed_in, ((0,), (0,))).astype(BF16).reshape(nf, -1, width)
    wdown_grad, wout_grad, grad_proj, grad_taps, misc = mixer_back_all(
        nf,
        5,
        (grad_wdown, wout_grad),
        ((0, 128), (0, 384), (0, 768), (0, 768), (1, 768), (1, 768), (1, 256), (1, 256)),
        grad_mixed_in,
        out_full,
        group_pos,
        conv_mine,
        prm,
        gain_head,
        proj,
        inv,
        new,
    )
    grad_one_part = mm(grad_proj, proj_full, ((1,), (1,)))
    gain_one_part = jnp.sum(grad_one_part * group_tokens * scale_one, axis=0)

    grad_taps = grad_taps[:CONV]
    k, v = LH * DK, LH * DV
    taps_all = jnp.zeros((CONV, 2 * key_width + value_width), F32)
    taps_all = lax.dynamic_update_slice(taps_all, grad_taps[:, :k], (0, me * k))
    taps_all = lax.dynamic_update_slice(taps_all, grad_taps[:, k : 2 * k], (0, key_width + me * k))
    taps_all = lax.dynamic_update_slice(taps_all, grad_taps[:, 2 * k :], (0, 2 * key_width + me * v))
    taps_all = taps_all.reshape(CONV, TP * nf, -1).swapaxes(0, 1).reshape(width, taps.shape[1])
    small = jnp.concatenate([gain_one_part[:, None], gain_two_part[:, None], taps_all], axis=1)
    columns = proj.shape[1]
    small = jnp.pad(small, ((0, 0), (columns - TAIL + 2 * LH, TAIL - 2 * LH - small.shape[1])))
    one_grad = (mm(normed_one, grad_proj, ((0,), (0,))) + small).astype(BF16).reshape(TP, nf, own, columns)

    heads_zero = jnp.zeros((HEADS,), F32)
    head_vec = jnp.concatenate(
        [
            lax.dynamic_update_slice(heads_zero, misc[1, :LH], (me * LH,)),
            lax.dynamic_update_slice(heads_zero, misc[2, :LH], (me * LH,)),
            misc[0],
        ]
    )
    head_vec = jnp.pad(head_vec, (0, 8 * TAIL - head_vec.shape[0])).reshape(8, TAIL)
    one_own, grad_one, down_sum, head_vec = reduce_all(
        nf,
        3,
        (one_grad,),
        ((0, 128), (0, 384), (0, 640), (0, 640), (0, 640), (0, 512), (0, 128), (0, 128)),
        (grad_one_part.astype(BF16).reshape(TP, rows, width), down_out),
        vec=head_vec,
    )
    head_vec = head_vec.reshape(-1)
    one_own = one_own.astype(F32)

    def columns_of(value):
        return value.swapaxes(0, 1).reshape(own, -1)

    w_gate_up_grad = jnp.concatenate(
        [columns_of(gate_grad.astype(F32)), columns_of(up_grad.astype(F32))], axis=1
    )
    w_proj_grad = jnp.concatenate(
        [
            columns_of(one_own[:, :, :k]),
            columns_of(one_own[:, :, k : 2 * k]),
            columns_of(one_own[:, :, 2 * k : 2 * k + v]),
            columns_of(one_own[:, :, 2 * k + v : 2 * k + 2 * v]),
        ],
        axis=1,
    )
    own_tail = one_own[:, :, columns - TAIL :]
    w_decay_grad = jnp.concatenate(
        [columns_of(own_tail[:, :, :LH]), columns_of(own_tail[:, :, LH : 2 * LH])], axis=1
    )
    own_small = jnp.sum(own_tail[:, :, 2 * LH : 2 * LH + 2 + taps.shape[1]], axis=0)
    norm1_gain_grad = own_small[:, 0]
    norm2_gain_grad = own_small[:, 1]
    conv_grad = own_small[:, 2:].reshape(CONV, -1)

    layer_out = (live * (residual + down_sum)).astype(BF16)
    tokens_f = tokens.astype(F32)
    scale_own = scale_one[:rows]
    weighted_one = grad_one * gain_one
    from_one = scale_own * weighted_one - tokens_f * (
        scale_own**3 * jnp.mean(tokens_f * weighted_one, axis=-1, keepdims=True)
    )
    tokens_grad = (grad_residual + from_one).astype(BF16)
    return (
        layer_out,
        tokens_grad,
        norm1_gain_grad,
        w_proj_grad,
        w_decay_grad,
        conv_grad,
        wout_grad.reshape(w_out.shape),
        head_vec[:HEADS],
        head_vec[HEADS : 2 * HEADS],
        head_vec[2 * HEADS : 2 * HEADS + DV],
        norm2_gain_grad,
        w_gate_up_grad,
        wdown_grad.reshape(w_down.shape),
    )


def solution(mesh):
    rows = P(("dp", "fsdp"), None)
    flat = P(("dp", "fsdp"))
    in_specs = (rows, rows, flat, flat, flat, rows, rows, P(None, ("dp", "fsdp")), rows, P(), P(), P(), flat, rows, rows)
    out_specs = (rows, rows, flat, rows, rows, P(None, ("dp", "fsdp")), rows, P(), P(), P(), flat, rows, rows)
    return jax.shard_map(
        partial(local, fsdp_size=mesh.shape["fsdp"]),
        mesh=mesh,
        in_specs=in_specs,
        out_specs=out_specs,
        check_vma=False,
    )
```

```python
from functools import partial

import jax
import jax.numpy as jnp
from jax import lax
from jax.experimental import pallas as pl
from jax.experimental.pallas import tpu as pltpu
from jax.sharding import PartitionSpec as P

HEADS = 16
DK = 128
DV = 256
CONV = 4
BLOCK = 64
TP = 4
LH = HEADS // TP
TAIL = 128
EPS = 1e-06
HIGH = lax.Precision.HIGHEST
F32 = jnp.float32
BF16 = jnp.bfloat16


def mm(left, right, dims=((1,), (0,))):
    return lax.dot_general(left, right, (dims, ((), ())), preferred_element_type=F32)


def mmb(left, right, dims=((1,), (0,))):
    return mm(left.astype(BF16), right.astype(BF16), dims)


def mm3(left, right, dims=((1,), (0,))):
    left_hi = left.astype(BF16)
    right_hi = right.astype(BF16)
    left_lo = (left - left_hi.astype(F32)).astype(BF16)
    right_lo = (right - right_hi.astype(F32)).astype(BF16)
    return mm(left_hi, right_hi, dims) + (mm(left_hi, right_lo, dims) + mm(left_lo, right_hi, dims))


def mmx(left, right, dims=((1,), (0,))):
    return lax.dot_general(left, right, (dims, ((), ())), precision=HIGH, preferred_element_type=F32)


def sigmoid(v):
    return 1.0 / (1.0 + jnp.exp(-v))


def conv_rows(raw, taps, pos):
    total = raw * taps[CONV - 1 : CONV]
    for lag in range(1, CONV):
        moved = pltpu.roll(raw, lag, 0)
        total = total + jnp.where(pos >= lag, moved, 0.0) * taps[CONV - 1 - lag : CONV - lag]
    return total


def conv_back(grad, raw, taps, pos):
    rows = raw.shape[0]
    total = grad * taps[CONV - 1 : CONV]
    sums = [jnp.sum(grad * raw, axis=0, keepdims=True)]
    for lag in range(1, CONV):
        kept = jnp.where(pos >= lag, grad, 0.0)
        total = total + pltpu.roll(kept, rows - lag, 0) * taps[CONV - 1 - lag : CONV - lag]
        sums.append(jnp.sum(kept * pltpu.roll(raw, lag, 0), axis=0, keepdims=True))
    return total, sums[::-1]


def unit(v, scale):
    inv = lax.rsqrt(jnp.sum(v * v, axis=-1, keepdims=True) + EPS)
    return v * (inv * scale), inv


def unit_back(grad, v, inv, scale):
    g = grad * scale
    return inv * g - v * (inv * inv * inv * jnp.sum(v * g, axis=-1, keepdims=True))


def silu_back(grad, pre, sig):
    return grad * (sig * (1.0 + pre * (1.0 - sig)))


def group_terms(tail_ref, prm_ref, pos_ref):
    rows = tail_ref.shape[0]
    pos = pos_ref[:, 0:1].astype(jnp.int32)
    row_i = lax.broadcasted_iota(jnp.int32, (rows, rows), 0)
    row_j = lax.broadcasted_iota(jnp.int32, (rows, rows), 1)
    lower = (row_j <= row_i) & (row_j >= row_i - pos)
    raw = tail_ref[...]
    shifted = raw + prm_ref[1:2]
    soft = jnp.maximum(shifted, 0.0) + jnp.log1p(jnp.exp(-jnp.abs(shifted)))
    log_decay = prm_ref[0:1] * soft
    beta = sigmoid(raw)
    lower_f = lower.astype(F32)
    cum = mmx(lower_f, log_decay)
    return pos, row_i, row_j, lower, lower_f, raw, shifted, log_decay, beta, cum, cum.T


def head_slices(head):
    key_width = LH * DK
    return (
        slice(head * DK, (head + 1) * DK),
        slice(key_width + head * DK, key_width + (head + 1) * DK),
        slice(2 * key_width + head * DV, 2 * key_width + (head + 1) * DV),
        slice(2 * key_width + (LH + head) * DV, 2 * key_width + (LH + head + 1) * DV),
    )


def mixer_forward(proj_ref, pos_ref, conv_ref, prm_ref, gain_ref, mixed_ref, inv_ref, new_ref):
    width = proj_ref.shape[1]
    tail_ref = proj_ref.at[:, width - TAIL :]
    pos, row_i, row_j, lower, _, _, _, _, beta_all, cum, cum_t = group_terms(tail_ref, prm_ref, pos_ref)
    strict = lower & (row_j < row_i)
    bits = row_i ^ row_j
    eye = (bits == 0).astype(F32)
    lows, attends, values = [], [], []
    for head in range(LH):
        sq, sk, sv, _ = head_slices(head)
        q_pre = conv_rows(proj_ref[:, sq], conv_ref[:, sq], pos)
        k_pre = conv_rows(proj_ref[:, sk], conv_ref[:, sk], pos)
        v_pre = conv_rows(proj_ref[:, sv], conv_ref[:, sv], pos)
        query, _ = unit(q_pre * sigmoid(q_pre), DK**-0.5)
        key, _ = unit(k_pre * sigmoid(k_pre), 1.0)
        beta = beta_all[:, LH + head : LH + head + 1]
        values.append(beta * (v_pre * sigmoid(v_pre)))
        gap = cum[:, head : head + 1] - cum_t[head : head + 1, :]
        decay = jnp.where(lower, jnp.exp(gap), 0.0)
        attends.append(mm3(query, key, ((1,), (1,))) * decay)
        lows.append(jnp.where(strict, beta * mm3(key, key, ((1,), (1,))) * decay, 0.0))
    invs = [eye - jnp.where(bits == 1, low, 0.0) for low in lows]
    step = 1
    while (2 << step) <= proj_ref.shape[0]:
        keep = (bits >> step) == 1
        parts = [mm3(jnp.where(keep, low, 0.0), inv) for low, inv in zip(lows, invs)]
        invs = [inv - mm3(inv, part) for inv, part in zip(invs, parts)]
        step += 1
    news = [mm3(inv, value) for inv, value in zip(invs, values)]
    mixes = [mm3(attend, new) for attend, new in zip(attends, news)]
    for head in range(LH):
        mix = mixes[head]
        scale = lax.rsqrt(jnp.mean(mix * mix, axis=-1, keepdims=True) + EPS)
        gate = proj_ref[:, head_slices(head)[3]]
        out = mix * scale * gain_ref[0:1] * (gate * sigmoid(gate))
        mixed_ref[:, head * DV : (head + 1) * DV] = out.astype(BF16)
        inv_ref[head] = invs[head]
        new_ref[:, head * DV : (head + 1) * DV] = news[head]


def mixer_back(
    proj_ref, pos_ref, conv_ref, prm_ref, gain_ref, inv_ref, new_ref, gmix_ref, gproj_ref, gconv_ref, misc_ref
):
    width = proj_ref.shape[1]
    rows = proj_ref.shape[0]
    tail_ref = proj_ref.at[:, width - TAIL :]
    pos, row_i, row_j, lower, lower_f, raw, shifted, log_decay, beta_all, cum, cum_t = group_terms(
        tail_ref, prm_ref, pos_ref
    )
    strict = lower & (row_j < row_i)
    lane = lax.broadcasted_iota(jnp.int32, (rows, TAIL), 1)
    ones = jnp.ones((rows, TAIL), F32)
    grad_cum = jnp.zeros((rows, TAIL), F32)
    grad_beta_all = jnp.zeros((rows, TAIL), F32)
    gain_sum = jnp.zeros((1, DV), F32)
    for head in range(LH):
        sq, sk, sv, sg = head_slices(head)
        q_raw, k_raw, v_raw = proj_ref[:, sq], proj_ref[:, sk], proj_ref[:, sv]
        q_pre = conv_rows(q_raw, conv_ref[:, sq], pos)
        k_pre = conv_rows(k_raw, conv_ref[:, sk], pos)
        v_pre = conv_rows(v_raw, conv_ref[:, sv], pos)
        q_sig, k_sig, v_sig = sigmoid(q_pre), sigmoid(k_pre), sigmoid(v_pre)
        q_act, k_act, value = q_pre * q_sig, k_pre * k_sig, v_pre * v_sig
        query, q_inv = unit(q_act, DK**-0.5)
        key, k_inv = unit(k_act, 1.0)
        query_b, key_b = query, key
        beta = beta_all[:, LH + head : LH + head + 1]
        gap = cum[:, head : head + 1] - cum_t[head : head + 1, :]
        decay = jnp.where(lower, jnp.exp(gap), 0.0)
        pair = mm3(key_b, key_b, ((1,), (1,)))
        query_pair = mm3(query_b, key_b, ((1,), (1,)))
        attend = query_pair * decay
        inv = inv_ref[head]
        new = new_ref[:, head * DV : (head + 1) * DV]
        mix = mm3(attend, new)
        scale = lax.rsqrt(jnp.mean(mix * mix, axis=-1, keepdims=True) + EPS)
        gate = proj_ref[:, sg]
        gate_sig = sigmoid(gate)
        grad_out = gmix_ref[:, head * DV : (head + 1) * DV]
        unscaled = mix * scale
        grad_norm = grad_out * (gate * gate_sig)
        grad_gate = silu_back(grad_out * unscaled * gain_ref[0:1], gate, gate_sig)
        gain_sum = gain_sum + jnp.sum(grad_norm * unscaled, axis=0, keepdims=True)
        weighted = grad_norm * gain_ref[0:1]
        grad_mix = scale * weighted - mix * (
            scale * scale * scale * jnp.mean(mix * weighted, axis=-1, keepdims=True)
        )
        grad_mix_b = grad_mix
        grad_new = mm3(attend, grad_mix_b, ((0,), (0,)))
        grad_attend = mm3(grad_mix_b, new, ((1,), (1,)))
        grad_rhs = mm3(inv, grad_new, ((0,), (0,)))
        grad_low = -mm3(grad_rhs, new, ((1,), (1,)))
        grad_value = beta * grad_rhs
        low_decay = jnp.where(strict, grad_low * decay, 0.0)
        low_pair = low_decay * pair
        grad_beta = jnp.sum(grad_rhs * value, axis=-1, keepdims=True) + jnp.sum(
            low_pair, axis=-1, keepdims=True
        )
        grad_pair = beta * low_decay
        grad_query_pair = grad_attend * decay
        both = beta * low_pair + grad_query_pair * query_pair
        column = jnp.sum(both, axis=-1, keepdims=True) - mmx(both, ones, ((0,), (0,)))
        grad_cum = jnp.where(lane == head, column, grad_cum)
        grad_beta_all = jnp.where(lane == LH + head, grad_beta, grad_beta_all)
        grad_pair_b = grad_pair
        grad_qp_b = grad_query_pair
        grad_query = mm3(grad_qp_b, key_b)
        grad_key = (
            mm3(grad_qp_b, query_b, ((0,), (0,))) + mm3(grad_pair_b, key_b) + mm3(grad_pair_b, key_b, ((0,), (0,)))
        )
        grad_q = silu_back(unit_back(grad_query, q_act, q_inv, DK**-0.5), q_pre, q_sig)
        grad_k = silu_back(unit_back(grad_key, k_act, k_inv, 1.0), k_pre, k_sig)
        grad_v = silu_back(grad_value, v_pre, v_sig)
        for grad, part, where in ((grad_q, q_raw, sq), (grad_k, k_raw, sk), (grad_v, v_raw, sv)):
            moved, sums = conv_back(grad, part, conv_ref[:, where], pos)
            gproj_ref[:, where] = moved.astype(BF16)
            for tap in range(CONV):
                gconv_ref[tap : tap + 1, where] += sums[tap]
        gproj_ref[:, sg] = grad_gate.astype(BF16)
    grad_log = mmx(lower_f, grad_cum, ((0,), (0,)))
    grad_step = grad_log * prm_ref[0:1] * sigmoid(shifted)
    grad_tail = grad_step + grad_beta_all * beta_all * (1.0 - beta_all)
    gproj_ref[:, width - TAIL :] = grad_tail.astype(BF16)
    misc_ref[0:1, :] += gain_sum
    misc_ref[1:2, 0:TAIL] += jnp.sum(grad_log * log_decay, axis=0, keepdims=True)
    misc_ref[2:3, 0:TAIL] += jnp.sum(grad_step, axis=0, keepdims=True)


VMEM_LIMIT = 60 * 1024 * 1024


MESH = pl.DeviceIdType.MESH


class Place:
    def __init__(self, nf):
        self.nf, self.nz = nf, nf // 2
        self.d = lax.axis_index("dp")
        self.f = lax.axis_index("fsdp")
        self.z, self.y = self.f // 2, self.f % 2
        self.over = self.z < self.nz - 1
        self.under = self.z > 0

    def flip(self, value, mask):
        return value + mask * (1 - 2 * ((value // mask) % 2))

    def dp(self, mask):
        if mask == 3:
            return (self.flip(self.flip(self.d, 1), 2), self.f)
        return (self.flip(self.d, mask), self.f)

    def at_z(self, z):
        return (self.d, z * 2 + self.y)

    def beside(self):
        return (self.d, self.flip(self.f, 1))

    def greet(self):
        barrier = pltpu.get_barrier_semaphore()
        for mask in (1, 2, 3):
            pl.semaphore_signal(barrier, inc=1, device_id=self.dp(mask), device_id_type=MESH)
        pl.semaphore_signal(barrier, inc=1, device_id=self.beside(), device_id_type=MESH)

        @pl.when(self.over)
        def _():
            pl.semaphore_signal(barrier, inc=1, device_id=self.at_z(self.z + 1), device_id_type=MESH)

        @pl.when(self.under)
        def _():
            pl.semaphore_signal(barrier, inc=1, device_id=self.at_z(self.z - 1), device_id_type=MESH)

        pl.semaphore_wait(barrier, 4 + self.over.astype(jnp.int32) + self.under.astype(jnp.int32))


def send(src, dst, send_sem, recv_sem, device):
    return pltpu.make_async_remote_copy(
        src_ref=src, dst_ref=dst, send_sem=send_sem, recv_sem=recv_sem, device_id=device, device_id_type=MESH
    )


def pieces(columns, count):
    tiles = columns // 128
    edges = [128 * (tiles * c // count) for c in range(count + 1)]
    return [(edge, after - edge) for edge, after in zip(edges, edges[1:])]


def nothing():
    return None


class Gather:
    def __init__(self, place, ahead, lag, views, ready, up_send, down_send, z_recv, y_send, y_recv, pair_send, pair_recv):
        self.p, self.ahead, self.views, self.ready = place, ahead, views, ready
        self.up_send, self.down_send, self.z_recv = up_send, down_send, z_recv
        self.y_send, self.y_recv, self.pair_send, self.pair_recv = y_send, y_recv, pair_send, pair_recv
        self.lag = lag
        self.ticks = len(views) + lag * (place.nz - 1)

    @staticmethod
    def scratch(units, nz):
        return [
            pltpu.SemaphoreType.DMA((units, nz)),
            pltpu.SemaphoreType.DMA((units, nz)),
            pltpu.SemaphoreType.DMA((units, nz)),
            pltpu.SemaphoreType.DMA((units, nz)),
            pltpu.SemaphoreType.DMA((units, nz)),
            pltpu.SemaphoreType.DMA((units,)),
            pltpu.SemaphoreType.DMA((units,)),
        ]

    def block(self, u, z, y):
        return self.views[u](z * 2 + y)

    def up(self, u, r):
        ref = self.block(u, self.p.z - (r - 1), self.p.y)
        return send(ref, ref, self.up_send.at[u, r], self.z_recv.at[u, r], self.p.at_z(self.p.z + 1))

    def down(self, u, r):
        ref = self.block(u, self.p.z + (r - 1), self.p.y)
        nz = self.p.nz
        return send(ref, ref, self.down_send.at[u, r], self.z_recv.at[u, nz - r], self.p.at_z(self.p.z - 1))

    def over_y(self, u, r):
        ref = self.block(u, lax.rem(self.p.z - r + self.p.nz, self.p.nz), self.p.y)
        return send(ref, ref, self.y_send.at[u, r], self.y_recv.at[u, r], self.p.beside())

    def pair(self, u):
        ref = self.block(u, self.p.z, 1 - self.p.y)
        return send(ref, ref, self.pair_send.at[u], self.pair_recv.at[u], self.p.at_z(self.p.flip(self.p.z, 1)))

    def wait_z(self, u, r):
        ref = self.block(u, lax.rem(self.p.z - r + self.p.nz, self.p.nz), self.p.y)
        send(ref, ref, self.up_send.at[u, 1], self.z_recv.at[u, r], self.p.beside()).wait_recv()

    def wait_y(self, u, r):
        ref = self.block(u, lax.rem(self.p.z - r + self.p.nz, self.p.nz), 1 - self.p.y)
        send(ref, ref, self.y_send.at[u, r], self.y_recv.at[u, r], self.p.beside()).wait_recv()

    def wait_pair(self, u):
        other = self.p.flip(self.p.z, 1)
        ref = self.block(u, other, 1 - self.p.y)
        send(ref, ref, self.pair_send.at[u], self.pair_recv.at[u], self.p.at_z(other)).wait_recv()

    def odd(self, u):
        return u % 2 == 1

    def skips(self, u, r):
        if not self.odd(u) or r not in (1, self.p.nz - 1):
            return None
        odd = self.p.z % 2 == 1
        if self.p.nz == 2:
            return odd | ~odd
        return odd if r == 1 else ~odd

    def unless_skipped(self, u, r, action):
        skip = self.skips(u, r)
        if skip is None:
            action()
        else:
            pl.when(~skip)(action)

    def own(self, t):
        p = self.p
        self.ready[t]()

        @pl.when(p.over)
        def _():
            self.up(t, 1).start()

        @pl.when(p.under)
        def _():
            self.down(t, 1).start()

        self.over_y(t, 0).start()

    def tick(self, t):
        p, nz = self.p, self.p.nz
        for u in range(self.ahead + 1) if t == 0 else (t + self.ahead,):
            if u < len(self.views):
                self.own(u)
        for s in range(1, nz):
            u = t - s * self.lag
            if not 0 <= u < len(self.views):
                continue

            @pl.when(p.z >= s)
            def _():
                self.wait_z(u, s)

                @pl.when(p.over)
                def _():
                    self.up(u, s + 1).start()

                self.unless_skipped(u, s, self.over_y(u, s).start)

            @pl.when(p.z <= nz - 1 - s)
            def _():
                self.wait_z(u, nz - s)

                @pl.when(p.under)
                def _():
                    self.down(u, s + 1).start()

                self.unless_skipped(u, nz - s, self.over_y(u, nz - s).start)

            if s == nz - 1 and self.odd(u):
                self.wait_y(u, 0)
                self.pair(u).start()

    def finish(self):
        p, nz = self.p, self.p.nz
        for u in range(len(self.views)):
            if not self.odd(u):
                self.wait_y(u, 0)
            else:
                self.wait_pair(u)
                self.pair(u).wait_send()
            self.over_y(u, 0).wait_send()
            for r in range(1, nz):

                def both():
                    self.wait_y(u, r)
                    self.over_y(u, r).wait_send()

                self.unless_skipped(u, r, both)
            for r in range(1, nz):

                @pl.when(p.over & (p.z >= r - 1))
                def _():
                    self.up(u, r).wait_send()

                @pl.when(p.under & (p.z <= nz - r))
                def _():
                    self.down(u, r).wait_send()


def gather_kernel(nf, splits, packs, shards, groups, *refs):
    count = len(packs) + len(shards) + groups
    ins, outs = refs[:count], refs[count : 2 * count]
    to_send, to_recv, near_send, near_recv, local_sem = refs[2 * count : 2 * count + 5]
    p = Place(nf)
    pack_in, shard_in, group_in = ins[: len(packs)], ins[len(packs) : len(packs) + len(shards)], ins[count - groups :]
    pack_out, shard_out, group_out = (
        outs[: len(packs)],
        outs[len(packs) : len(packs) + len(shards)],
        outs[count - groups :],
    )

    def own_pack(i, d):
        return pack_out[i].at[d, p.f] if packs[i] else pack_out[i].at[d]

    def exchange(i, m):
        target = p.dp(m)
        return send(pack_in[i].at[target[0]], own_pack(i, p.d), to_send.at[i, m], to_recv.at[i, m], target)

    def wait_exchange(i, m):
        source = p.dp(m)
        ref = own_pack(i, source[0])
        send(ref, ref, to_send.at[i, m], to_recv.at[i, m], source).wait_recv()

    def near(j, k):
        src, dst, mask = ((group_in[j], 2, 2), (group_in[j], 1, 1), (group_out[j].at[2], 3, 1))[k]
        return send(src, group_out[j].at[dst], near_send.at[j, k], near_recv.at[j, k], p.dp(mask))

    def wait_near(j, k):
        ref = group_out[j].at[(2, 1, 3)[k]]
        send(ref, ref, near_send.at[j, k], near_recv.at[j, k], p.dp(1)).wait_recv()

    def local(n):
        if n < len(packs):
            return pltpu.make_async_copy(pack_in[n].at[p.d], own_pack(n, p.d), local_sem.at[n])
        if n < len(packs) + len(shards):
            i = n - len(packs)
            return pltpu.make_async_copy(shard_in[i], shard_out[i].at[p.f], local_sem.at[n])
        j = n - len(packs) - len(shards)
        return pltpu.make_async_copy(group_in[j], group_out[j].at[0], local_sem.at[n])

    p.greet()
    views, ready = [], []
    for i, whole in enumerate(packs):
        for m in range(TP if whole else 0):
            source = p.dp(m)[0] if m else p.d
            for c, (start, size) in enumerate(pieces(pack_in[i].shape[-1], splits[0])):
                views.append(lambda f, i=i, d=source, at=pl.ds(start, size): pack_out[i].at[d, f, :, at])
                ready.append(nothing if c else partial(wait_exchange, i, m) if m else local(i).wait)
    for i in range(len(shards)):
        for c, (start, size) in enumerate(pieces(shard_in[i].shape[-1], splits[1])):
            views.append(lambda f, i=i, at=pl.ds(start, size): shard_out[i].at[f, :, at])
            ready.append(nothing if c else local(len(packs) + i).wait)
    gather = Gather(p, 3, 1, views, ready, *refs[2 * count + 5 :])
    for n in range(count):
        local(n).start()
    for m in (1, 2, 3):
        exchange(0, m).start()
    for j in range(groups):
        near(j, 0).start()
        near(j, 1).start()
    for i in range(1, len(packs)):
        for m in (2, 3, 1):
            exchange(i, m).start()
    for t in range(gather.ticks):
        gather.tick(t)
        if t == 2:
            for j in range(groups):
                wait_near(j, 0)
                near(j, 2).start()
    gather.finish()
    for i, whole in enumerate(packs):
        for m in (1, 2, 3):
            exchange(i, m).wait_send()
            if not whole:
                wait_exchange(i, m)
        if not whole:
            local(i).wait()
    for j in range(groups):
        wait_near(j, 1)
        wait_near(j, 2)
        for k in range(3):
            near(j, k).wait_send()
        local(len(packs) + len(shards) + j).wait()


def gather_all(nf, collective_id, splits, packs, shards, groups):
    marks = tuple(whole for _, whole in packs)
    ins = [array for array, _ in packs] + list(shards) + list(groups)
    outs = (
        [
            jax.ShapeDtypeStruct(array.shape[:1] + ((nf,) if whole else ()) + array.shape[1:], array.dtype)
            for array, whole in packs
        ]
        + [jax.ShapeDtypeStruct((nf,) + array.shape, array.dtype) for array in shards]
        + [jax.ShapeDtypeStruct((TP,) + array.shape, array.dtype) for array in groups]
    )
    units = TP * sum(marks) * splits[0] + len(shards) * splits[1]
    sent = sum(out.size * 2 for out in outs)
    any_space = pl.BlockSpec(memory_space=pl.ANY)
    return pl.pallas_call(
        partial(gather_kernel, nf, splits, marks, (True,) * len(shards), len(groups)),
        in_specs=[any_space] * len(ins),
        out_specs=[any_space] * len(outs),
        out_shape=outs,
        scratch_shapes=[
            pltpu.SemaphoreType.DMA((len(packs), TP)),
            pltpu.SemaphoreType.DMA((len(packs), TP)),
            pltpu.SemaphoreType.DMA((max(len(groups), 1), 3)),
            pltpu.SemaphoreType.DMA((max(len(groups), 1), 3)),
            pltpu.SemaphoreType.DMA((len(ins),)),
        ]
        + Gather.scratch(units, nf // 2),
        compiler_params=pltpu.CompilerParams(
            collective_id=collective_id, has_side_effects=True, vmem_limit_bytes=1024 * 1024
        ),
        cost_estimate=pl.CostEstimate(flops=0, bytes_accessed=2 * sent, transcendentals=0),
        name="gather_" + str(collective_id),
    )(*ins)


def add_into(dst, srcs):
    rows = dst.shape[-2]
    size = 16 if rows % 16 == 0 else rows
    lead = dst.shape[0] if len(dst.shape) == 3 else 1

    def body(i, _):
        at = pl.ds(pl.multiple_of((i % (rows // size)) * size, size), size)
        where = (i // (rows // size), at) if len(dst.shape) == 3 else (at,)
        total = srcs[0][where].astype(F32)
        for src in srcs[1:]:
            total = total + src[where].astype(F32)
        dst[where] = total.astype(dst.dtype)
        return 0

    lax.fori_loop(0, lead * (rows // size), body, 0)


PER = 2


def forward_kernel(nf, split, *refs):
    (x_hbm, w_hbm, out_hbm, pos_ref, conv_ref, prm_ref, gain_ref, gain_two_ref, tokens_ref), refs = refs[:9], refs[9:]
    pack_in, shard_in, refs = refs[:2], refs[2], refs[3:]
    (proj_hbm, mixed_hbm, inv_hbm, new_hbm, residual_ref, group_hbm), refs = refs[:6], refs[6:]
    pack_out, shard_out, refs = refs[:2], refs[2], refs[3:]
    (proj_ref, mixed_ref, inv_ref, new_ref, parts_ref, near_ref, stage_sem), refs = refs[:7], refs[7:]
    (part_send, part_recv, group_send, group_recv, local_sem), refs = refs[:5], refs[5:]
    (x_ref, w_ref, out_ref, normed_ref, load_sem), refs = refs[:5], refs[5:]
    p = Place(nf)
    quarter = w_hbm.shape[0] // 4
    loads = [pltpu.make_async_copy(x_hbm, x_ref, load_sem.at[0])]
    for k in range(4):
        at = pl.ds(k * quarter, quarter)
        loads.append(pltpu.make_async_copy(w_hbm.at[at], w_ref.at[at], load_sem.at[1 + k]))
    loads.append(pltpu.make_async_copy(out_hbm, out_ref, load_sem.at[5]))
    rows = tokens_ref.shape[0]
    width = tokens_ref.shape[1]

    local = [pltpu.make_async_copy(pack_in[i], pack_out[i].at[:, p.f], local_sem.at[i]) for i in range(2)]
    local.append(pltpu.make_async_copy(shard_in, shard_out.at[p.f], local_sem.at[2]))

    views, ready = [], []
    for i in range(2):
        for d in range(TP):
            views.append(lambda f, i=i, d=d: pack_out[i].at[d, f])
            ready.append(nothing if d else local[i].wait)
    for c, (start, size) in enumerate(pieces(width, split)):
        views.append(lambda f, at=pl.ds(start, size): shard_out.at[f, :, at])
        ready.append(nothing if c else local[2].wait)
    p.greet()
    for copy in local:
        copy.start()
    gather = Gather(p, 3, 1, views, ready, *refs)

    def part_copy(k):
        src, mask = ((parts_ref.at[1], 1), (parts_ref.at[3], 1), (near_ref.at[1], 2))[k]
        return send(src, near_ref.at[k], part_send.at[k], part_recv.at[k], p.dp(mask))

    def group_copy(k):
        src, dst, mask = ((normed_ref, 2, 2), (normed_ref, 1, 1), (group_hbm.at[2], 3, 1))[k]
        return send(src, group_hbm.at[dst], group_send.at[k], group_recv.at[k], p.dp(mask))

    own_normed = pltpu.make_async_copy(normed_ref, group_hbm.at[0], load_sem.at[6])

    def stage_copies(g):
        at = pl.ds(pl.multiple_of(g * rows, rows), rows)
        return (
            pltpu.make_async_copy(proj_ref, proj_hbm.at[at], stage_sem.at[0]),
            pltpu.make_async_copy(mixed_ref, mixed_hbm.at[at], stage_sem.at[1]),
            pltpu.make_async_copy(inv_ref, inv_hbm.at[pl.ds(pl.multiple_of(g * LH, LH), LH)], stage_sem.at[2]),
            pltpu.make_async_copy(new_ref, new_hbm.at[at], stage_sem.at[3]),
        )

    columns = w_ref.shape[1]
    tile = 640
    gather.tick(0)
    for load in loads:
        load.start()
    for load in loads:
        load.wait()

    def group(i, _):
        half = i // 2
        g = 2 * i + 1 - half * (3 + 4 * (i - 2 * half))

        @pl.when(i > 0)
        def _():
            for copy in stage_copies(0):
                copy.wait()

        at = pl.ds(pl.multiple_of(g * rows, rows), rows)

        def project(c, _):
            where = pl.ds(pl.multiple_of(c * tile, tile), tile)
            proj_ref[:, where] = mm(x_ref[at, :], w_ref[:, where])
            return 0

        lax.fori_loop(0, columns // tile, project, 0)
        for step in range(TP):

            @pl.when(i == step)
            def _():
                for t in range(PER // 2):
                    gather.tick(1 + PER * step + t)

        mixer_forward(proj_ref, pos_ref.at[at], conv_ref, prm_ref, gain_ref, mixed_ref, inv_ref, new_ref)
        for copy in stage_copies(g):
            copy.start()

        def project_out(c, _):
            where = pl.ds(pl.multiple_of(c * 512, 512), 512)
            parts_ref[g, :, where] = mm(mixed_ref[...], out_ref[:, where]).astype(BF16)
            return 0

        lax.fori_loop(0, width // 512, project_out, 0)
        for step in range(TP):

            @pl.when(i == step)
            def _():
                if step < 2:
                    part_copy(step).start()
                if step == 2:
                    part_copy(1).wait_recv()
                    add_into(parts_ref.at[2], [parts_ref.at[2], near_ref.at[1]])
                    send(parts_ref.at[2], near_ref.at[2], part_send.at[2], part_recv.at[2], p.dp(2)).start()
                for t in range(PER // 2, PER):
                    gather.tick(1 + PER * step + t)

        return 0

    lax.fori_loop(0, TP, group, 0)
    part_copy(0).wait_recv()
    far = send(parts_ref.at[2], near_ref.at[2], part_send.at[2], part_recv.at[2], p.dp(2))
    far.wait_recv()

    def norm(c, _):
        where = pl.ds(pl.multiple_of(c * 64, 64), 64)
        total = tokens_ref[where, :].astype(F32) + parts_ref[0, where, :].astype(F32)
        total = total + near_ref[0, where, :].astype(F32) + near_ref[2, where, :].astype(F32)
        residual_ref[where, :] = total
        scale = lax.rsqrt(jnp.mean(total * total, axis=-1, keepdims=True) + EPS)
        normed_ref[where, :] = (total * scale * gain_two_ref[0:1]).astype(BF16)
        return 0

    lax.fori_loop(0, rows // 64, norm, 0)
    group_copy(0).start()
    group_copy(1).start()
    own_normed.start()
    for t in range(1 + PER * TP, gather.ticks):
        gather.tick(t)
        if t == min(3 + PER * TP, gather.ticks - 1):
            group_copy(0).wait_recv()
            group_copy(2).start()
    gather.finish()
    for copy in stage_copies(0):
        copy.wait()
    part_copy(0).wait_send()
    part_copy(1).wait_send()
    far.wait_send()
    own_normed.wait()
    for k in (1, 2):
        group_copy(k).wait_recv()
    for k in range(3):
        group_copy(k).wait_send()


def forward(nf, x, w, out, pos, conv, prm, gain, gain_two, tokens, packs, shard):
    total, columns = x.shape[0], w.shape[1]
    rows, width = tokens.shape
    split = 4 if nf <= 8 else 1
    vmem, any_space = pl.BlockSpec(memory_space=pltpu.VMEM), pl.BlockSpec(memory_space=pl.ANY)
    outs = [
        jax.ShapeDtypeStruct((total, columns), F32),
        jax.ShapeDtypeStruct((total, LH * DV), BF16),
        jax.ShapeDtypeStruct((TP * LH, rows, rows), F32),
        jax.ShapeDtypeStruct((total, LH * DV), F32),
        jax.ShapeDtypeStruct((rows, width), F32),
        jax.ShapeDtypeStruct((TP, rows, width), BF16),
    ]
    outs += [jax.ShapeDtypeStruct((TP, nf) + pack.shape[1:], BF16) for pack in packs]
    outs += [jax.ShapeDtypeStruct((nf,) + shard.shape, BF16)]
    return pl.pallas_call(
        partial(forward_kernel, nf, split),
        in_specs=[any_space] * 3 + [vmem] * 6 + [any_space] * 3,
        out_specs=[any_space] * 4 + [vmem] + [any_space] * 4,
        out_shape=outs,
        scratch_shapes=[
            pltpu.VMEM((rows, columns), F32),
            pltpu.VMEM((rows, LH * DV), BF16),
            pltpu.VMEM((LH, rows, rows), F32),
            pltpu.VMEM((rows, LH * DV), F32),
            pltpu.VMEM((TP, rows, width), BF16),
            pltpu.VMEM((3, rows, width), BF16),
            pltpu.SemaphoreType.DMA((4,)),
            pltpu.SemaphoreType.DMA((3,)),
            pltpu.SemaphoreType.DMA((3,)),
            pltpu.SemaphoreType.DMA((3,)),
            pltpu.SemaphoreType.DMA((3,)),
            pltpu.SemaphoreType.DMA((3,)),
            pltpu.VMEM(x.shape, BF16),
            pltpu.VMEM(w.shape, BF16),
            pltpu.VMEM(out.shape, BF16),
            pltpu.VMEM((rows, width), BF16),
            pltpu.SemaphoreType.DMA((7,)),
        ]
        + Gather.scratch(2 * TP + split, nf // 2),
        compiler_params=pltpu.CompilerParams(
            collective_id=4, has_side_effects=True, vmem_limit_bytes=VMEM_LIMIT
        ),
        cost_estimate=pl.CostEstimate(flops=45_000_000_000, bytes_accessed=80_000_000, transcendentals=5_000_000),
        name="forward",
    )(x, w, out, pos, conv, prm, gain, gain_two, tokens, *packs, shard)


AHEAD, OLD_FIRST = 2, True


class Reduce:
    def __init__(self, place, part, done, own, y_in, z_in, pair_in, sems):
        self.p, self.part, self.done = place, part, done
        self.own, self.y_in, self.z_in, self.pair_in = own, y_in, z_in, pair_in
        self.y_send, self.y_recv, self.z_send, self.z_recv, self.pair_send, self.pair_recv, self.load_sem = sems
        self.count = len(y_in)
        self.ticks = self.count + place.nz

    @staticmethod
    def scratch(blocks, nz):
        units = len(blocks)
        return (
            [pltpu.VMEM((nz + u % 2,) + block, BF16) for u, block in enumerate(blocks)]
            + [pltpu.VMEM((nz,) + block, BF16) for block in blocks]
            + [pltpu.VMEM((nz + 1,) + block, BF16) for block in blocks]
            + [pltpu.VMEM(block if u % 2 else (8, 128), BF16) for u, block in enumerate(blocks)]
            + [pltpu.SemaphoreType.DMA((units, nz))] * 3
            + [pltpu.SemaphoreType.DMA((units, nz + 1))]
            + [pltpu.SemaphoreType.DMA((units,))] * 2
            + [pltpu.SemaphoreType.DMA((units, nz + 1))]
        )

    def odd(self, u):
        return u % 2 == 1

    def copy_y(self, u, z0):
        src = self.part(u, z0 * 2 + 1 - self.p.y)
        return send(src, self.y_in[u].at[z0], self.y_send.at[u, z0], self.y_recv.at[u, z0], self.p.beside())

    def copy_late(self, u):
        z = self.p.z
        return send(self.pair_in[u], self.y_in[u].at[z], self.y_send.at[u, z], self.y_recv.at[u, z], self.p.beside())

    def copy_pair(self, u):
        other = self.p.flip(self.p.z, 1)
        src = self.part(u, other * 2 + 1 - self.p.y)
        return send(src, self.pair_in[u], self.pair_send.at[u], self.pair_recv.at[u], self.p.at_z(other))

    def copy_z(self, u, z0, slot, z):
        return send(self.y_in[u].at[z0], self.z_in[u].at[slot], self.z_send.at[u, z0], self.z_recv.at[u, slot], self.p.at_z(z))

    def wait_z(self, u, slot):
        ref = self.z_in[u].at[slot]
        send(ref, ref, self.z_send.at[u, 0], self.z_recv.at[u, slot], self.p.beside()).wait_recv()

    def pass_on(self, u, z0, arrived, slot, z):
        own = self.own[u].at[z0]
        here = self.y_in[u].at[z0]
        if self.odd(u):
            other = self.p.flip(self.p.z, 1)

            @pl.when(other != z0)
            def _():
                add_into(here, [own, here] + arrived)

            @pl.when(other == z0)
            def _():
                add_into(here, [own] + arrived)
        else:
            add_into(here, [own, here] + arrived)
        self.copy_z(u, z0, slot, z).start()

    def loads(self, u):
        p, nz = self.p, self.p.nz
        copies = [
            pltpu.make_async_copy(self.part(u, z0 * 2 + p.y), self.own[u].at[z0], self.load_sem.at[u, z0])
            for z0 in range(nz)
        ]
        if self.odd(u):
            src = self.part(u, p.z * 2 + 1 - p.y)
            copies.append(pltpu.make_async_copy(src, self.own[u].at[nz], self.load_sem.at[u, nz]))
        return copies

    def begin(self, u):
        p, nz = self.p, self.p.nz
        if self.odd(u):
            self.copy_pair(u).start()
            other = p.flip(p.z, 1)
            for z0 in range(nz):

                @pl.when((z0 != p.z) & (z0 != other))
                def _():
                    self.copy_y(u, z0).start()
        else:
            for z0 in range(nz):
                self.copy_y(u, z0).start()
        for load in self.loads(u):
            load.start()

    def set_out(self, u):
        p, nz = self.p, self.p.nz
        for load in self.loads(u):
            load.wait()
        if self.odd(u):
            self.copy_pair(u).wait_recv()
            add_into(self.pair_in[u], [self.pair_in[u], self.own[u].at[nz]])
            self.copy_late(u).start()
        other = p.flip(p.z, 1)
        for z0 in range(nz):
            needed = (z0 != p.z) & (z0 != other) if self.odd(u) else z0 != p.z

            @pl.when(needed)
            def _():
                self.copy_y(u, z0).wait_recv()

        @pl.when(p.z == nz - 1)
        def _():
            for z0 in range(nz - 1):
                self.pass_on(u, z0, [], z0, p.z - 1)

        @pl.when(p.z == 0)
        def _():
            for z0 in range(nz - 1, 0, -1):
                self.pass_on(u, z0, [], nz if z0 == 1 else z0, p.z + 1)

    def relay(self, u, hop):
        p, nz = self.p, self.p.nz

        @pl.when(p.z == nz - 1 - hop)
        def _():
            for z0 in range(nz - hop):
                self.wait_z(u, z0)
                if z0 < nz - 1 - hop:
                    self.pass_on(u, z0, [self.z_in[u].at[z0]], z0, p.z - 1)

        @pl.when(p.z == hop)
        def _():
            for z0 in range(nz - 1, hop - 1, -1):
                slot = nz if z0 == hop else z0
                self.wait_z(u, slot)
                if z0 > hop:
                    self.pass_on(u, z0, [self.z_in[u].at[z0]], nz if z0 == hop + 1 else z0, p.z + 1)

    def settle(self, u):
        p, nz = self.p, self.p.nz
        self.copy_y(u, p.z).wait_recv()
        own = [self.own[u].at[p.z], self.y_in[u].at[p.z]]
        above, below = self.z_in[u].at[p.z], self.z_in[u].at[nz]

        @pl.when(p.z == 0)
        def _():
            self.done(u, own + [above])

        @pl.when(p.z == nz - 1)
        def _():
            self.done(u, own + [below])

        @pl.when(p.over & p.under)
        def _():
            self.done(u, own + [above, below])

    def tick(self, t):
        for u in range(1 + AHEAD) if t == 0 else (t + AHEAD,):
            if u < self.count:
                self.begin(u)
        stages = [(t - 1 - hop, hop) for hop in range(self.p.nz - 1, -1, -1)]
        if not OLD_FIRST:
            stages = stages[::-1]
        for u, hop in stages:
            if 0 <= u < self.count:
                if hop:
                    self.relay(u, hop)
                else:
                    self.set_out(u)
        if 0 <= t - self.p.nz < self.count:
            self.settle(t - self.p.nz)

    def finish(self):
        p, nz = self.p, self.p.nz
        other = p.flip(p.z, 1)
        for u in range(self.count):
            if self.odd(u):
                self.copy_pair(u).wait_send()
                self.copy_late(u).wait_send()
            for z0 in range(nz):
                needed = (z0 != p.z) & (z0 != other) if self.odd(u) else None
                if needed is None:
                    self.copy_y(u, z0).wait_send()
                else:

                    @pl.when(needed)
                    def _():
                        self.copy_y(u, z0).wait_send()

                @pl.when(z0 != p.z)
                def _():
                    self.copy_z(u, z0, z0, p.z).wait_send()


class Owners:
    def __init__(self, place, kinds, units, ins, outs, final, to_send, to_recv, to_local):
        self.p, self.kinds, self.units, self.ins, self.outs = place, kinds, units, ins, outs
        self.packs = [u for u, (i, _, _) in enumerate(units) if kinds[i]]
        self.final = dict(zip(self.packs, final))
        self.to_send, self.to_recv, self.to_local = to_send, to_recv, to_local

    @staticmethod
    def scratch(kinds, units, blocks):
        final = [pltpu.VMEM(block, BF16) for block, unit in zip(blocks, units) if kinds[unit[0]]]
        return final, [
            pltpu.SemaphoreType.DMA((len(units), TP)),
            pltpu.SemaphoreType.DMA((len(units), TP)),
            pltpu.SemaphoreType.DMA((len(units),)),
        ]

    def part(self, u, f):
        i, start, size = self.units[u]
        columns = pl.ds(start, size)
        return self.ins[i].at[:, f, :, columns] if self.kinds[i] else self.ins[i].at[f, :, columns]

    def place(self, u, d):
        i, start, size = self.units[u]
        return self.outs[i].at[d, :, pl.ds(start, size)]

    def copy(self, u, m):
        target = self.p.dp(m)
        src = self.final[u].at[target[0]]
        return send(src, self.place(u, self.p.d), self.to_send.at[u, m], self.to_recv.at[u, m], target)

    def local(self, u):
        return pltpu.make_async_copy(self.final[u].at[self.p.d], self.place(u, self.p.d), self.to_local.at[u])

    def done(self, u, sources):
        i, start, size = self.units[u]
        add_into(self.final[u] if self.kinds[i] else self.outs[i].at[:, pl.ds(start, size)], sources)

    def send_off(self, u):
        if u in self.final:
            for m in (2, 3, 1):
                self.copy(u, m).start()
            self.local(u).start()

    def finish(self):
        for u in self.packs:
            self.local(u).wait()
            for m in (1, 2, 3):
                self.copy(u, m).wait_send()
                source = self.p.dp(m)
                ref = self.place(u, source[0])
                send(ref, ref, self.to_send.at[u, m], self.to_recv.at[u, m], source).wait_recv()


def take(refs, *counts):
    parts = []
    for count in counts:
        parts.append(refs[:count])
        refs = refs[count:]
    return parts + [refs]


def reduce_kernel(nf, kinds, units, groups, chain, vecs, *refs):
    arrays, n = len(kinds), len(units)
    ins, group, more, vec, outs, group_outs, vec_out, refs = take(
        refs, arrays, groups, 3 if chain else 0, vecs, arrays, 3 if chain else groups, vecs
    )
    p = Place(nf)
    nz = p.nz
    own, y_in, z_in, pair_in, sems, refs = take(refs, n, n, n, n, 7)
    final, to_sems, (near, kept, near_send, near_recv, keep_sem), refs = take(
        refs, sum(kinds[i] for i, _, _ in units), 3, 5
    )
    owners = Owners(p, kinds, units, ins, outs, final, *to_sems)
    red = Reduce(p, owners.part, owners.done, own, y_in, z_in, pair_in, sems)
    if chain:
        (residual_ref, cotangent_ref, gain_ref), (sum_ref, all_ref, gain_sum_ref) = more, group_outs
        normed_ref, spread_send, spread_recv, spread_local = refs
        own_spread = pltpu.make_async_copy(normed_ref, all_ref.at[0], spread_local)
    if vecs:
        vec_in, vec_own, vec_send, vec_recv = refs

    def group_copy(j, k):
        src, mask = ((group[j].at[1], 1), (group[j].at[3], 1), (near.at[j, 1], 2))[k]
        return send(src, near.at[j, k], near_send.at[j, k], near_recv.at[j, k], p.dp(mask))

    def spread(k):
        src, dst, mask = ((normed_ref, 2, 2), (normed_ref, 1, 1), (all_ref.at[2], 3, 1))[k]
        return send(src, all_ref.at[dst], spread_send.at[k], spread_recv.at[k], p.dp(mask))

    def keep(j, k):
        return pltpu.make_async_copy(group[j].at[2 * k], kept.at[j, k], keep_sem.at[j, k])

    def norm_back(c, gain_sum):
        where = pl.ds(pl.multiple_of(c * 32, 32), 32)
        grad = kept[0, 0, where, :].astype(F32) + near[0, 0, where, :].astype(F32)
        grad = grad + near[0, 2, where, :].astype(F32)
        value = residual_ref[where, :]
        scale = lax.rsqrt(jnp.mean(value * value, axis=-1, keepdims=True) + EPS)
        weighted = grad * gain_ref[0:1]
        total = (
            cotangent_ref[where, :].astype(F32)
            + scale * weighted
            - value * (scale * scale * scale * jnp.mean(value * weighted, axis=-1, keepdims=True))
        )
        sum_ref[where, :] = total
        normed_ref[where, :] = total.astype(BF16)
        return gain_sum + jnp.sum(grad * value * scale, axis=0, keepdims=True)

    def vec_copy(k):
        device = (p.dp(1), p.dp(2), p.beside())[k]
        return send(vec_own.at[k], vec_in.at[k], vec_send.at[k], vec_recv.at[k], device)

    def vec_z(k):
        z = lax.rem(p.z + k, nz)
        return send(vec_own.at[3], vec_in.at[3 + p.z], vec_send.at[2 + k], vec_recv.at[2 + k], p.at_z(z))

    def vec_step(k):
        if k:
            vec_copy(k - 1).wait()
            vec_own[k] = vec_own[k - 1] + vec_in[k - 1]
        else:
            vec_own[0] = vec[0][...]
        if k < 3:
            vec_copy(k).start()

    p.greet()
    for j in range(groups):
        group_copy(j, 0).start()
        group_copy(j, 1).start()
        keep(j, 0).start()
        keep(j, 1).start()
    vec_ticks = (0, 3, 6, 9) if red.ticks >= 12 else (0, 1, 2, 3)
    late = min(7, red.ticks - 1)
    for t in range(red.ticks):
        red.tick(t)
        if t >= nz:
            owners.send_off(t - nz)
        if t == 0:
            for j in range(groups):
                group_copy(j, 0).wait_recv()
                group_copy(j, 1).wait_recv()
                keep(j, 0).wait()
                keep(j, 1).wait()
                add_into(near.at[j, 1], [kept.at[j, 1], near.at[j, 1]])
                group_copy(j, 2).start()
        if t == min(3, red.ticks - 2):
            if chain:
                group_copy(0, 2).wait_recv()
                rows, width = residual_ref.shape
                gain_sum = lax.fori_loop(0, rows // 32, norm_back, jnp.zeros((1, width), F32))
                gain_sum_ref[...] = jnp.broadcast_to(gain_sum, gain_sum_ref.shape)
                spread(0).start()
                spread(1).start()
                own_spread.start()
        if chain and t == min(7, red.ticks - 1):
            spread(0).wait_recv()
            spread(2).start()
        if vecs and t in vec_ticks:
            vec_step(vec_ticks.index(t))
        if vecs and t == vec_ticks[3]:
            vec_in[3 + p.z] = vec_own[3]
            for k in range(1, nz):
                vec_z(k).start()
        if t == late and not chain:
            for j in range(groups):
                group_copy(j, 2).wait_recv()
                add_into(group_outs[j], [kept.at[j, 0], near.at[j, 0], near.at[j, 2]])
    for j in range(groups):
        for k in range(3):
            group_copy(j, k).wait_send()
    if chain:
        own_spread.wait()
        spread(1).wait_recv()
        spread(2).wait_recv()
        for k in range(3):
            spread(k).wait_send()
    if vecs:
        for k in range(1, nz):
            source = lax.rem(p.z - k + nz, nz)
            ref = vec_in.at[3 + source]
            send(ref, ref, vec_send.at[2 + k], vec_recv.at[2 + k], p.at_z(source)).wait_recv()
        total = vec_in[3]
        for k in range(1, nz):
            total = total + vec_in[3 + k]
        vec_out[0][...] = total
        for k in range(1, nz):
            vec_z(k).wait_send()
    red.finish()
    owners.finish()


def make_units(nf, arrays, units):
    kinds = tuple(array.ndim == 4 for array in arrays)
    if nf > 8:
        units = [(i, array.shape[-1]) for i, array in enumerate(arrays)]
    start = [0] * len(arrays)
    full, blocks = [], []
    for i, size in units:
        full.append((i, start[i], size))
        start[i] += size
        blocks.append(((TP,) if kinds[i] else ()) + (arrays[i].shape[-2], size))
    assert all(done == array.shape[-1] for done, array in zip(start, arrays))
    return kinds, tuple(full), blocks


def reduce_outs(arrays, kinds):
    vmem, any_space = pl.BlockSpec(memory_space=pltpu.VMEM), pl.BlockSpec(memory_space=pl.ANY)
    outs = [
        jax.ShapeDtypeStruct((TP,) + array.shape[2:], BF16) if kind else jax.ShapeDtypeStruct(array.shape[1:], F32)
        for array, kind in zip(arrays, kinds)
    ]
    return outs, [any_space if kind else vmem for kind in kinds]


def reduce_all(nf, collective_id, arrays, units, groups, chain=None, vec=None):
    nz = nf // 2
    kinds, units, blocks = make_units(nf, arrays, units)
    final, to_sems = Owners.scratch(kinds, units, blocks)
    scratch = Reduce.scratch(blocks, nz) + final + to_sems
    group = groups[0]
    scratch += [pltpu.VMEM((len(groups), 3) + group.shape[1:], BF16), pltpu.VMEM((len(groups), 2) + group.shape[1:], BF16)]
    scratch += [pltpu.SemaphoreType.DMA((len(groups), 3))] * 2 + [pltpu.SemaphoreType.DMA((len(groups), 2))]
    vmem = pl.BlockSpec(memory_space=pltpu.VMEM)
    outs, out_specs = reduce_outs(arrays, kinds)
    outs += [jax.ShapeDtypeStruct(group.shape[1:], F32)] * len(groups)
    ins = list(arrays) + list(groups)
    held = len(ins)
    any_space = pl.BlockSpec(memory_space=pl.ANY)
    group_specs = [vmem] * (len(groups) + int(vec is not None))
    if chain is not None:
        group_specs = [vmem, any_space, vmem]
        scratch += [pltpu.VMEM(group.shape[1:], BF16)] + [pltpu.SemaphoreType.DMA((3,))] * 2 + [pltpu.SemaphoreType.DMA]
        outs.append(jax.ShapeDtypeStruct(group.shape, BF16))
        outs.append(jax.ShapeDtypeStruct((8, group.shape[2]), F32))
        ins += chain
    if vec is not None:
        scratch += [pltpu.VMEM((3 + nz, 8, TAIL), F32), pltpu.VMEM((4, 8, TAIL), F32)]
        scratch += [pltpu.SemaphoreType.DMA((2 + nz,))] * 2
        outs.append(jax.ShapeDtypeStruct(vec.shape, F32))
        ins.append(vec)
    return pl.pallas_call(
        partial(reduce_kernel, nf, kinds, units, len(groups), chain is not None, int(vec is not None)),
        in_specs=[any_space] * held + [vmem] * (len(ins) - held),
        out_specs=out_specs + group_specs,
        out_shape=outs,
        scratch_shapes=scratch,
        compiler_params=pltpu.CompilerParams(
            collective_id=collective_id, has_side_effects=True, vmem_limit_bytes=VMEM_LIMIT
        ),
        cost_estimate=pl.CostEstimate(
            flops=0, bytes_accessed=sum(2 * a.size * a.dtype.itemsize for a in ins), transcendentals=0
        ),
        name="reduce_" + str(collective_id),
    )(*ins)


def mixer_back_kernel(nf, kinds, units, *refs):
    arrays, n = len(kinds), len(units)
    ins, (grad_hbm, out_hbm, pos_ref, conv_ref, prm_ref, gain_ref), (proj_hbm, inv_hbm, new_hbm), refs = take(
        refs, arrays, 6, 3
    )
    outs, (gproj_hbm, gconv_ref, misc_ref), refs = take(refs, arrays, 3)
    p = Place(nf)
    own, y_in, z_in, pair_in, sems, refs = take(refs, n, n, n, n, 7)
    final, to_sems, refs = take(refs, sum(kinds[i] for i, _, _ in units), 3)
    proj_ref, inv_ref, new_ref, gmix_ref, gproj_ref, grad_ref, out_ref, load_sem, store_sem = refs
    owners = Owners(p, kinds, units, ins, outs, final, *to_sems)
    red = Reduce(p, owners.part, owners.done, own, y_in, z_in, pair_in, sems)
    rows = proj_ref.shape[0]

    def loads(g):
        at = pl.ds(pl.multiple_of(g * rows, rows), rows)
        return (
            pltpu.make_async_copy(proj_hbm.at[at], proj_ref, load_sem.at[0]),
            pltpu.make_async_copy(inv_hbm.at[pl.ds(pl.multiple_of(g * LH, LH), LH)], inv_ref, load_sem.at[1]),
            pltpu.make_async_copy(new_hbm.at[at], new_ref, load_sem.at[2]),
        )

    whole = (
        pltpu.make_async_copy(grad_hbm, grad_ref, load_sem.at[3]),
        pltpu.make_async_copy(out_hbm, out_ref, load_sem.at[4]),
    )

    def store(g):
        at = pl.ds(pl.multiple_of(g * rows, rows), rows)
        return pltpu.make_async_copy(gproj_ref, gproj_hbm.at[at], store_sem)

    def tick(t):
        if t < red.ticks:
            red.tick(t)
            if t >= p.nz:
                owners.send_off(t - p.nz)

    p.greet()
    for copy in loads(0):
        copy.start()
    gconv_ref[...] = jnp.zeros_like(gconv_ref)
    misc_ref[...] = jnp.zeros_like(misc_ref)
    tick(0)
    for copy in whole:
        copy.start()
    for copy in whole:
        copy.wait()
    every = 2

    def group(g, _):
        at = pl.ds(pl.multiple_of(g * rows, rows), rows)

        def back(c, _):
            where = pl.ds(pl.multiple_of(c * 256, 256), 256)
            gmix_ref[:, where] = mm(grad_ref[at, :], out_ref[where, :], ((1,), (1,)))
            return 0

        lax.fori_loop(0, LH * DV // 256, back, 0)
        for copy in loads(g):
            copy.wait()

        @pl.when(g > 0)
        def _():
            store(0).wait()

        for step in range(TP):

            @pl.when(g == step)
            def _():
                tick(1 + every * step)

        mixer_back(
            proj_ref, pos_ref.at[at], conv_ref, prm_ref, gain_ref, inv_ref, new_ref, gmix_ref, gproj_ref, gconv_ref, misc_ref
        )
        store(g).start()

        @pl.when(g < TP - 1)
        def _():
            for copy in loads(g + 1):
                copy.start()

        for step in range(TP):

            @pl.when(g == step)
            def _():
                tick(2 + every * step)

        return 0

    lax.fori_loop(0, TP, group, 0)
    for t in range(1 + every * TP, red.ticks):
        tick(t)
    store(0).wait()
    red.finish()
    owners.finish()


def mixer_back_all(nf, collective_id, arrays, units, grad, out, pos, conv, prm, gain, proj, inv, new):
    nz = nf // 2
    kinds, units, blocks = make_units(nf, arrays, units)
    final, to_sems = Owners.scratch(kinds, units, blocks)
    total, columns = proj.shape
    rows = total // TP
    vmem, any_space = pl.BlockSpec(memory_space=pltpu.VMEM), pl.BlockSpec(memory_space=pl.ANY)
    outs, out_specs = reduce_outs(arrays, kinds)
    outs += [
        jax.ShapeDtypeStruct((total, columns), BF16),
        jax.ShapeDtypeStruct(conv.shape, F32),
        jax.ShapeDtypeStruct((8, DV), F32),
    ]
    return pl.pallas_call(
        partial(mixer_back_kernel, nf, kinds, units),
        in_specs=[any_space] * (len(arrays) + 2) + [vmem] * 4 + [any_space] * 3,
        out_specs=out_specs + [any_space, vmem, vmem],
        out_shape=outs,
        scratch_shapes=Reduce.scratch(blocks, nz)
        + final
        + to_sems
        + [
            pltpu.VMEM((rows, columns), F32),
            pltpu.VMEM((LH, rows, rows), F32),
            pltpu.VMEM((rows, LH * DV), F32),
            pltpu.VMEM((rows, LH * DV), F32),
            pltpu.VMEM((rows, columns), BF16),
            pltpu.VMEM(grad.shape, BF16),
            pltpu.VMEM(out.shape, BF16),
            pltpu.SemaphoreType.DMA((5,)),
            pltpu.SemaphoreType.DMA,
        ],
        compiler_params=pltpu.CompilerParams(
            collective_id=collective_id, has_side_effects=True, vmem_limit_bytes=VMEM_LIMIT
        ),
        cost_estimate=pl.CostEstimate(flops=60_000_000_000, bytes_accessed=80_000_000, transcendentals=5_000_000),
        name="mixer_back",
    )(*arrays, grad, out, pos, conv, prm, gain, proj, inv, new)


def local(
    tokens,
    out_grad,
    block_first,
    block_live,
    norm1_gain,
    w_proj,
    w_decay,
    conv_w,
    w_out,
    a_log,
    dt_bias,
    head_gain,
    norm2_gain,
    w_gate_up,
    w_down,
    *,
    fsdp_size,
):
    nf = fsdp_size
    me = lax.axis_index("dp")
    rows, width = tokens.shape
    own = w_proj.shape[0]
    key_width = HEADS * DK
    value_width = HEADS * DV
    ff = w_down.shape[0] * nf

    block_index = jnp.arange(block_first.shape[0], dtype=jnp.int32)
    earlier = (block_index[:, None] >= block_index[None]) & (block_first[None] > 0)
    bucket_starts = jnp.max(jnp.where(earlier, block_index[None] * BLOCK, 0), axis=1)
    row_index = jnp.arange(rows, dtype=jnp.int32)
    position = row_index - jnp.repeat(bucket_starts, BLOCK)
    live = (row_index % BLOCK < jnp.repeat(block_live, BLOCK)).astype(F32)[:, None]

    def by_target(value):
        return value.reshape(own, TP, -1).swapaxes(0, 1)

    taps = conv_w.reshape(own, -1)
    tail = jnp.concatenate(
        [
            by_target(w_decay[:, :HEADS]),
            by_target(w_decay[:, HEADS:]),
            jnp.broadcast_to(
                jnp.concatenate([norm1_gain[:, None], norm2_gain[:, None], taps], axis=1)[None],
                (TP, own, 2 + taps.shape[1]),
            ),
        ],
        axis=2,
    )
    tail = jnp.pad(tail, ((0, 0), (0, 0), (0, TAIL - tail.shape[2])))
    pack_one = jnp.concatenate(
        [
            by_target(w_proj[:, :key_width]),
            by_target(w_proj[:, key_width : 2 * key_width]),
            by_target(w_proj[:, 2 * key_width : 2 * key_width + value_width]),
            by_target(w_proj[:, 2 * key_width + value_width :]),
            tail,
        ],
        axis=2,
    )
    pack_gate = by_target(w_gate_up[:, : ff * TP])
    pack_up = by_target(w_gate_up[:, ff * TP :])
    extra = jnp.broadcast_to(position.astype(BF16)[:, None], (rows, TAIL))
    cotangent = live * out_grad.astype(F32)
    proj_full, pack_gate, pack_up, out_full, group, grad_down = gather_all(
        nf,
        1,
        (1, 2) if nf <= 8 else (1, 1),
        ((pack_one, True), (pack_gate, False), (pack_up, False)),
        (w_out,),
        (jnp.concatenate([tokens, extra], axis=1), cotangent.astype(BF16)),
    )
    proj_full = proj_full.reshape(width, -1)
    out_full = out_full.reshape(-1, width)
    group = group.reshape(TP * rows, width + TAIL)
    grad_down = grad_down.reshape(TP * rows, width)
    group_pos = group[:, width:].astype(F32)
    group_tokens = group[:, :width].astype(F32)

    tail_full = proj_full[:, -TAIL:]
    gain_one = tail_full[:, 2 * LH].astype(F32)
    gain_two = tail_full[:, 2 * LH + 1].astype(F32)
    taps_full = tail_full[:, 2 * LH + 2 : 2 * LH + 2 + taps.shape[1]]
    taps_full = (
        taps_full.reshape(TP * nf, CONV, -1).swapaxes(0, 1).reshape(CONV, 2 * key_width + value_width).astype(F32)
    )

    def my_columns(value):
        k, v = LH * DK, LH * DV
        return jnp.concatenate(
            [
                lax.dynamic_slice_in_dim(value, me * k, k, 1),
                lax.dynamic_slice_in_dim(value, key_width + me * k, k, 1),
                lax.dynamic_slice_in_dim(value, 2 * key_width + me * v, v, 1),
            ],
            axis=1,
        )

    conv_mine = jnp.pad(my_columns(taps_full), ((0, 8 - CONV), (0, 0)))
    rate = -jnp.exp(lax.dynamic_slice_in_dim(a_log, me * LH, LH))
    bias = lax.dynamic_slice_in_dim(dt_bias, me * LH, LH)
    prm = jnp.pad(jnp.stack([rate, bias]), ((0, 6), (0, TAIL - LH)))
    gain_head = jnp.broadcast_to(head_gain[None], (8, DV))

    scale_one = lax.rsqrt(jnp.mean(group_tokens * group_tokens, axis=-1, keepdims=True) + EPS)
    normed_one = (group_tokens * scale_one * gain_one).astype(BF16)
    gain_two_rows = jnp.broadcast_to(gain_two[None], (8, width))
    proj, mixed, inv, new, residual, normed_two, gate_full, up_full, down_full = forward(
        nf,
        normed_one,
        proj_full,
        out_full,
        group_pos,
        conv_mine,
        prm,
        gain_head,
        gain_two_rows,
        tokens,
        (pack_gate, pack_up),
        w_down,
    )
    gate_full = gate_full.reshape(width, ff)
    up_full = up_full.reshape(width, ff)
    down_full = down_full.reshape(ff, width)
    normed_two = normed_two.reshape(TP * rows, width)
    gate = mm(normed_two, gate_full)
    up = mm(normed_two, up_full)
    gate_sig = jax.nn.sigmoid(gate)
    gate_act = gate * gate_sig
    hidden = (gate_act * up).astype(BF16)
    down_out = mm(hidden, down_full).astype(BF16).reshape(TP, rows, width)

    grad_wdown = mm(hidden, grad_down, ((0,), (0,))).astype(BF16).reshape(nf, -1, width)
    grad_hidden = mm(grad_down, down_full, ((1,), (1,)))
    grad_gate = (grad_hidden * up * gate_sig * (1.0 + gate * (1.0 - gate_sig))).astype(BF16)
    grad_up = (grad_hidden * gate_act).astype(BF16)
    gate_grad, up_grad = (
        mm(normed_two, grad, ((0,), (0,))).astype(BF16).reshape(TP, nf, own, ff) for grad in (grad_gate, grad_up)
    )
    grad_two = mm(grad_gate, gate_full, ((1,), (1,))) + mm(grad_up, up_full, ((1,), (1,)))
    gate_grad, up_grad, grad_residual, grad_mixed_in, gain_two_part = reduce_all(
        nf,
        2,
        (gate_grad, up_grad),
        ((0, 128), (0, 256), (0, 512), (0, 512), (1, 640), (1, 512), (1, 128), (1, 128)),
        (grad_two.astype(BF16).reshape(TP, rows, width),),
        chain=[residual, cotangent.astype(BF16), gain_two_rows],
    )
    gain_two_part = gain_two_part[0]
    grad_mixed_in = grad_mixed_in.reshape(TP * rows, width)

    wout_grad = mm(mixed, grad_mixed_in, ((0,), (0,))).astype(BF16).reshape(nf, -1, width)
    wdown_grad, wout_grad, grad_proj, grad_taps, misc = mixer_back_all(
        nf,
        5,
        (grad_wdown, wout_grad),
        ((0, 128), (0, 384), (0, 768), (0, 768), (1, 768), (1, 768), (1, 256), (1, 256)),
        grad_mixed_in,
        out_full,
        group_pos,
        conv_mine,
        prm,
        gain_head,
        proj,
        inv,
        new,
    )
    grad_one_part = mm(grad_proj, proj_full, ((1,), (1,)))
    gain_one_part = jnp.sum(grad_one_part * group_tokens * scale_one, axis=0)

    grad_taps = grad_taps[:CONV]
    k, v = LH * DK, LH * DV
    taps_all = jnp.zeros((CONV, 2 * key_width + value_width), F32)
    taps_all = lax.dynamic_update_slice(taps_all, grad_taps[:, :k], (0, me * k))
    taps_all = lax.dynamic_update_slice(taps_all, grad_taps[:, k : 2 * k], (0, key_width + me * k))
    taps_all = lax.dynamic_update_slice(taps_all, grad_taps[:, 2 * k :], (0, 2 * key_width + me * v))
    taps_all = taps_all.reshape(CONV, TP * nf, -1).swapaxes(0, 1).reshape(width, taps.shape[1])
    small = jnp.concatenate([gain_one_part[:, None], gain_two_part[:, None], taps_all], axis=1)
    columns = proj.shape[1]
    small = jnp.pad(small, ((0, 0), (columns - TAIL + 2 * LH, TAIL - 2 * LH - small.shape[1])))
    one_grad = (mm(normed_one, grad_proj, ((0,), (0,))) + small).astype(BF16).reshape(TP, nf, own, columns)

    heads_zero = jnp.zeros((HEADS,), F32)
    head_vec = jnp.concatenate(
        [
            lax.dynamic_update_slice(heads_zero, misc[1, :LH], (me * LH,)),
            lax.dynamic_update_slice(heads_zero, misc[2, :LH], (me * LH,)),
            misc[0],
        ]
    )
    head_vec = jnp.pad(head_vec, (0, 8 * TAIL - head_vec.shape[0])).reshape(8, TAIL)
    one_own, grad_one, down_sum, head_vec = reduce_all(
        nf,
        3,
        (one_grad,),
        ((0, 128), (0, 384), (0, 640), (0, 640), (0, 640), (0, 512), (0, 128), (0, 128)),
        (grad_one_part.astype(BF16).reshape(TP, rows, width), down_out),
        vec=head_vec,
    )
    head_vec = head_vec.reshape(-1)
    one_own = one_own.astype(F32)

    def columns_of(value):
        return value.swapaxes(0, 1).reshape(own, -1)

    w_gate_up_grad = jnp.concatenate(
        [columns_of(gate_grad.astype(F32)), columns_of(up_grad.astype(F32))], axis=1
    )
    w_proj_grad = jnp.concatenate(
        [
            columns_of(one_own[:, :, :k]),
            columns_of(one_own[:, :, k : 2 * k]),
            columns_of(one_own[:, :, 2 * k : 2 * k + v]),
            columns_of(one_own[:, :, 2 * k + v : 2 * k + 2 * v]),
        ],
        axis=1,
    )
    own_tail = one_own[:, :, columns - TAIL :]
    w_decay_grad = jnp.concatenate(
        [columns_of(own_tail[:, :, :LH]), columns_of(own_tail[:, :, LH : 2 * LH])], axis=1
    )
    own_small = jnp.sum(own_tail[:, :, 2 * LH : 2 * LH + 2 + taps.shape[1]], axis=0)
    norm1_gain_grad = own_small[:, 0]
    norm2_gain_grad = own_small[:, 1]
    conv_grad = own_small[:, 2:].reshape(CONV, -1)

    layer_out = (live * (residual + down_sum)).astype(BF16)
    tokens_f = tokens.astype(F32)
    scale_own = scale_one[:rows]
    weighted_one = grad_one * gain_one
    from_one = scale_own * weighted_one - tokens_f * (
        scale_own**3 * jnp.mean(tokens_f * weighted_one, axis=-1, keepdims=True)
    )
    tokens_grad = (grad_residual + from_one).astype(BF16)
    return (
        layer_out,
        tokens_grad,
        norm1_gain_grad,
        w_proj_grad,
        w_decay_grad,
        conv_grad,
        wout_grad.reshape(w_out.shape),
        head_vec[:HEADS],
        head_vec[HEADS : 2 * HEADS],
        head_vec[2 * HEADS : 2 * HEADS + DV],
        norm2_gain_grad,
        w_gate_up_grad,
        wdown_grad.reshape(w_down.shape),
    )


def solution(mesh):
    rows = P(("dp", "fsdp"), None)
    flat = P(("dp", "fsdp"))
    in_specs = (rows, rows, flat, flat, flat, rows, rows, P(None, ("dp", "fsdp")), rows, P(), P(), P(), flat, rows, rows)
    out_specs = (rows, rows, flat, rows, rows, P(None, ("dp", "fsdp")), rows, P(), P(), P(), flat, rows, rows)
    return jax.shard_map(
        partial(local, fsdp_size=mesh.shape["fsdp"]),
        mesh=mesh,
        in_specs=in_specs,
        out_specs=out_specs,
        check_vma=False,
    )
```

```python
from functools import partial

import jax
import jax.numpy as jnp
from jax import lax
from jax.experimental import pallas as pl
from jax.experimental.pallas import tpu as pltpu
from jax.sharding import PartitionSpec as P

HEADS = 16
DK = 128
DV = 256
CONV = 4
BLOCK = 64
TP = 4
LH = HEADS // TP
TAIL = 128
EPS = 1e-06
HIGH = lax.Precision.HIGHEST
F32 = jnp.float32
BF16 = jnp.bfloat16


def mm(left, right, dims=((1,), (0,))):
    return lax.dot_general(left, right, (dims, ((), ())), preferred_element_type=F32)


def mmb(left, right, dims=((1,), (0,))):
    return mm(left.astype(BF16), right.astype(BF16), dims)


def mm3(left, right, dims=((1,), (0,))):
    left_hi = left.astype(BF16)
    right_hi = right.astype(BF16)
    left_lo = (left - left_hi.astype(F32)).astype(BF16)
    right_lo = (right - right_hi.astype(F32)).astype(BF16)
    return mm(left_hi, right_hi, dims) + (mm(left_hi, right_lo, dims) + mm(left_lo, right_hi, dims))


def mmx(left, right, dims=((1,), (0,))):
    return lax.dot_general(left, right, (dims, ((), ())), precision=HIGH, preferred_element_type=F32)


def sigmoid(v):
    return 1.0 / (1.0 + jnp.exp(-v))


def conv_rows(raw, taps, pos):
    total = raw * taps[CONV - 1 : CONV]
    for lag in range(1, CONV):
        moved = pltpu.roll(raw, lag, 0)
        total = total + jnp.where(pos >= lag, moved, 0.0) * taps[CONV - 1 - lag : CONV - lag]
    return total


def conv_back(grad, raw, taps, pos):
    rows = raw.shape[0]
    total = grad * taps[CONV - 1 : CONV]
    sums = [jnp.sum(grad * raw, axis=0, keepdims=True)]
    for lag in range(1, CONV):
        kept = jnp.where(pos >= lag, grad, 0.0)
        total = total + pltpu.roll(kept, rows - lag, 0) * taps[CONV - 1 - lag : CONV - lag]
        sums.append(jnp.sum(kept * pltpu.roll(raw, lag, 0), axis=0, keepdims=True))
    return total, sums[::-1]


def unit(v, scale):
    inv = lax.rsqrt(jnp.sum(v * v, axis=-1, keepdims=True) + EPS)
    return v * (inv * scale), inv


def unit_back(grad, v, inv, scale):
    g = grad * scale
    return inv * g - v * (inv * inv * inv * jnp.sum(v * g, axis=-1, keepdims=True))


def silu_back(grad, pre, sig):
    return grad * (sig * (1.0 + pre * (1.0 - sig)))


def group_terms(tail_ref, prm_ref, pos_ref):
    rows = tail_ref.shape[0]
    pos = pos_ref[:, 0:1].astype(jnp.int32)
    row_i = lax.broadcasted_iota(jnp.int32, (rows, rows), 0)
    row_j = lax.broadcasted_iota(jnp.int32, (rows, rows), 1)
    lower = (row_j <= row_i) & (row_j >= row_i - pos)
    raw = tail_ref[...]
    shifted = raw + prm_ref[1:2]
    soft = jnp.maximum(shifted, 0.0) + jnp.log1p(jnp.exp(-jnp.abs(shifted)))
    log_decay = prm_ref[0:1] * soft
    beta = sigmoid(raw)
    lower_f = lower.astype(F32)
    cum = mmx(lower_f, log_decay)
    return pos, row_i, row_j, lower, lower_f, raw, shifted, log_decay, beta, cum, cum.T


def head_slices(head):
    key_width = LH * DK
    return (
        slice(head * DK, (head + 1) * DK),
        slice(key_width + head * DK, key_width + (head + 1) * DK),
        slice(2 * key_width + head * DV, 2 * key_width + (head + 1) * DV),
        slice(2 * key_width + (LH + head) * DV, 2 * key_width + (LH + head + 1) * DV),
    )


def mixer_forward(proj_ref, pos_ref, conv_ref, prm_ref, gain_ref, mixed_ref, inv_ref, new_ref):
    width = proj_ref.shape[1]
    tail_ref = proj_ref.at[:, width - TAIL :]
    pos, row_i, row_j, lower, _, _, _, _, beta_all, cum, cum_t = group_terms(tail_ref, prm_ref, pos_ref)
    strict = lower & (row_j < row_i)
    bits = row_i ^ row_j
    eye = (bits == 0).astype(F32)
    lows, attends, values = [], [], []
    for head in range(LH):
        sq, sk, sv, _ = head_slices(head)
        q_pre = conv_rows(proj_ref[:, sq], conv_ref[:, sq], pos)
        k_pre = conv_rows(proj_ref[:, sk], conv_ref[:, sk], pos)
        v_pre = conv_rows(proj_ref[:, sv], conv_ref[:, sv], pos)
        query, _ = unit(q_pre * sigmoid(q_pre), DK**-0.5)
        key, _ = unit(k_pre * sigmoid(k_pre), 1.0)
        beta = beta_all[:, LH + head : LH + head + 1]
        values.append(beta * (v_pre * sigmoid(v_pre)))
        gap = cum[:, head : head + 1] - cum_t[head : head + 1, :]
        decay = jnp.where(lower, jnp.exp(gap), 0.0)
        attends.append(mm3(query, key, ((1,), (1,))) * decay)
        lows.append(jnp.where(strict, beta * mm3(key, key, ((1,), (1,))) * decay, 0.0))
    invs = [eye - jnp.where(bits == 1, low, 0.0) for low in lows]
    step = 1
    while (2 << step) <= proj_ref.shape[0]:
        keep = (bits >> step) == 1
        parts = [mm3(jnp.where(keep, low, 0.0), inv) for low, inv in zip(lows, invs)]
        invs = [inv - mm3(inv, part) for inv, part in zip(invs, parts)]
        step += 1
    news = [mm3(inv, value) for inv, value in zip(invs, values)]
    mixes = [mm3(attend, new) for attend, new in zip(attends, news)]
    for head in range(LH):
        mix = mixes[head]
        scale = lax.rsqrt(jnp.mean(mix * mix, axis=-1, keepdims=True) + EPS)
        gate = proj_ref[:, head_slices(head)[3]]
        out = mix * scale * gain_ref[0:1] * (gate * sigmoid(gate))
        mixed_ref[:, head * DV : (head + 1) * DV] = out.astype(BF16)
        inv_ref[head] = invs[head]
        new_ref[:, head * DV : (head + 1) * DV] = news[head]


def mixer_back(
    proj_ref, pos_ref, conv_ref, prm_ref, gain_ref, inv_ref, new_ref, gmix_ref, gproj_ref, gconv_ref, misc_ref
):
    width = proj_ref.shape[1]
    rows = proj_ref.shape[0]
    tail_ref = proj_ref.at[:, width - TAIL :]
    pos, row_i, row_j, lower, lower_f, raw, shifted, log_decay, beta_all, cum, cum_t = group_terms(
        tail_ref, prm_ref, pos_ref
    )
    strict = lower & (row_j < row_i)
    lane = lax.broadcasted_iota(jnp.int32, (rows, TAIL), 1)
    ones = jnp.ones((rows, TAIL), F32)
    grad_cum = jnp.zeros((rows, TAIL), F32)
    grad_beta_all = jnp.zeros((rows, TAIL), F32)
    gain_sum = jnp.zeros((1, DV), F32)
    for head in range(LH):
        sq, sk, sv, sg = head_slices(head)
        q_raw, k_raw, v_raw = proj_ref[:, sq], proj_ref[:, sk], proj_ref[:, sv]
        q_pre = conv_rows(q_raw, conv_ref[:, sq], pos)
        k_pre = conv_rows(k_raw, conv_ref[:, sk], pos)
        v_pre = conv_rows(v_raw, conv_ref[:, sv], pos)
        q_sig, k_sig, v_sig = sigmoid(q_pre), sigmoid(k_pre), sigmoid(v_pre)
        q_act, k_act, value = q_pre * q_sig, k_pre * k_sig, v_pre * v_sig
        query, q_inv = unit(q_act, DK**-0.5)
        key, k_inv = unit(k_act, 1.0)
        query_b, key_b = query, key
        beta = beta_all[:, LH + head : LH + head + 1]
        gap = cum[:, head : head + 1] - cum_t[head : head + 1, :]
        decay = jnp.where(lower, jnp.exp(gap), 0.0)
        pair = mm3(key_b, key_b, ((1,), (1,)))
        query_pair = mm3(query_b, key_b, ((1,), (1,)))
        attend = query_pair * decay
        inv = inv_ref[head]
        new = new_ref[:, head * DV : (head + 1) * DV]
        mix = mm3(attend, new)
        scale = lax.rsqrt(jnp.mean(mix * mix, axis=-1, keepdims=True) + EPS)
        gate = proj_ref[:, sg]
        gate_sig = sigmoid(gate)
        grad_out = gmix_ref[:, head * DV : (head + 1) * DV]
        unscaled = mix * scale
        grad_norm = grad_out * (gate * gate_sig)
        grad_gate = silu_back(grad_out * unscaled * gain_ref[0:1], gate, gate_sig)
        gain_sum = gain_sum + jnp.sum(grad_norm * unscaled, axis=0, keepdims=True)
        weighted = grad_norm * gain_ref[0:1]
        grad_mix = scale * weighted - mix * (
            scale * scale * scale * jnp.mean(mix * weighted, axis=-1, keepdims=True)
        )
        grad_mix_b = grad_mix
        grad_new = mm3(attend, grad_mix_b, ((0,), (0,)))
        grad_attend = mm3(grad_mix_b, new, ((1,), (1,)))
        grad_rhs = mm3(inv, grad_new, ((0,), (0,)))
        grad_low = -mm3(grad_rhs, new, ((1,), (1,)))
        grad_value = beta * grad_rhs
        low_decay = jnp.where(strict, grad_low * decay, 0.0)
        low_pair = low_decay * pair
        grad_beta = jnp.sum(grad_rhs * value, axis=-1, keepdims=True) + jnp.sum(
            low_pair, axis=-1, keepdims=True
        )
        grad_pair = beta * low_decay
        grad_query_pair = grad_attend * decay
        both = beta * low_pair + grad_query_pair * query_pair
        column = jnp.sum(both, axis=-1, keepdims=True) - mmx(both, ones, ((0,), (0,)))
        grad_cum = jnp.where(lane == head, column, grad_cum)
        grad_beta_all = jnp.where(lane == LH + head, grad_beta, grad_beta_all)
        grad_pair_b = grad_pair
        grad_qp_b = grad_query_pair
        grad_query = mm3(grad_qp_b, key_b)
        grad_key = (
            mm3(grad_qp_b, query_b, ((0,), (0,))) + mm3(grad_pair_b, key_b) + mm3(grad_pair_b, key_b, ((0,), (0,)))
        )
        grad_q = silu_back(unit_back(grad_query, q_act, q_inv, DK**-0.5), q_pre, q_sig)
        grad_k = silu_back(unit_back(grad_key, k_act, k_inv, 1.0), k_pre, k_sig)
        grad_v = silu_back(grad_value, v_pre, v_sig)
        for grad, part, where in ((grad_q, q_raw, sq), (grad_k, k_raw, sk), (grad_v, v_raw, sv)):
            moved, sums = conv_back(grad, part, conv_ref[:, where], pos)
            gproj_ref[:, where] = moved.astype(BF16)
            for tap in range(CONV):
                gconv_ref[tap : tap + 1, where] += sums[tap]
        gproj_ref[:, sg] = grad_gate.astype(BF16)
    grad_log = mmx(lower_f, grad_cum, ((0,), (0,)))
    grad_step = grad_log * prm_ref[0:1] * sigmoid(shifted)
    grad_tail = grad_step + grad_beta_all * beta_all * (1.0 - beta_all)
    gproj_ref[:, width - TAIL :] = grad_tail.astype(BF16)
    misc_ref[0:1, :] += gain_sum
    misc_ref[1:2, 0:TAIL] += jnp.sum(grad_log * log_decay, axis=0, keepdims=True)
    misc_ref[2:3, 0:TAIL] += jnp.sum(grad_step, axis=0, keepdims=True)


VMEM_LIMIT = 60 * 1024 * 1024


MESH = pl.DeviceIdType.MESH


class Place:
    def __init__(self, nf):
        self.nf, self.nz = nf, nf // 2
        self.d = lax.axis_index("dp")
        self.f = lax.axis_index("fsdp")
        self.z, self.y = self.f // 2, self.f % 2
        self.over = self.z < self.nz - 1
        self.under = self.z > 0

    def flip(self, value, mask):
        return value + mask * (1 - 2 * ((value // mask) % 2))

    def dp(self, mask):
        if mask == 3:
            return (self.flip(self.flip(self.d, 1), 2), self.f)
        return (self.flip(self.d, mask), self.f)

    def at_z(self, z):
        return (self.d, z * 2 + self.y)

    def beside(self):
        return (self.d, self.flip(self.f, 1))

    def greet(self):
        barrier = pltpu.get_barrier_semaphore()
        for mask in (1, 2, 3):
            pl.semaphore_signal(barrier, inc=1, device_id=self.dp(mask), device_id_type=MESH)
        pl.semaphore_signal(barrier, inc=1, device_id=self.beside(), device_id_type=MESH)

        @pl.when(self.over)
        def _():
            pl.semaphore_signal(barrier, inc=1, device_id=self.at_z(self.z + 1), device_id_type=MESH)

        @pl.when(self.under)
        def _():
            pl.semaphore_signal(barrier, inc=1, device_id=self.at_z(self.z - 1), device_id_type=MESH)

        pl.semaphore_wait(barrier, 4 + self.over.astype(jnp.int32) + self.under.astype(jnp.int32))


def send(src, dst, send_sem, recv_sem, device):
    return pltpu.make_async_remote_copy(
        src_ref=src, dst_ref=dst, send_sem=send_sem, recv_sem=recv_sem, device_id=device, device_id_type=MESH
    )


def pieces(columns, count):
    tiles = columns // 128
    edges = [128 * (tiles * c // count) for c in range(count + 1)]
    return [(edge, after - edge) for edge, after in zip(edges, edges[1:])]


def nothing():
    return None


class Gather:
    def __init__(self, place, ahead, lag, views, ready, up_send, down_send, z_recv, y_send, y_recv, pair_send, pair_recv):
        self.p, self.ahead, self.views, self.ready = place, ahead, views, ready
        self.up_send, self.down_send, self.z_recv = up_send, down_send, z_recv
        self.y_send, self.y_recv, self.pair_send, self.pair_recv = y_send, y_recv, pair_send, pair_recv
        self.lag = lag
        self.ticks = len(views) + lag * (place.nz - 1)

    @staticmethod
    def scratch(units, nz):
        return [
            pltpu.SemaphoreType.DMA((units, nz)),
            pltpu.SemaphoreType.DMA((units, nz)),
            pltpu.SemaphoreType.DMA((units, nz)),
            pltpu.SemaphoreType.DMA((units, nz)),
            pltpu.SemaphoreType.DMA((units, nz)),
            pltpu.SemaphoreType.DMA((units,)),
            pltpu.SemaphoreType.DMA((units,)),
        ]

    def block(self, u, z, y):
        return self.views[u](z * 2 + y)

    def up(self, u, r):
        ref = self.block(u, self.p.z - (r - 1), self.p.y)
        return send(ref, ref, self.up_send.at[u, r], self.z_recv.at[u, r], self.p.at_z(self.p.z + 1))

    def down(self, u, r):
        ref = self.block(u, self.p.z + (r - 1), self.p.y)
        nz = self.p.nz
        return send(ref, ref, self.down_send.at[u, r], self.z_recv.at[u, nz - r], self.p.at_z(self.p.z - 1))

    def over_y(self, u, r):
        ref = self.block(u, lax.rem(self.p.z - r + self.p.nz, self.p.nz), self.p.y)
        return send(ref, ref, self.y_send.at[u, r], self.y_recv.at[u, r], self.p.beside())

    def pair(self, u):
        ref = self.block(u, self.p.z, 1 - self.p.y)
        return send(ref, ref, self.pair_send.at[u], self.pair_recv.at[u], self.p.at_z(self.p.flip(self.p.z, 1)))

    def wait_z(self, u, r):
        ref = self.block(u, lax.rem(self.p.z - r + self.p.nz, self.p.nz), self.p.y)
        send(ref, ref, self.up_send.at[u, 1], self.z_recv.at[u, r], self.p.beside()).wait_recv()

    def wait_y(self, u, r):
        ref = self.block(u, lax.rem(self.p.z - r + self.p.nz, self.p.nz), 1 - self.p.y)
        send(ref, ref, self.y_send.at[u, r], self.y_recv.at[u, r], self.p.beside()).wait_recv()

    def wait_pair(self, u):
        other = self.p.flip(self.p.z, 1)
        ref = self.block(u, other, 1 - self.p.y)
        send(ref, ref, self.pair_send.at[u], self.pair_recv.at[u], self.p.at_z(other)).wait_recv()

    def odd(self, u):
        return u % 2 == 1

    def skips(self, u, r):
        if not self.odd(u) or r not in (1, self.p.nz - 1):
            return None
        odd = self.p.z % 2 == 1
        if self.p.nz == 2:
            return odd | ~odd
        return odd if r == 1 else ~odd

    def unless_skipped(self, u, r, action):
        skip = self.skips(u, r)
        if skip is None:
            action()
        else:
            pl.when(~skip)(action)

    def own(self, t):
        p = self.p
        self.ready[t]()

        @pl.when(p.over)
        def _():
            self.up(t, 1).start()

        @pl.when(p.under)
        def _():
            self.down(t, 1).start()

        self.over_y(t, 0).start()

    def tick(self, t):
        p, nz = self.p, self.p.nz
        for u in range(self.ahead + 1) if t == 0 else (t + self.ahead,):
            if u < len(self.views):
                self.own(u)
        for s in range(1, nz):
            u = t - s * self.lag
            if not 0 <= u < len(self.views):
                continue

            @pl.when(p.z >= s)
            def _():
                self.wait_z(u, s)

                @pl.when(p.over)
                def _():
                    self.up(u, s + 1).start()

                self.unless_skipped(u, s, self.over_y(u, s).start)

            @pl.when(p.z <= nz - 1 - s)
            def _():
                self.wait_z(u, nz - s)

                @pl.when(p.under)
                def _():
                    self.down(u, s + 1).start()

                self.unless_skipped(u, nz - s, self.over_y(u, nz - s).start)

            if s == nz - 1 and self.odd(u):
                self.wait_y(u, 0)
                self.pair(u).start()

    def finish(self):
        p, nz = self.p, self.p.nz
        for u in range(len(self.views)):
            if not self.odd(u):
                self.wait_y(u, 0)
            else:
                self.wait_pair(u)
                self.pair(u).wait_send()
            self.over_y(u, 0).wait_send()
            for r in range(1, nz):

                def both():
                    self.wait_y(u, r)
                    self.over_y(u, r).wait_send()

                self.unless_skipped(u, r, both)
            for r in range(1, nz):

                @pl.when(p.over & (p.z >= r - 1))
                def _():
                    self.up(u, r).wait_send()

                @pl.when(p.under & (p.z <= nz - r))
                def _():
                    self.down(u, r).wait_send()


def gather_kernel(nf, splits, packs, shards, groups, *refs):
    count = len(packs) + len(shards) + groups
    ins, outs = refs[:count], refs[count : 2 * count]
    to_send, to_recv, near_send, near_recv, local_sem = refs[2 * count : 2 * count + 5]
    p = Place(nf)
    pack_in, shard_in, group_in = ins[: len(packs)], ins[len(packs) : len(packs) + len(shards)], ins[count - groups :]
    pack_out, shard_out, group_out = (
        outs[: len(packs)],
        outs[len(packs) : len(packs) + len(shards)],
        outs[count - groups :],
    )

    def own_pack(i, d):
        return pack_out[i].at[d, p.f] if packs[i] else pack_out[i].at[d]

    def exchange(i, m):
        target = p.dp(m)
        return send(pack_in[i].at[target[0]], own_pack(i, p.d), to_send.at[i, m], to_recv.at[i, m], target)

    def wait_exchange(i, m):
        source = p.dp(m)
        ref = own_pack(i, source[0])
        send(ref, ref, to_send.at[i, m], to_recv.at[i, m], source).wait_recv()

    def near(j, k):
        src, dst, mask = ((group_in[j], 2, 2), (group_in[j], 1, 1), (group_out[j].at[2], 3, 1))[k]
        return send(src, group_out[j].at[dst], near_send.at[j, k], near_recv.at[j, k], p.dp(mask))

    def wait_near(j, k):
        ref = group_out[j].at[(2, 1, 3)[k]]
        send(ref, ref, near_send.at[j, k], near_recv.at[j, k], p.dp(1)).wait_recv()

    def local(n):
        if n < len(packs):
            return pltpu.make_async_copy(pack_in[n].at[p.d], own_pack(n, p.d), local_sem.at[n])
        if n < len(packs) + len(shards):
            i = n - len(packs)
            return pltpu.make_async_copy(shard_in[i], shard_out[i].at[p.f], local_sem.at[n])
        j = n - len(packs) - len(shards)
        return pltpu.make_async_copy(group_in[j], group_out[j].at[0], local_sem.at[n])

    p.greet()
    views, ready = [], []
    for i, whole in enumerate(packs):
        for m in range(TP if whole else 0):
            source = p.dp(m)[0] if m else p.d
            for c, (start, size) in enumerate(pieces(pack_in[i].shape[-1], splits[0])):
                views.append(lambda f, i=i, d=source, at=pl.ds(start, size): pack_out[i].at[d, f, :, at])
                ready.append(nothing if c else partial(wait_exchange, i, m) if m else local(i).wait)
    for i in range(len(shards)):
        for c, (start, size) in enumerate(pieces(shard_in[i].shape[-1], splits[1])):
            views.append(lambda f, i=i, at=pl.ds(start, size): shard_out[i].at[f, :, at])
            ready.append(nothing if c else local(len(packs) + i).wait)
    gather = Gather(p, 3, 1, views, ready, *refs[2 * count + 5 :])
    for n in range(count):
        local(n).start()
    for m in (1, 2, 3):
        exchange(0, m).start()
    for j in range(groups):
        near(j, 0).start()
        near(j, 1).start()
    for i in range(1, len(packs)):
        for m in (2, 3, 1):
            exchange(i, m).start()
    for t in range(gather.ticks):
        gather.tick(t)
        if t == 2:
            for j in range(groups):
                wait_near(j, 0)
                near(j, 2).start()
    gather.finish()
    for i, whole in enumerate(packs):
        for m in (1, 2, 3):
            exchange(i, m).wait_send()
            if not whole:
                wait_exchange(i, m)
        if not whole:
            local(i).wait()
    for j in range(groups):
        wait_near(j, 1)
        wait_near(j, 2)
        for k in range(3):
            near(j, k).wait_send()
        local(len(packs) + len(shards) + j).wait()


def gather_all(nf, collective_id, splits, packs, shards, groups):
    marks = tuple(whole for _, whole in packs)
    ins = [array for array, _ in packs] + list(shards) + list(groups)
    outs = (
        [
            jax.ShapeDtypeStruct(array.shape[:1] + ((nf,) if whole else ()) + array.shape[1:], array.dtype)
            for array, whole in packs
        ]
        + [jax.ShapeDtypeStruct((nf,) + array.shape, array.dtype) for array in shards]
        + [jax.ShapeDtypeStruct((TP,) + array.shape, array.dtype) for array in groups]
    )
    units = TP * sum(marks) * splits[0] + len(shards) * splits[1]
    sent = sum(out.size * 2 for out in outs)
    any_space = pl.BlockSpec(memory_space=pl.ANY)
    return pl.pallas_call(
        partial(gather_kernel, nf, splits, marks, (True,) * len(shards), len(groups)),
        in_specs=[any_space] * len(ins),
        out_specs=[any_space] * len(outs),
        out_shape=outs,
        scratch_shapes=[
            pltpu.SemaphoreType.DMA((len(packs), TP)),
            pltpu.SemaphoreType.DMA((len(packs), TP)),
            pltpu.SemaphoreType.DMA((max(len(groups), 1), 3)),
            pltpu.SemaphoreType.DMA((max(len(groups), 1), 3)),
            pltpu.SemaphoreType.DMA((len(ins),)),
        ]
        + Gather.scratch(units, nf // 2),
        compiler_params=pltpu.CompilerParams(
            collective_id=collective_id, has_side_effects=True, vmem_limit_bytes=1024 * 1024
        ),
        cost_estimate=pl.CostEstimate(flops=0, bytes_accessed=2 * sent, transcendentals=0),
        name="gather_" + str(collective_id),
    )(*ins)


def add_into(dst, srcs):
    rows = dst.shape[-2]
    size = 16 if rows % 16 == 0 else rows
    lead = dst.shape[0] if len(dst.shape) == 3 else 1

    def body(i, _):
        at = pl.ds(pl.multiple_of((i % (rows // size)) * size, size), size)
        where = (i // (rows // size), at) if len(dst.shape) == 3 else (at,)
        total = srcs[0][where].astype(F32)
        for src in srcs[1:]:
            total = total + src[where].astype(F32)
        dst[where] = total.astype(dst.dtype)
        return 0

    lax.fori_loop(0, lead * (rows // size), body, 0)


PER = 2


def forward_kernel(nf, split, *refs):
    (x_hbm, w_hbm, out_hbm, pos_ref, conv_ref, prm_ref, gain_ref, gain_two_ref, tokens_ref), refs = refs[:9], refs[9:]
    pack_in, shard_in, refs = refs[:2], refs[2], refs[3:]
    (proj_hbm, mixed_hbm, inv_hbm, new_hbm, residual_ref, group_hbm), refs = refs[:6], refs[6:]
    pack_out, shard_out, refs = refs[:2], refs[2], refs[3:]
    (proj_ref, mixed_ref, inv_ref, new_ref, parts_ref, near_ref, stage_sem), refs = refs[:7], refs[7:]
    (part_send, part_recv, group_send, group_recv, local_sem), refs = refs[:5], refs[5:]
    (x_ref, w_ref, out_ref, normed_ref, load_sem), refs = refs[:5], refs[5:]
    p = Place(nf)
    quarter = w_hbm.shape[0] // 4
    loads = [pltpu.make_async_copy(x_hbm, x_ref, load_sem.at[0])]
    for k in range(4):
        at = pl.ds(k * quarter, quarter)
        loads.append(pltpu.make_async_copy(w_hbm.at[at], w_ref.at[at], load_sem.at[1 + k]))
    loads.append(pltpu.make_async_copy(out_hbm, out_ref, load_sem.at[5]))
    rows = tokens_ref.shape[0]
    width = tokens_ref.shape[1]

    local = [pltpu.make_async_copy(pack_in[i], pack_out[i].at[:, p.f], local_sem.at[i]) for i in range(2)]
    local.append(pltpu.make_async_copy(shard_in, shard_out.at[p.f], local_sem.at[2]))

    views, ready = [], []
    for i in range(2):
        for d in range(TP):
            views.append(lambda f, i=i, d=d: pack_out[i].at[d, f])
            ready.append(nothing if d else local[i].wait)
    for c, (start, size) in enumerate(pieces(width, split)):
        views.append(lambda f, at=pl.ds(start, size): shard_out.at[f, :, at])
        ready.append(nothing if c else local[2].wait)
    p.greet()
    for copy in local:
        copy.start()
    gather = Gather(p, 3, 1, views, ready, *refs)

    def part_copy(k):
        src, mask = ((parts_ref.at[1], 1), (parts_ref.at[3], 1), (near_ref.at[1], 2))[k]
        return send(src, near_ref.at[k], part_send.at[k], part_recv.at[k], p.dp(mask))

    def group_copy(k):
        src, dst, mask = ((normed_ref, 2, 2), (normed_ref, 1, 1), (group_hbm.at[2], 3, 1))[k]
        return send(src, group_hbm.at[dst], group_send.at[k], group_recv.at[k], p.dp(mask))

    own_normed = pltpu.make_async_copy(normed_ref, group_hbm.at[0], load_sem.at[6])

    def stage_copies(g):
        at = pl.ds(pl.multiple_of(g * rows, rows), rows)
        return (
            pltpu.make_async_copy(proj_ref, proj_hbm.at[at], stage_sem.at[0]),
            pltpu.make_async_copy(mixed_ref, mixed_hbm.at[at], stage_sem.at[1]),
            pltpu.make_async_copy(inv_ref, inv_hbm.at[pl.ds(pl.multiple_of(g * LH, LH), LH)], stage_sem.at[2]),
            pltpu.make_async_copy(new_ref, new_hbm.at[at], stage_sem.at[3]),
        )

    columns = w_ref.shape[1]
    tile = 640
    gather.tick(0)
    for load in loads:
        load.start()
    for load in loads:
        load.wait()

    def group(i, _):
        half = i // 2
        g = 2 * i + 1 - half * (3 + 4 * (i - 2 * half))

        @pl.when(i > 0)
        def _():
            for copy in stage_copies(0):
                copy.wait()

        at = pl.ds(pl.multiple_of(g * rows, rows), rows)

        def project(c, _):
            where = pl.ds(pl.multiple_of(c * tile, tile), tile)
            proj_ref[:, where] = mm(x_ref[at, :], w_ref[:, where])
            return 0

        lax.fori_loop(0, columns // tile, project, 0)
        for step in range(TP):

            @pl.when(i == step)
            def _():
                for t in range(PER // 2):
                    gather.tick(1 + PER * step + t)

        mixer_forward(proj_ref, pos_ref.at[at], conv_ref, prm_ref, gain_ref, mixed_ref, inv_ref, new_ref)
        for copy in stage_copies(g):
            copy.start()

        def project_out(c, _):
            where = pl.ds(pl.multiple_of(c * 512, 512), 512)
            parts_ref[g, :, where] = mm(mixed_ref[...], out_ref[:, where]).astype(BF16)
            return 0

        lax.fori_loop(0, width // 512, project_out, 0)
        for step in range(TP):

            @pl.when(i == step)
            def _():
                if step < 2:
                    part_copy(step).start()
                if step == 2:
                    part_copy(1).wait_recv()
                    add_into(parts_ref.at[2], [parts_ref.at[2], near_ref.at[1]])
                    send(parts_ref.at[2], near_ref.at[2], part_send.at[2], part_recv.at[2], p.dp(2)).start()
                for t in range(PER // 2, PER):
                    gather.tick(1 + PER * step + t)

        return 0

    lax.fori_loop(0, TP, group, 0)
    part_copy(0).wait_recv()
    far = send(parts_ref.at[2], near_ref.at[2], part_send.at[2], part_recv.at[2], p.dp(2))
    far.wait_recv()

    def norm(c, _):
        where = pl.ds(pl.multiple_of(c * 64, 64), 64)
        total = tokens_ref[where, :].astype(F32) + parts_ref[0, where, :].astype(F32)
        total = total + near_ref[0, where, :].astype(F32) + near_ref[2, where, :].astype(F32)
        residual_ref[where, :] = total
        scale = lax.rsqrt(jnp.mean(total * total, axis=-1, keepdims=True) + EPS)
        normed_ref[where, :] = (total * scale * gain_two_ref[0:1]).astype(BF16)
        return 0

    lax.fori_loop(0, rows // 64, norm, 0)
    group_copy(0).start()
    group_copy(1).start()
    own_normed.start()
    for t in range(1 + PER * TP, gather.ticks):
        gather.tick(t)
        if t == min(3 + PER * TP, gather.ticks - 1):
            group_copy(0).wait_recv()
            group_copy(2).start()
    gather.finish()
    for copy in stage_copies(0):
        copy.wait()
    part_copy(0).wait_send()
    part_copy(1).wait_send()
    far.wait_send()
    own_normed.wait()
    for k in (1, 2):
        group_copy(k).wait_recv()
    for k in range(3):
        group_copy(k).wait_send()


def forward(nf, x, w, out, pos, conv, prm, gain, gain_two, tokens, packs, shard):
    total, columns = x.shape[0], w.shape[1]
    rows, width = tokens.shape
    split = 4 if nf <= 8 else 1
    vmem, any_space = pl.BlockSpec(memory_space=pltpu.VMEM), pl.BlockSpec(memory_space=pl.ANY)
    outs = [
        jax.ShapeDtypeStruct((total, columns), F32),
        jax.ShapeDtypeStruct((total, LH * DV), BF16),
        jax.ShapeDtypeStruct((TP * LH, rows, rows), F32),
        jax.ShapeDtypeStruct((total, LH * DV), F32),
        jax.ShapeDtypeStruct((rows, width), F32),
        jax.ShapeDtypeStruct((TP, rows, width), BF16),
    ]
    outs += [jax.ShapeDtypeStruct((TP, nf) + pack.shape[1:], BF16) for pack in packs]
    outs += [jax.ShapeDtypeStruct((nf,) + shard.shape, BF16)]
    return pl.pallas_call(
        partial(forward_kernel, nf, split),
        in_specs=[any_space] * 3 + [vmem] * 6 + [any_space] * 3,
        out_specs=[any_space] * 4 + [vmem] + [any_space] * 4,
        out_shape=outs,
        scratch_shapes=[
            pltpu.VMEM((rows, columns), F32),
            pltpu.VMEM((rows, LH * DV), BF16),
            pltpu.VMEM((LH, rows, rows), F32),
            pltpu.VMEM((rows, LH * DV), F32),
            pltpu.VMEM((TP, rows, width), BF16),
            pltpu.VMEM((3, rows, width), BF16),
            pltpu.SemaphoreType.DMA((4,)),
            pltpu.SemaphoreType.DMA((3,)),
            pltpu.SemaphoreType.DMA((3,)),
            pltpu.SemaphoreType.DMA((3,)),
            pltpu.SemaphoreType.DMA((3,)),
            pltpu.SemaphoreType.DMA((3,)),
            pltpu.VMEM(x.shape, BF16),
            pltpu.VMEM(w.shape, BF16),
            pltpu.VMEM(out.shape, BF16),
            pltpu.VMEM((rows, width), BF16),
            pltpu.SemaphoreType.DMA((7,)),
        ]
        + Gather.scratch(2 * TP + split, nf // 2),
        compiler_params=pltpu.CompilerParams(
            collective_id=4, has_side_effects=True, vmem_limit_bytes=VMEM_LIMIT
        ),
        cost_estimate=pl.CostEstimate(flops=45_000_000_000, bytes_accessed=80_000_000, transcendentals=5_000_000),
        name="forward",
    )(x, w, out, pos, conv, prm, gain, gain_two, tokens, *packs, shard)


AHEAD, OLD_FIRST = 2, True


class Reduce:
    def __init__(self, place, part, done, own, y_in, z_in, pair_in, sems):
        self.p, self.part, self.done = place, part, done
        self.own, self.y_in, self.z_in, self.pair_in = own, y_in, z_in, pair_in
        self.y_send, self.y_recv, self.z_send, self.z_recv, self.pair_send, self.pair_recv, self.load_sem = sems
        self.count = len(y_in)
        self.ticks = self.count + place.nz

    @staticmethod
    def scratch(blocks, nz):
        units = len(blocks)
        return (
            [pltpu.VMEM((nz + u % 2,) + block, BF16) for u, block in enumerate(blocks)]
            + [pltpu.VMEM((nz,) + block, BF16) for block in blocks]
            + [pltpu.VMEM((nz + 1,) + block, BF16) for block in blocks]
            + [pltpu.VMEM(block if u % 2 else (8, 128), BF16) for u, block in enumerate(blocks)]
            + [pltpu.SemaphoreType.DMA((units, nz))] * 3
            + [pltpu.SemaphoreType.DMA((units, nz + 1))]
            + [pltpu.SemaphoreType.DMA((units,))] * 2
            + [pltpu.SemaphoreType.DMA((units, nz + 1))]
        )

    def odd(self, u):
        return u % 2 == 1

    def copy_y(self, u, z0):
        src = self.part(u, z0 * 2 + 1 - self.p.y)
        return send(src, self.y_in[u].at[z0], self.y_send.at[u, z0], self.y_recv.at[u, z0], self.p.beside())

    def copy_late(self, u):
        z = self.p.z
        return send(self.pair_in[u], self.y_in[u].at[z], self.y_send.at[u, z], self.y_recv.at[u, z], self.p.beside())

    def copy_pair(self, u):
        other = self.p.flip(self.p.z, 1)
        src = self.part(u, other * 2 + 1 - self.p.y)
        return send(src, self.pair_in[u], self.pair_send.at[u], self.pair_recv.at[u], self.p.at_z(other))

    def copy_z(self, u, z0, slot, z):
        return send(self.y_in[u].at[z0], self.z_in[u].at[slot], self.z_send.at[u, z0], self.z_recv.at[u, slot], self.p.at_z(z))

    def wait_z(self, u, slot):
        ref = self.z_in[u].at[slot]
        send(ref, ref, self.z_send.at[u, 0], self.z_recv.at[u, slot], self.p.beside()).wait_recv()

    def pass_on(self, u, z0, arrived, slot, z):
        own = self.own[u].at[z0]
        here = self.y_in[u].at[z0]
        if self.odd(u):
            other = self.p.flip(self.p.z, 1)

            @pl.when(other != z0)
            def _():
                add_into(here, [own, here] + arrived)

            @pl.when(other == z0)
            def _():
                add_into(here, [own] + arrived)
        else:
            add_into(here, [own, here] + arrived)
        self.copy_z(u, z0, slot, z).start()

    def loads(self, u):
        p, nz = self.p, self.p.nz
        copies = [
            pltpu.make_async_copy(self.part(u, z0 * 2 + p.y), self.own[u].at[z0], self.load_sem.at[u, z0])
            for z0 in range(nz)
        ]
        if self.odd(u):
            src = self.part(u, p.z * 2 + 1 - p.y)
            copies.append(pltpu.make_async_copy(src, self.own[u].at[nz], self.load_sem.at[u, nz]))
        return copies

    def begin(self, u):
        p, nz = self.p, self.p.nz
        if self.odd(u):
            self.copy_pair(u).start()
            other = p.flip(p.z, 1)
            for z0 in range(nz):

                @pl.when((z0 != p.z) & (z0 != other))
                def _():
                    self.copy_y(u, z0).start()
        else:
            for z0 in range(nz):
                self.copy_y(u, z0).start()
        for load in self.loads(u):
            load.start()

    def set_out(self, u):
        p, nz = self.p, self.p.nz
        for load in self.loads(u):
            load.wait()
        if self.odd(u):
            self.copy_pair(u).wait_recv()
            add_into(self.pair_in[u], [self.pair_in[u], self.own[u].at[nz]])
            self.copy_late(u).start()
        other = p.flip(p.z, 1)
        for z0 in range(nz):
            needed = (z0 != p.z) & (z0 != other) if self.odd(u) else z0 != p.z

            @pl.when(needed)
            def _():
                self.copy_y(u, z0).wait_recv()

        @pl.when(p.z == nz - 1)
        def _():
            for z0 in range(nz - 1):
                self.pass_on(u, z0, [], z0, p.z - 1)

        @pl.when(p.z == 0)
        def _():
            for z0 in range(nz - 1, 0, -1):
                self.pass_on(u, z0, [], nz if z0 == 1 else z0, p.z + 1)

    def relay(self, u, hop):
        p, nz = self.p, self.p.nz

        @pl.when(p.z == nz - 1 - hop)
        def _():
            for z0 in range(nz - hop):
                self.wait_z(u, z0)
                if z0 < nz - 1 - hop:
                    self.pass_on(u, z0, [self.z_in[u].at[z0]], z0, p.z - 1)

        @pl.when(p.z == hop)
        def _():
            for z0 in range(nz - 1, hop - 1, -1):
                slot = nz if z0 == hop else z0
                self.wait_z(u, slot)
                if z0 > hop:
                    self.pass_on(u, z0, [self.z_in[u].at[z0]], nz if z0 == hop + 1 else z0, p.z + 1)

    def settle(self, u):
        p, nz = self.p, self.p.nz
        self.copy_y(u, p.z).wait_recv()
        own = [self.own[u].at[p.z], self.y_in[u].at[p.z]]
        above, below = self.z_in[u].at[p.z], self.z_in[u].at[nz]

        @pl.when(p.z == 0)
        def _():
            self.done(u, own + [above])

        @pl.when(p.z == nz - 1)
        def _():
            self.done(u, own + [below])

        @pl.when(p.over & p.under)
        def _():
            self.done(u, own + [above, below])

    def tick(self, t):
        for u in range(1 + AHEAD) if t == 0 else (t + AHEAD,):
            if u < self.count:
                self.begin(u)
        stages = [(t - 1 - hop, hop) for hop in range(self.p.nz - 1, -1, -1)]
        if not OLD_FIRST:
            stages = stages[::-1]
        for u, hop in stages:
            if 0 <= u < self.count:
                if hop:
                    self.relay(u, hop)
                else:
                    self.set_out(u)
        if 0 <= t - self.p.nz < self.count:
            self.settle(t - self.p.nz)

    def finish(self):
        p, nz = self.p, self.p.nz
        other = p.flip(p.z, 1)
        for u in range(self.count):
            if self.odd(u):
                self.copy_pair(u).wait_send()
                self.copy_late(u).wait_send()
            for z0 in range(nz):
                needed = (z0 != p.z) & (z0 != other) if self.odd(u) else None
                if needed is None:
                    self.copy_y(u, z0).wait_send()
                else:

                    @pl.when(needed)
                    def _():
                        self.copy_y(u, z0).wait_send()

                @pl.when(z0 != p.z)
                def _():
                    self.copy_z(u, z0, z0, p.z).wait_send()


class Owners:
    def __init__(self, place, kinds, units, ins, outs, final, to_send, to_recv, to_local):
        self.p, self.kinds, self.units, self.ins, self.outs = place, kinds, units, ins, outs
        self.packs = [u for u, (i, _, _) in enumerate(units) if kinds[i]]
        self.final = dict(zip(self.packs, final))
        self.to_send, self.to_recv, self.to_local = to_send, to_recv, to_local

    @staticmethod
    def scratch(kinds, units, blocks):
        final = [pltpu.VMEM(block, BF16) for block, unit in zip(blocks, units) if kinds[unit[0]]]
        return final, [
            pltpu.SemaphoreType.DMA((len(units), TP)),
            pltpu.SemaphoreType.DMA((len(units), TP)),
            pltpu.SemaphoreType.DMA((len(units),)),
        ]

    def part(self, u, f):
        i, start, size = self.units[u]
        columns = pl.ds(start, size)
        return self.ins[i].at[:, f, :, columns] if self.kinds[i] else self.ins[i].at[f, :, columns]

    def place(self, u, d):
        i, start, size = self.units[u]
        return self.outs[i].at[d, :, pl.ds(start, size)]

    def copy(self, u, m):
        target = self.p.dp(m)
        src = self.final[u].at[target[0]]
        return send(src, self.place(u, self.p.d), self.to_send.at[u, m], self.to_recv.at[u, m], target)

    def local(self, u):
        return pltpu.make_async_copy(self.final[u].at[self.p.d], self.place(u, self.p.d), self.to_local.at[u])

    def done(self, u, sources):
        i, start, size = self.units[u]
        add_into(self.final[u] if self.kinds[i] else self.outs[i].at[:, pl.ds(start, size)], sources)

    def send_off(self, u):
        if u in self.final:
            for m in (2, 3, 1):
                self.copy(u, m).start()
            self.local(u).start()

    def finish(self):
        for u in self.packs:
            self.local(u).wait()
            for m in (1, 2, 3):
                self.copy(u, m).wait_send()
                source = self.p.dp(m)
                ref = self.place(u, source[0])
                send(ref, ref, self.to_send.at[u, m], self.to_recv.at[u, m], source).wait_recv()


def take(refs, *counts):
    parts = []
    for count in counts:
        parts.append(refs[:count])
        refs = refs[count:]
    return parts + [refs]


def reduce_kernel(nf, kinds, units, groups, chain, vecs, *refs):
    arrays, n = len(kinds), len(units)
    ins, group, more, vec, outs, group_outs, vec_out, refs = take(
        refs, arrays, groups, 3 if chain else 0, vecs, arrays, 3 if chain else groups, vecs
    )
    p = Place(nf)
    nz = p.nz
    own, y_in, z_in, pair_in, sems, refs = take(refs, n, n, n, n, 7)
    final, to_sems, (near, kept, near_send, near_recv, keep_sem), refs = take(
        refs, sum(kinds[i] for i, _, _ in units), 3, 5
    )
    owners = Owners(p, kinds, units, ins, outs, final, *to_sems)
    red = Reduce(p, owners.part, owners.done, own, y_in, z_in, pair_in, sems)
    if chain:
        (residual_ref, cotangent_ref, gain_ref), (sum_ref, all_ref, gain_sum_ref) = more, group_outs
        normed_ref, spread_send, spread_recv, spread_local = refs
        own_spread = pltpu.make_async_copy(normed_ref, all_ref.at[0], spread_local)
    if vecs:
        vec_in, vec_own, vec_send, vec_recv = refs

    def group_copy(j, k):
        src, mask = ((group[j].at[1], 1), (group[j].at[3], 1), (near.at[j, 1], 2))[k]
        return send(src, near.at[j, k], near_send.at[j, k], near_recv.at[j, k], p.dp(mask))

    def spread(k):
        src, dst, mask = ((normed_ref, 2, 2), (normed_ref, 1, 1), (all_ref.at[2], 3, 1))[k]
        return send(src, all_ref.at[dst], spread_send.at[k], spread_recv.at[k], p.dp(mask))

    def keep(j, k):
        return pltpu.make_async_copy(group[j].at[2 * k], kept.at[j, k], keep_sem.at[j, k])

    def norm_back(c, gain_sum):
        where = pl.ds(pl.multiple_of(c * 32, 32), 32)
        grad = kept[0, 0, where, :].astype(F32) + near[0, 0, where, :].astype(F32)
        grad = grad + near[0, 2, where, :].astype(F32)
        value = residual_ref[where, :]
        scale = lax.rsqrt(jnp.mean(value * value, axis=-1, keepdims=True) + EPS)
        weighted = grad * gain_ref[0:1]
        total = (
            cotangent_ref[where, :].astype(F32)
            + scale * weighted
            - value * (scale * scale * scale * jnp.mean(value * weighted, axis=-1, keepdims=True))
        )
        sum_ref[where, :] = total
        normed_ref[where, :] = total.astype(BF16)
        return gain_sum + jnp.sum(grad * value * scale, axis=0, keepdims=True)

    def vec_copy(k):
        device = (p.dp(1), p.dp(2), p.beside())[k]
        return send(vec_own.at[k], vec_in.at[k], vec_send.at[k], vec_recv.at[k], device)

    def vec_z(k):
        z = lax.rem(p.z + k, nz)
        return send(vec_own.at[3], vec_in.at[3 + p.z], vec_send.at[2 + k], vec_recv.at[2 + k], p.at_z(z))

    def vec_step(k):
        if k:
            vec_copy(k - 1).wait()
            vec_own[k] = vec_own[k - 1] + vec_in[k - 1]
        else:
            vec_own[0] = vec[0][...]
        if k < 3:
            vec_copy(k).start()

    p.greet()
    for j in range(groups):
        group_copy(j, 0).start()
        group_copy(j, 1).start()
        keep(j, 0).start()
        keep(j, 1).start()
    vec_ticks = (0, 3, 6, 8) if red.ticks >= 11 else (0, 1, 2, 3)
    late = min(7, red.ticks - 1)
    for t in range(red.ticks):
        red.tick(t)
        if t >= nz:
            owners.send_off(t - nz)
        if t == 0:
            for j in range(groups):
                group_copy(j, 0).wait_recv()
                group_copy(j, 1).wait_recv()
                keep(j, 0).wait()
                keep(j, 1).wait()
                add_into(near.at[j, 1], [kept.at[j, 1], near.at[j, 1]])
                group_copy(j, 2).start()
        if t == min(3, red.ticks - 2):
            if chain:
                group_copy(0, 2).wait_recv()
                rows, width = residual_ref.shape
                gain_sum = lax.fori_loop(0, rows // 32, norm_back, jnp.zeros((1, width), F32))
                gain_sum_ref[...] = jnp.broadcast_to(gain_sum, gain_sum_ref.shape)
                spread(0).start()
                spread(1).start()
                own_spread.start()
        if chain and t == min(7, red.ticks - 1):
            spread(0).wait_recv()
            spread(2).start()
        if vecs and t in vec_ticks:
            vec_step(vec_ticks.index(t))
        if vecs and t == vec_ticks[3]:
            vec_in[3 + p.z] = vec_own[3]
            for k in range(1, nz):
                vec_z(k).start()
        if t == late and not chain:
            for j in range(groups):
                group_copy(j, 2).wait_recv()
                add_into(group_outs[j], [kept.at[j, 0], near.at[j, 0], near.at[j, 2]])
    for j in range(groups):
        for k in range(3):
            group_copy(j, k).wait_send()
    if chain:
        own_spread.wait()
        spread(1).wait_recv()
        spread(2).wait_recv()
        for k in range(3):
            spread(k).wait_send()
    if vecs:
        for k in range(1, nz):
            source = lax.rem(p.z - k + nz, nz)
            ref = vec_in.at[3 + source]
            send(ref, ref, vec_send.at[2 + k], vec_recv.at[2 + k], p.at_z(source)).wait_recv()
        total = vec_in[3]
        for k in range(1, nz):
            total = total + vec_in[3 + k]
        vec_out[0][...] = total
        for k in range(1, nz):
            vec_z(k).wait_send()
    red.finish()
    owners.finish()


def make_units(nf, arrays, units):
    kinds = tuple(array.ndim == 4 for array in arrays)
    if nf > 8:
        units = [(i, array.shape[-1]) for i, array in enumerate(arrays)]
    start = [0] * len(arrays)
    full, blocks = [], []
    for i, size in units:
        full.append((i, start[i], size))
        start[i] += size
        blocks.append(((TP,) if kinds[i] else ()) + (arrays[i].shape[-2], size))
    assert all(done == array.shape[-1] for done, array in zip(start, arrays))
    return kinds, tuple(full), blocks


def reduce_outs(arrays, kinds):
    vmem, any_space = pl.BlockSpec(memory_space=pltpu.VMEM), pl.BlockSpec(memory_space=pl.ANY)
    outs = [
        jax.ShapeDtypeStruct((TP,) + array.shape[2:], BF16) if kind else jax.ShapeDtypeStruct(array.shape[1:], F32)
        for array, kind in zip(arrays, kinds)
    ]
    return outs, [any_space if kind else vmem for kind in kinds]


def reduce_all(nf, collective_id, arrays, units, groups, chain=None, vec=None):
    nz = nf // 2
    kinds, units, blocks = make_units(nf, arrays, units)
    final, to_sems = Owners.scratch(kinds, units, blocks)
    scratch = Reduce.scratch(blocks, nz) + final + to_sems
    group = groups[0]
    scratch += [pltpu.VMEM((len(groups), 3) + group.shape[1:], BF16), pltpu.VMEM((len(groups), 2) + group.shape[1:], BF16)]
    scratch += [pltpu.SemaphoreType.DMA((len(groups), 3))] * 2 + [pltpu.SemaphoreType.DMA((len(groups), 2))]
    vmem = pl.BlockSpec(memory_space=pltpu.VMEM)
    outs, out_specs = reduce_outs(arrays, kinds)
    outs += [jax.ShapeDtypeStruct(group.shape[1:], F32)] * len(groups)
    ins = list(arrays) + list(groups)
    held = len(ins)
    any_space = pl.BlockSpec(memory_space=pl.ANY)
    group_specs = [vmem] * (len(groups) + int(vec is not None))
    if chain is not None:
        group_specs = [vmem, any_space, vmem]
        scratch += [pltpu.VMEM(group.shape[1:], BF16)] + [pltpu.SemaphoreType.DMA((3,))] * 2 + [pltpu.SemaphoreType.DMA]
        outs.append(jax.ShapeDtypeStruct(group.shape, BF16))
        outs.append(jax.ShapeDtypeStruct((8, group.shape[2]), F32))
        ins += chain
    if vec is not None:
        scratch += [pltpu.VMEM((3 + nz, 8, TAIL), F32), pltpu.VMEM((4, 8, TAIL), F32)]
        scratch += [pltpu.SemaphoreType.DMA((2 + nz,))] * 2
        outs.append(jax.ShapeDtypeStruct(vec.shape, F32))
        ins.append(vec)
    return pl.pallas_call(
        partial(reduce_kernel, nf, kinds, units, len(groups), chain is not None, int(vec is not None)),
        in_specs=[any_space] * held + [vmem] * (len(ins) - held),
        out_specs=out_specs + group_specs,
        out_shape=outs,
        scratch_shapes=scratch,
        compiler_params=pltpu.CompilerParams(
            collective_id=collective_id, has_side_effects=True, vmem_limit_bytes=VMEM_LIMIT
        ),
        cost_estimate=pl.CostEstimate(
            flops=0, bytes_accessed=sum(2 * a.size * a.dtype.itemsize for a in ins), transcendentals=0
        ),
        name="reduce_" + str(collective_id),
    )(*ins)


def mixer_back_kernel(nf, kinds, units, *refs):
    arrays, n = len(kinds), len(units)
    ins, (grad_hbm, out_hbm, pos_ref, conv_ref, prm_ref, gain_ref), (proj_hbm, inv_hbm, new_hbm), refs = take(
        refs, arrays, 6, 3
    )
    outs, (gproj_hbm, gconv_ref, misc_ref), refs = take(refs, arrays, 3)
    p = Place(nf)
    own, y_in, z_in, pair_in, sems, refs = take(refs, n, n, n, n, 7)
    final, to_sems, refs = take(refs, sum(kinds[i] for i, _, _ in units), 3)
    proj_ref, inv_ref, new_ref, gmix_ref, gproj_ref, grad_ref, out_ref, load_sem, store_sem = refs
    owners = Owners(p, kinds, units, ins, outs, final, *to_sems)
    red = Reduce(p, owners.part, owners.done, own, y_in, z_in, pair_in, sems)
    rows = proj_ref.shape[0]

    def loads(g):
        at = pl.ds(pl.multiple_of(g * rows, rows), rows)
        return (
            pltpu.make_async_copy(proj_hbm.at[at], proj_ref, load_sem.at[0]),
            pltpu.make_async_copy(inv_hbm.at[pl.ds(pl.multiple_of(g * LH, LH), LH)], inv_ref, load_sem.at[1]),
            pltpu.make_async_copy(new_hbm.at[at], new_ref, load_sem.at[2]),
        )

    whole = (
        pltpu.make_async_copy(grad_hbm, grad_ref, load_sem.at[3]),
        pltpu.make_async_copy(out_hbm, out_ref, load_sem.at[4]),
    )

    def store(g):
        at = pl.ds(pl.multiple_of(g * rows, rows), rows)
        return pltpu.make_async_copy(gproj_ref, gproj_hbm.at[at], store_sem)

    def tick(t):
        if t < red.ticks:
            red.tick(t)
            if t >= p.nz:
                owners.send_off(t - p.nz)

    p.greet()
    for copy in loads(0):
        copy.start()
    gconv_ref[...] = jnp.zeros_like(gconv_ref)
    misc_ref[...] = jnp.zeros_like(misc_ref)
    tick(0)
    for copy in whole:
        copy.start()
    for copy in whole:
        copy.wait()
    every = 2

    def group(g, _):
        at = pl.ds(pl.multiple_of(g * rows, rows), rows)

        def back(c, _):
            where = pl.ds(pl.multiple_of(c * 256, 256), 256)
            gmix_ref[:, where] = mm(grad_ref[at, :], out_ref[where, :], ((1,), (1,)))
            return 0

        lax.fori_loop(0, LH * DV // 256, back, 0)
        for copy in loads(g):
            copy.wait()

        @pl.when(g > 0)
        def _():
            store(0).wait()

        for step in range(TP):

            @pl.when(g == step)
            def _():
                tick(1 + every * step)

        mixer_back(
            proj_ref, pos_ref.at[at], conv_ref, prm_ref, gain_ref, inv_ref, new_ref, gmix_ref, gproj_ref, gconv_ref, misc_ref
        )
        store(g).start()

        @pl.when(g < TP - 1)
        def _():
            for copy in loads(g + 1):
                copy.start()

        for step in range(TP):

            @pl.when(g == step)
            def _():
                tick(2 + every * step)

        return 0

    lax.fori_loop(0, TP, group, 0)
    for t in range(1 + every * TP, red.ticks):
        tick(t)
    store(0).wait()
    red.finish()
    owners.finish()


def mixer_back_all(nf, collective_id, arrays, units, grad, out, pos, conv, prm, gain, proj, inv, new):
    nz = nf // 2
    kinds, units, blocks = make_units(nf, arrays, units)
    final, to_sems = Owners.scratch(kinds, units, blocks)
    total, columns = proj.shape
    rows = total // TP
    vmem, any_space = pl.BlockSpec(memory_space=pltpu.VMEM), pl.BlockSpec(memory_space=pl.ANY)
    outs, out_specs = reduce_outs(arrays, kinds)
    outs += [
        jax.ShapeDtypeStruct((total, columns), BF16),
        jax.ShapeDtypeStruct(conv.shape, F32),
        jax.ShapeDtypeStruct((8, DV), F32),
    ]
    return pl.pallas_call(
        partial(mixer_back_kernel, nf, kinds, units),
        in_specs=[any_space] * (len(arrays) + 2) + [vmem] * 4 + [any_space] * 3,
        out_specs=out_specs + [any_space, vmem, vmem],
        out_shape=outs,
        scratch_shapes=Reduce.scratch(blocks, nz)
        + final
        + to_sems
        + [
            pltpu.VMEM((rows, columns), F32),
            pltpu.VMEM((LH, rows, rows), F32),
            pltpu.VMEM((rows, LH * DV), F32),
            pltpu.VMEM((rows, LH * DV), F32),
            pltpu.VMEM((rows, columns), BF16),
            pltpu.VMEM(grad.shape, BF16),
            pltpu.VMEM(out.shape, BF16),
            pltpu.SemaphoreType.DMA((5,)),
            pltpu.SemaphoreType.DMA,
        ],
        compiler_params=pltpu.CompilerParams(
            collective_id=collective_id, has_side_effects=True, vmem_limit_bytes=VMEM_LIMIT
        ),
        cost_estimate=pl.CostEstimate(flops=60_000_000_000, bytes_accessed=80_000_000, transcendentals=5_000_000),
        name="mixer_back",
    )(*arrays, grad, out, pos, conv, prm, gain, proj, inv, new)


def local(
    tokens,
    out_grad,
    block_first,
    block_live,
    norm1_gain,
    w_proj,
    w_decay,
    conv_w,
    w_out,
    a_log,
    dt_bias,
    head_gain,
    norm2_gain,
    w_gate_up,
    w_down,
    *,
    fsdp_size,
):
    nf = fsdp_size
    me = lax.axis_index("dp")
    rows, width = tokens.shape
    own = w_proj.shape[0]
    key_width = HEADS * DK
    value_width = HEADS * DV
    ff = w_down.shape[0] * nf

    block_index = jnp.arange(block_first.shape[0], dtype=jnp.int32)
    earlier = (block_index[:, None] >= block_index[None]) & (block_first[None] > 0)
    bucket_starts = jnp.max(jnp.where(earlier, block_index[None] * BLOCK, 0), axis=1)
    row_index = jnp.arange(rows, dtype=jnp.int32)
    position = row_index - jnp.repeat(bucket_starts, BLOCK)
    live = (row_index % BLOCK < jnp.repeat(block_live, BLOCK)).astype(F32)[:, None]

    def by_target(value):
        return value.reshape(own, TP, -1).swapaxes(0, 1)

    taps = conv_w.reshape(own, -1)
    tail = jnp.concatenate(
        [
            by_target(w_decay[:, :HEADS]),
            by_target(w_decay[:, HEADS:]),
            jnp.broadcast_to(
                jnp.concatenate([norm1_gain[:, None], norm2_gain[:, None], taps], axis=1)[None],
                (TP, own, 2 + taps.shape[1]),
            ),
        ],
        axis=2,
    )
    tail = jnp.pad(tail, ((0, 0), (0, 0), (0, TAIL - tail.shape[2])))
    pack_one = jnp.concatenate(
        [
            by_target(w_proj[:, :key_width]),
            by_target(w_proj[:, key_width : 2 * key_width]),
            by_target(w_proj[:, 2 * key_width : 2 * key_width + value_width]),
            by_target(w_proj[:, 2 * key_width + value_width :]),
            tail,
        ],
        axis=2,
    )
    pack_gate = by_target(w_gate_up[:, : ff * TP])
    pack_up = by_target(w_gate_up[:, ff * TP :])
    extra = jnp.broadcast_to(position.astype(BF16)[:, None], (rows, TAIL))
    cotangent = live * out_grad.astype(F32)
    proj_full, pack_gate, pack_up, out_full, group, grad_down = gather_all(
        nf,
        1,
        (1, 2) if nf <= 8 else (1, 1),
        ((pack_one, True), (pack_gate, False), (pack_up, False)),
        (w_out,),
        (jnp.concatenate([tokens, extra], axis=1), cotangent.astype(BF16)),
    )
    proj_full = proj_full.reshape(width, -1)
    out_full = out_full.reshape(-1, width)
    group = group.reshape(TP * rows, width + TAIL)
    grad_down = grad_down.reshape(TP * rows, width)
    group_pos = group[:, width:].astype(F32)
    group_tokens = group[:, :width].astype(F32)

    tail_full = proj_full[:, -TAIL:]
    gain_one = tail_full[:, 2 * LH].astype(F32)
    gain_two = tail_full[:, 2 * LH + 1].astype(F32)
    taps_full = tail_full[:, 2 * LH + 2 : 2 * LH + 2 + taps.shape[1]]
    taps_full = (
        taps_full.reshape(TP * nf, CONV, -1).swapaxes(0, 1).reshape(CONV, 2 * key_width + value_width).astype(F32)
    )

    def my_columns(value):
        k, v = LH * DK, LH * DV
        return jnp.concatenate(
            [
                lax.dynamic_slice_in_dim(value, me * k, k, 1),
                lax.dynamic_slice_in_dim(value, key_width + me * k, k, 1),
                lax.dynamic_slice_in_dim(value, 2 * key_width + me * v, v, 1),
            ],
            axis=1,
        )

    conv_mine = jnp.pad(my_columns(taps_full), ((0, 8 - CONV), (0, 0)))
    rate = -jnp.exp(lax.dynamic_slice_in_dim(a_log, me * LH, LH))
    bias = lax.dynamic_slice_in_dim(dt_bias, me * LH, LH)
    prm = jnp.pad(jnp.stack([rate, bias]), ((0, 6), (0, TAIL - LH)))
    gain_head = jnp.broadcast_to(head_gain[None], (8, DV))

    scale_one = lax.rsqrt(jnp.mean(group_tokens * group_tokens, axis=-1, keepdims=True) + EPS)
    normed_one = (group_tokens * scale_one * gain_one).astype(BF16)
    gain_two_rows = jnp.broadcast_to(gain_two[None], (8, width))
    proj, mixed, inv, new, residual, normed_two, gate_full, up_full, down_full = forward(
        nf,
        normed_one,
        proj_full,
        out_full,
        group_pos,
        conv_mine,
        prm,
        gain_head,
        gain_two_rows,
        tokens,
        (pack_gate, pack_up),
        w_down,
    )
    gate_full = gate_full.reshape(width, ff)
    up_full = up_full.reshape(width, ff)
    down_full = down_full.reshape(ff, width)
    normed_two = normed_two.reshape(TP * rows, width)
    gate = mm(normed_two, gate_full)
    up = mm(normed_two, up_full)
    gate_sig = jax.nn.sigmoid(gate)
    gate_act = gate * gate_sig
    hidden = (gate_act * up).astype(BF16)
    down_out = mm(hidden, down_full).astype(BF16).reshape(TP, rows, width)

    grad_wdown = mm(hidden, grad_down, ((0,), (0,))).astype(BF16).reshape(nf, -1, width)
    grad_hidden = mm(grad_down, down_full, ((1,), (1,)))
    grad_gate = (grad_hidden * up * gate_sig * (1.0 + gate * (1.0 - gate_sig))).astype(BF16)
    grad_up = (grad_hidden * gate_act).astype(BF16)
    gate_grad, up_grad = (
        mm(normed_two, grad, ((0,), (0,))).astype(BF16).reshape(TP, nf, own, ff) for grad in (grad_gate, grad_up)
    )
    grad_two = mm(grad_gate, gate_full, ((1,), (1,))) + mm(grad_up, up_full, ((1,), (1,)))
    gate_grad, up_grad, grad_residual, grad_mixed_in, gain_two_part = reduce_all(
        nf,
        2,
        (gate_grad, up_grad),
        ((0, 128), (0, 512), (0, 768), (1, 768), (1, 512), (1, 128)),
        (grad_two.astype(BF16).reshape(TP, rows, width),),
        chain=[residual, cotangent.astype(BF16), gain_two_rows],
    )
    gain_two_part = gain_two_part[0]
    grad_mixed_in = grad_mixed_in.reshape(TP * rows, width)

    wout_grad = mm(mixed, grad_mixed_in, ((0,), (0,))).astype(BF16).reshape(nf, -1, width)
    wdown_grad, wout_grad, grad_proj, grad_taps, misc = mixer_back_all(
        nf,
        5,
        (grad_wdown, wout_grad),
        ((0, 128), (0, 640), (0, 1280), (1, 1024), (1, 768), (1, 256)),
        grad_mixed_in,
        out_full,
        group_pos,
        conv_mine,
        prm,
        gain_head,
        proj,
        inv,
        new,
    )
    grad_one_part = mm(grad_proj, proj_full, ((1,), (1,)))
    gain_one_part = jnp.sum(grad_one_part * group_tokens * scale_one, axis=0)

    grad_taps = grad_taps[:CONV]
    k, v = LH * DK, LH * DV
    taps_all = jnp.zeros((CONV, 2 * key_width + value_width), F32)
    taps_all = lax.dynamic_update_slice(taps_all, grad_taps[:, :k], (0, me * k))
    taps_all = lax.dynamic_update_slice(taps_all, grad_taps[:, k : 2 * k], (0, key_width + me * k))
    taps_all = lax.dynamic_update_slice(taps_all, grad_taps[:, 2 * k :], (0, 2 * key_width + me * v))
    taps_all = taps_all.reshape(CONV, TP * nf, -1).swapaxes(0, 1).reshape(width, taps.shape[1])
    small = jnp.concatenate([gain_one_part[:, None], gain_two_part[:, None], taps_all], axis=1)
    columns = proj.shape[1]
    small = jnp.pad(small, ((0, 0), (columns - TAIL + 2 * LH, TAIL - 2 * LH - small.shape[1])))
    one_grad = (mm(normed_one, grad_proj, ((0,), (0,))) + small).astype(BF16).reshape(TP, nf, own, columns)

    heads_zero = jnp.zeros((HEADS,), F32)
    head_vec = jnp.concatenate(
        [
            lax.dynamic_update_slice(heads_zero, misc[1, :LH], (me * LH,)),
            lax.dynamic_update_slice(heads_zero, misc[2, :LH], (me * LH,)),
            misc[0],
        ]
    )
    head_vec = jnp.pad(head_vec, (0, 8 * TAIL - head_vec.shape[0])).reshape(8, TAIL)
    one_own, grad_one, down_sum, head_vec = reduce_all(
        nf,
        3,
        (one_grad,),
        ((0, 128), (0, 512), (0, 768), (0, 768), (0, 640), (0, 256), (0, 128)),
        (grad_one_part.astype(BF16).reshape(TP, rows, width), down_out),
        vec=head_vec,
    )
    head_vec = head_vec.reshape(-1)
    one_own = one_own.astype(F32)

    def columns_of(value):
        return value.swapaxes(0, 1).reshape(own, -1)

    w_gate_up_grad = jnp.concatenate(
        [columns_of(gate_grad.astype(F32)), columns_of(up_grad.astype(F32))], axis=1
    )
    w_proj_grad = jnp.concatenate(
        [
            columns_of(one_own[:, :, :k]),
            columns_of(one_own[:, :, k : 2 * k]),
            columns_of(one_own[:, :, 2 * k : 2 * k + v]),
            columns_of(one_own[:, :, 2 * k + v : 2 * k + 2 * v]),
        ],
        axis=1,
    )
    own_tail = one_own[:, :, columns - TAIL :]
    w_decay_grad = jnp.concatenate(
        [columns_of(own_tail[:, :, :LH]), columns_of(own_tail[:, :, LH : 2 * LH])], axis=1
    )
    own_small = jnp.sum(own_tail[:, :, 2 * LH : 2 * LH + 2 + taps.shape[1]], axis=0)
    norm1_gain_grad = own_small[:, 0]
    norm2_gain_grad = own_small[:, 1]
    conv_grad = own_small[:, 2:].reshape(CONV, -1)

    layer_out = (live * (residual + down_sum)).astype(BF16)
    tokens_f = tokens.astype(F32)
    scale_own = scale_one[:rows]
    weighted_one = grad_one * gain_one
    from_one = scale_own * weighted_one - tokens_f * (
        scale_own**3 * jnp.mean(tokens_f * weighted_one, axis=-1, keepdims=True)
    )
    tokens_grad = (grad_residual + from_one).astype(BF16)
    return (
        layer_out,
        tokens_grad,
        norm1_gain_grad,
        w_proj_grad,
        w_decay_grad,
        conv_grad,
        wout_grad.reshape(w_out.shape),
        head_vec[:HEADS],
        head_vec[HEADS : 2 * HEADS],
        head_vec[2 * HEADS : 2 * HEADS + DV],
        norm2_gain_grad,
        w_gate_up_grad,
        wdown_grad.reshape(w_down.shape),
    )


def solution(mesh):
    rows = P(("dp", "fsdp"), None)
    flat = P(("dp", "fsdp"))
    in_specs = (rows, rows, flat, flat, flat, rows, rows, P(None, ("dp", "fsdp")), rows, P(), P(), P(), flat, rows, rows)
    out_specs = (rows, rows, flat, rows, rows, P(None, ("dp", "fsdp")), rows, P(), P(), P(), flat, rows, rows)
    return jax.shard_map(
        partial(local, fsdp_size=mesh.shape["fsdp"]),
        mesh=mesh,
        in_specs=in_specs,
        out_specs=out_specs,
        check_vma=False,
    )
```
